32 devices in a mesh: dp: 4 (over y, core), fsdp: 8 (over z, x).
Axes of the slice: x: 2, y: 2, z: 4, core: 2. Of those that a mesh axis runs over, the one named last changes fastest.
Arguments:
- latent: bfloat16 [182272, 256], P(('dp', 'fsdp')), may hold values from -6 to 6
- actions: int32 [182272], P(('dp', 'fsdp')), may hold values from 0 to 3
- value_bins: int32 [182272], P(('dp', 'fsdp')), may hold values from 0 to 600
- chance_codes: int32 [182272], P(('dp', 'fsdp')), may hold values from 0 to 31
- step_mask: int32 [182272], P(('dp', 'fsdp')), may hold values 0 or 1
- stem_weight: bfloat16 [256, 256], P('fsdp'), may hold values from -0.375 to 0.375
- action_table: bfloat16 [4, 256], P(None, 'fsdp'), may hold values from -6 to 6
- stem_bias: bfloat16 [256], P('fsdp'), may hold values from -4 to 4
- stem_gain: bfloat16 [256], P('fsdp'), may hold values from 0.099609375 to 1.8984375
- stem_shift: bfloat16 [256], P('fsdp'), may hold values from -3 to 3
- block_weight: bfloat16 [10, 256, 256], P(None, 'fsdp'), may hold values from -0.375 to 0.375
- block_gain: bfloat16 [10, 256], P(None, 'fsdp'), may hold values from 0.099609375 to 1.8984375
- block_shift: bfloat16 [10, 256], P(None, 'fsdp'), may hold values from -3 to 3
- block_bias: bfloat16 [10, 256], P(None, 'fsdp'), may hold values from -3 to 3
- value_weight: bfloat16 [256, 601], P('fsdp'), may hold values from -0.375 to 0.375
- value_bias: bfloat16 [601], replicated, may hold values from -4 to 4
- chance_weight: bfloat16 [256, 32], P('fsdp'), may hold values from -0.375 to 0.375
- chance_bias: bfloat16 [32], replicated, may hold values from -4 to 4
Outputs:
- latents: bfloat16 [182272, 256], P(('dp', 'fsdp'))
- value_logits: bfloat16 [182272, 601], P(('dp', 'fsdp'))
- chance_logits: bfloat16 [182272, 32], P(('dp', 'fsdp'))
- loss: float32 [], replicated
- latent_grad: bfloat16 [182272, 256], P(('dp', 'fsdp'))
- stem_weight_grad: float32 [256, 256], P('fsdp')
- action_table_grad: float32 [4, 256], P(None, 'fsdp')
- stem_bias_grad: float32 [256], P('fsdp')
- stem_gain_grad: float32 [256], P('fsdp')
- stem_shift_grad: float32 [256], P('fsdp')
- block_weight_grad: float32 [10, 256, 256], P(None, 'fsdp')
- block_gain_grad: float32 [10, 256], P(None, 'fsdp')
- block_shift_grad: float32 [10, 256], P(None, 'fsdp')
- block_bias_grad: float32 [10, 256], P(None, 'fsdp')
- value_weight_grad: float32 [256, 601], P('fsdp')
- value_bias_grad: float32 [601], replicated
- chance_weight_grad: float32 [256, 32], P('fsdp')
- chance_bias_grad: float32 [32], replicated
The draws below stay inside these ranges and needn't reach their ends.
All inputs are finite; a program needn't handle non-finite values. No bound on the sum of `step_mask` on one device may be relied on, other than what follows from the above.
Results may differ from the reference program's by a relative error of at most 0.009.
Values may be sent and summed in bfloat16 or wider, within the bound.
No kernel may reach another device: no remote copies, remote signals or barrier semaphores. Data moves between devices by JAX's collectives and lax.ppermute only.
A program may use at most 192 MiB of HBM per device.

```python
import jax
import jax.numpy as jnp
from jax import lax

D = 256
Q = 601
C = 32
ACTIONS = 4
LAYERS = 10
ROWS_DEV = 5696
ROWS = 182272


def plant(array, own_key, smallest, high):
    longest = array.shape.index(max(array.shape))
    spots = []
    for shift in (0, 1):
        where = [jax.random.randint(jax.random.fold_in(own_key, axis), (), 0, length) for axis, length in enumerate(array.shape)]
        where[longest] = (where[longest] + shift) % array.shape[longest]
        spots.append(tuple(where))
    return array.at[spots[0]].set(smallest).at[spots[1]].set(high)


def shard_levels(stream_key, shape, shards, low, high):
    level = 1.0
    for axis_at, shards_of in shards:
        heights = jax.random.uniform(jax.random.fold_in(jax.random.fold_in(stream_key, 6), axis_at), (shards_of,), jnp.float32, low / len(shards), high / len(shards))
        level = level * jnp.repeat(jnp.exp(heights), shape[axis_at] // shards_of).reshape((-1,) + (1,) * (len(shape) - 1 - axis_at))
    return level


def centred(rng, extent, scale, bound, shards=(), held_as=jnp.bfloat16):
    array = scale * jax.random.normal(rng, extent, jnp.float32)
    if shards:
        array = array * shard_levels(rng, extent, shards, -0.22, 0.18)
    return jnp.clip(array, -bound, bound).astype(held_as)


def setup_inputs(seed: int = 0) -> dict:
    key_of = jax.random.split(jax.random.key(seed), 19)
    latent = centred(key_of[0], (ROWS, D), 1.0, 6.0, ((0, 32),))
    actions = plant(jax.random.randint(key_of[1], (ROWS,), 0, ACTIONS), jax.random.fold_in(key_of[1], 1), 0, ACTIONS - 1).astype(jnp.int32)
    value_bins = plant(jax.random.randint(key_of[2], (ROWS,), 0, Q), jax.random.fold_in(key_of[2], 1), 0, Q - 1).astype(jnp.int32)
    chance_codes = plant(jax.random.randint(key_of[3], (ROWS,), 0, C), jax.random.fold_in(key_of[3], 1), 0, C - 1).astype(jnp.int32)
    step_mask = plant((jax.random.randint(key_of[4], (ROWS,), 0, 5) < 4).astype(jnp.int32), jax.random.fold_in(key_of[4], 1), 0, 1)
    stem_weight = centred(key_of[5], (D, D), D ** -0.5, 0.375, ((0, 8),))
    action_table = centred(key_of[6], (ACTIONS, D), 1.0, 6.0, ((1, 8),))
    stem_bias = centred(key_of[7], (D,), 0.5, 4.0, ((0, 8),))
    stem_gain = jnp.clip(1.0 + 0.18 * jax.random.normal(key_of[8], (D,), jnp.float32), 0.099609375, 1.8984375).astype(jnp.bfloat16)
    stem_shift = centred(key_of[9], (D,), 0.3, 3.0, ((0, 8),))
    block_weight = centred(key_of[10], (LAYERS, D, D), D ** -0.5, 0.375, ((1, 8),))
    block_gain = jnp.clip(1.0 + 0.18 * jax.random.normal(key_of[11], (LAYERS, D), jnp.float32), 0.099609375, 1.8984375).astype(jnp.bfloat16)
    block_shift = centred(key_of[12], (LAYERS, D), 0.3, 3.0, ((1, 8),))
    block_bias = centred(key_of[13], (LAYERS, D), 0.3, 3.0, ((1, 8),))
    value_weight = centred(key_of[14], (D, Q), D ** -0.5, 0.375, ((0, 8),))
    value_bias = centred(key_of[15], (Q,), 0.5, 4.0)
    chance_weight = centred(key_of[16], (D, C), D ** -0.5, 0.375, ((0, 8),))
    chance_bias = centred(key_of[17], (C,), 0.5, 4.0)
    return dict(latent=latent, actions=actions, value_bins=value_bins, chance_codes=chance_codes, step_mask=step_mask, stem_weight=stem_weight, action_table=action_table, stem_bias=stem_bias, stem_gain=stem_gain, stem_shift=stem_shift, block_weight=block_weight, block_gain=block_gain, block_shift=block_shift, block_bias=block_bias, value_weight=value_weight, value_bias=value_bias, chance_weight=chance_weight, chance_bias=chance_bias)


@jax.custom_vjp
def low(v):
    return lax.optimization_barrier(v.astype(jnp.bfloat16)).astype(jnp.float32)

@jax.custom_vjp
def low_back(v):
    return v

def low_keep(v):
    return (low(v), None)

def low_pass(kept, grad):
    return (grad,)

def back_keep(v):
    return (v, None)

def back_low(kept, grad):
    return (low(grad),)
low.defvjp(low_keep, low_pass)
low_back.defvjp(back_keep, back_low)

def product(left, right):
    return jnp.dot(left, right, precision=lax.Precision.HIGHEST, preferred_element_type=jnp.float32)

def norm_act(values, gain, shift):
    center = values - lax.optimization_barrier(jnp.mean(values, axis=-1, keepdims=True))
    spread = lax.optimization_barrier(jnp.mean(center * center, axis=-1, keepdims=True))
    return jax.nn.gelu(center * lax.rsqrt(spread + 1e-05) * gain + shift, approximate=True)

def cross_rows(logits, target):
    target_hot = (target[:, None] == jnp.arange(logits.shape[1], dtype=jnp.int32)[None, :]).astype(logits.dtype)
    return jax.nn.logsumexp(logits, axis=-1) - lax.optimization_barrier(jnp.sum(logits * target_hot, axis=-1))

def forward(lat, params, actions_b, bins_b, codes_b, mask_b):
    stem_weight, action_table, stem_bias, stem_gain, stem_shift, block_weight, block_gain, block_shift, block_bias, value_weight, value_bias, chance_weight, chance_bias = params
    onehot = (actions_b[:, None] == jnp.arange(ACTIONS, dtype=jnp.int32)[None, :]).astype(lat.dtype)
    pre = low_back(product(lat, stem_weight) + product(onehot, action_table)) + stem_bias
    stream = norm_act(pre, stem_gain, stem_shift)
    for layer in range(LAYERS):
        activated = low(norm_act(stream, block_gain[layer], block_shift[layer]))
        stream = stream + low_back(product(activated, block_weight[layer])) + block_bias[layer]
    rounded = low(stream)
    value_full = low_back(product(rounded, value_weight)) + value_bias
    chance_full = low_back(product(rounded, chance_weight)) + chance_bias
    per_state = mask_b * (cross_rows(value_full, bins_b) + cross_rows(chance_full, codes_b))
    return (jnp.sum(per_state), (stream, value_full, chance_full))

def reference(latent, actions, value_bins, chance_codes, step_mask, stem_weight, action_table, stem_bias, stem_gain, stem_shift, block_weight, block_gain, block_shift, block_bias, value_weight, value_bias, chance_weight, chance_bias):
    params = tuple((item.astype(jnp.float32) for item in (stem_weight, action_table, stem_bias, stem_gain, stem_shift, block_weight, block_gain, block_shift, block_bias, value_weight, value_bias, chance_weight, chance_bias)))
    row_count = latent.shape[0]
    blocks = row_count // ROWS_DEV

    def split(values):
        return values.reshape((blocks, ROWS_DEV) + values.shape[1:])

    def step(carry, item):
        lat_b, actions_b, bins_b, codes_b, mask_b = item
        summed, accum = carry
        mask_f = mask_b.astype(jnp.float32)

        def local_loss(lat_in, params_in):
            return forward(lat_in, params_in, actions_b, bins_b, codes_b, mask_f)
        value, back_fn, extra = jax.vjp(local_loss, lat_b.astype(jnp.float32), params, has_aux=True)
        d_lat, d_params = back_fn(jnp.ones_like(value))
        accum = jax.tree.map(lambda first, second: first + second, accum, d_params)
        outputs = (extra[0].astype(jnp.bfloat16), extra[1].astype(jnp.bfloat16), extra[2].astype(jnp.bfloat16), d_lat.astype(jnp.bfloat16))
        return ((summed + value, accum), outputs)
    start = (jnp.zeros((), jnp.float32), jax.tree.map(jnp.zeros_like, params))
    (summed, accum), outputs = lax.scan(step, start, (split(latent), split(actions), split(value_bins), split(chance_codes), split(step_mask)))
    latents = outputs[0].reshape(row_count, D)
    value_logits = outputs[1].reshape(row_count, Q)
    chance_logits = outputs[2].reshape(row_count, C)
    latent_grad = outputs[3].reshape(row_count, D)
    grads = tuple((item / row_count for item in accum))
    return (latents, value_logits, chance_logits, summed / row_count, latent_grad, grads[0], grads[1], grads[2], grads[3], grads[4], grads[5], grads[6], grads[7], grads[8], grads[9], grads[10], grads[11], grads[12])
```

```python
import functools
import jax
import jax.numpy as jnp
from jax import lax
from jax.experimental import pallas as pl
from jax.experimental.pallas import tpu as pltpu
from jax.sharding import PartitionSpec as P

F32 = jnp.float32
BF16 = jnp.bfloat16
WIDTH = 256
UNIT = 16
TILE = 1440
HEAD_CHUNK = 240
SPLIT = 3
K0 = 2 * 0.7978845608028654
K1 = 8 * 0.7978845608028654 * 0.044715


def mm(a, b):
    return lax.dot_general(a, b, (((1,), (0,)), ((), ())), preferred_element_type=F32)


def mm_nt(a, b):
    return lax.dot_general(a, b, (((1,), (1,)), ((), ())), preferred_element_type=F32)


def mm_tn(a, b):
    return lax.dot_general(a, b, (((0,), (0,)), ((), ())), preferred_element_type=F32)


def norm_gelu(s, gain8, gain_slope, shift_half):
    mean = jnp.sum(s, axis=1, keepdims=True) * (1.0 / WIDTH)
    center = s - mean
    r = lax.rsqrt(jnp.sum(center * center, axis=1, keepdims=True) + WIDTH * 1e-5)
    n = center * r
    h = n * gain8 + shift_half
    y = h * h
    t = jnp.tanh(h * (K0 + K1 * y))
    e1 = 1.0 + t
    bend = (h * (y + K0 / (3 * K1))) * (1.0 - t)
    slope = (e1 * gain_slope) * (1.0 / (3 * K1) + bend)
    return h * e1, n.astype(BF16), slope.astype(BF16), jnp.broadcast_to(r, (UNIT, 128))


def scales(vec_ref, at, layers):
    gain = vec_ref[pl.ds(at, 1), :]
    return gain * 8.0, gain * (8.0 * 3 * K1), vec_ref[pl.ds(at + layers, 1), :] * 0.5


def norm_back(da, slope, n, r):
    w = da * slope.astype(F32)
    m1 = jnp.sum(w, axis=1, keepdims=True) * (1.0 / WIDTH)
    w16 = w.astype(BF16)
    wn = w16 * n
    wide = (wn[:, 0:128] + wn[:, 128:256]).astype(F32)
    m2 = jnp.sum(wide, axis=1, keepdims=True)
    m1 = jnp.broadcast_to(m1, (UNIT, 128)).astype(BF16)
    m2 = jnp.broadcast_to(m2, (UNIT, 128)).astype(BF16)
    halves = [
        (w[:, k:k + 128] - (m1 + n[:, k:k + 128] * m2).astype(F32)) * r for k in (0, 128)
    ]
    return jnp.concatenate(halves, axis=1), w, wn


def forward_chunk(base, size, s_ref, save, i, scale, w, bias):
    act_ref, n_ref, slope_ref, r_ref = save
    for u in range(0, size, UNIT):
        rows = pl.ds(base + u, UNIT)
        act, n, slope, r = norm_gelu(s_ref[rows, :], *scale)
        act_ref[i, rows, :] = act.astype(BF16)
        n_ref[i, rows, :] = n
        slope_ref[i, rows, :] = slope
        r_ref[i, rows, :] = r
    out = mm(act_ref[i, pl.ds(base, size), :], w)
    for u in range(0, size, UNIT):
        rows = pl.ds(base + u, UNIT)
        s_ref[rows, :] = s_ref[rows, :] + (out[u:u + UNIT, :] + bias)


def forward_layers(chunk_rows, first, last, layers, s_ref, save, vec_ref, w_ref, w_at, save_at):
    def layer(i, carry):
        scale = scales(vec_ref, 7 + i, layers)
        bias = vec_ref[pl.ds(7 + 2 * layers + i, 1), :]
        def chunk(c, carry):
            base = pl.multiple_of(c * chunk_rows, UNIT)
            forward_chunk(base, chunk_rows, s_ref, save, i - save_at, scale, w_ref[i - w_at], bias)
            return carry
        return lax.fori_loop(0, TILE // chunk_rows, chunk, carry)
    lax.fori_loop(first, last, layer, 0)


def column_sums(parts):
    total = parts[0]
    for part in parts[1:]:
        total = total + part
    return total.astype(F32)


GROUP = 3


def backward_chunk(base, size, s_ref, low_ref, save, i, w, gw_ref, g_at):
    act_ref, n_ref, slope_ref, r_ref = save
    zero = jnp.zeros((UNIT, WIDTH), F32)
    shift, gain, bias = zero, zero, zero
    low = low_ref[pl.ds(base, size), :]
    da = mm_nt(low, w)
    gw_ref[g_at] += mm_tn(act_ref[i, pl.ds(base, size), :], low)
    held = []
    for u in range(0, size, UNIT):
        rows = pl.ds(base + u, UNIT)
        d_in, wf, wn = norm_back(da[u:u + UNIT, :], slope_ref[i, rows, :], n_ref[i, rows, :], r_ref[i, rows, :])
        shift = shift + wf
        held.append(wn)
        if len(held) == GROUP:
            gain = gain + column_sums(held)
            held = []
        ds = s_ref[rows, :]
        bias = bias + ds
        ds = ds + d_in
        s_ref[rows, :] = ds
        low_ref[rows, :] = ds.astype(BF16)
    return gain, shift, bias


def fold(x):
    return jnp.sum(x, axis=0, keepdims=True)


def backward_layers(chunk_rows, first, last, layers, s_ref, low_ref, save, w_ref, w_at, save_at, gw_ref, gv_ref, g_at):
    def layer(j, carry):
        i = last - 1 - j
        def chunk(c, carry):
            base = pl.multiple_of(c * chunk_rows, UNIT)
            sums = backward_chunk(base, chunk_rows, s_ref, low_ref, save, i - save_at, w_ref[i - w_at], gw_ref, i - g_at)
            for k in range(3):
                gv_ref[pl.ds(7 + k * layers + i, 1), :] += fold(sums[k])
            return carry
        return lax.fori_loop(0, TILE // chunk_rows, chunk, carry)
    lax.fori_loop(0, last - first, layer, 0)


def cross(logits, target, mask, lane):
    top = jnp.max(logits, axis=1, keepdims=True)
    shifted = logits - top
    expon = jnp.exp(shifted)
    total = jnp.sum(expon, axis=1, keepdims=True)
    hit = lane == target
    grad = expon * (mask * (1.0 / total))
    grad = grad - jnp.where(hit, mask, 0.0)
    return jnp.log(total), jnp.where(hit, shifted, 0.0), grad


def heads_chunk(base, nq, s_ref, low_ref, col_ref, w_ref, w_at, hb_ref, latents_ref, value_ref, chance_ref, dlog_ref, loss_ref, ghb_ref):
    size = HEAD_CHUNK
    span = pl.ds(base, size)
    lane_v = lax.broadcasted_iota(jnp.int32, (1, 640), 1).astype(F32)
    lane_c = lane_v[:, 0:128]
    bias_v = hb_ref[0:1, 0:640]
    bias_c = hb_ref[0:1, 640:768]
    lat = s_ref[span, :].astype(BF16)
    latents_ref[span, :] = lat
    full = [mm(lat, w_ref[w_at + k]) for k in range(3)]
    loss = jnp.zeros((UNIT, 128), F32)
    sum_v = jnp.zeros((UNIT, 640), F32)
    sum_c = jnp.zeros((UNIT, 128), F32)
    for u in range(0, size, UNIT):
        rows = pl.ds(base + u, UNIT)
        parts = [f[u:u + UNIT, :] for f in full]
        value = jnp.concatenate([parts[0], parts[1], parts[2][:, 0:128]], axis=1) + bias_v
        chance = parts[2][:, 128:256] + bias_c
        value_ref[rows, :] = value[:, 0:nq].astype(BF16)
        chance_ref[rows, :] = chance[:, 0:chance_ref.shape[1]].astype(BF16)
        bins, codes, mask = (col_ref[k, rows, :] for k in range(3))
        wide = lambda x: jnp.concatenate([x] * 5, axis=1)
        log_v, at_v, grad_v = cross(value, wide(bins), wide(mask), lane_v)
        log_c, at_c, grad_c = cross(chance, codes, mask, lane_c)
        hits = at_c
        for k in range(5):
            hits = hits + at_v[:, k * 128:(k + 1) * 128]
        loss = loss + mask * ((log_v + log_c) * (1.0 / 128) - hits)
        sum_v = sum_v + grad_v
        sum_c = sum_c + grad_c
        dlog_ref[0, rows, :] = grad_v[:, 0:256].astype(BF16)
        dlog_ref[1, rows, :] = grad_v[:, 256:512].astype(BF16)
        dlog_ref[2, rows, 0:128] = grad_v[:, 512:640].astype(BF16)
        dlog_ref[2, rows, 128:256] = grad_c.astype(BF16)
    loss_ref[...] += loss
    ghb_ref[:, 0:640] += sum_v
    ghb_ref[:, 640:768] += sum_c
    ds = mm_nt(dlog_ref[0, span, :], w_ref[w_at])
    ds += mm_nt(dlog_ref[1, span, :], w_ref[w_at + 1])
    ds += mm_nt(dlog_ref[2, span, :], w_ref[w_at + 2])
    s_ref[span, :] = ds
    low_ref[span, :] = ds.astype(BF16)


def spread_columns(ints, col_ref):
    k = lax.broadcasted_iota(jnp.int32, (16, 384), 0)
    j = lax.broadcasted_iota(jnp.int32, (16, 384), 1) >> 7
    pick = jnp.where((j == 0) & (k == 1), 32.0, 0.0) + jnp.where(
        ((j == 0) & (k == 2)) | ((j == 1) & (k == 3)) | ((j == 2) & (k == 4)), 1.0, 0.0
    )
    cols = mm_tn(ints, pick.astype(BF16))
    for c in range(3):
        col_ref[c] = cols[0:TILE, c * 128:(c + 1) * 128]


def unpack_vec(w, vec_ref):
    vec_ref[...] = w[:, 0:128].astype(F32).T


def moves_hot(ints):
    rows = lax.broadcasted_iota(jnp.int32, ints.shape, 0).astype(F32)
    return jnp.where((rows == ints[0:1, :].astype(F32)) | (rows == 4.0), 1.0, 0.0).astype(BF16)


def table_of(vec_ref):
    rows = lax.broadcasted_iota(jnp.int32, (16, WIDTH), 0)
    return jnp.where(rows < 5, vec_ref[0:16, :], 0.0).astype(BF16)


def stem_forward(chunk_rows, latent_ref, hot_ref, vec_ref, w, s_ref, n_ref, slope_ref, r_ref, n_at):
    table = table_of(vec_ref)
    scale = scales(vec_ref, 5, 1)
    def chunk(c, carry):
        base = pl.multiple_of(c * chunk_rows, UNIT)
        span = pl.ds(base, chunk_rows)
        pre = mm(latent_ref[span, :], w) + mm(hot_ref[span, :], table)
        for u in range(0, chunk_rows, UNIT):
            rows = pl.ds(base + u, UNIT)
            act, n, slope, r = norm_gelu(pre[u:u + UNIT, :], *scale)
            s_ref[rows, :] = act
            n_ref[n_at, rows, :] = n
            slope_ref[n_at, rows, :] = slope
            r_ref[n_at, rows, :] = r
        return carry
    lax.fori_loop(0, TILE // chunk_rows, chunk, 0)


def stem_backward(chunk_rows, latent_ref, hot, s_ref, low_ref, n_ref, slope_ref, r_ref, n_at, w, lgrad_ref, gw_ref, g_at, gv_ref):
    def chunk(c, carry):
        base = pl.multiple_of(c * chunk_rows, UNIT)
        span = pl.ds(base, chunk_rows)
        shift = jnp.zeros((UNIT, WIDTH), F32)
        gain = shift
        held = []
        for u in range(0, chunk_rows, UNIT):
            rows = pl.ds(base + u, UNIT)
            d_in, wf, wn = norm_back(s_ref[rows, :], slope_ref[n_at, rows, :], n_ref[n_at, rows, :], r_ref[n_at, rows, :])
            shift = shift + wf
            held.append(wn)
            if len(held) == GROUP:
                gain = gain + column_sums(held)
                held = []
            low_ref[rows, :] = d_in.astype(BF16)
        low = low_ref[span, :]
        lgrad_ref[span, :] = mm_nt(low, w).astype(BF16)
        gw_ref[g_at] += mm_tn(latent_ref[span, :], low)
        gv_ref[5:6, :] += fold(gain)
        gv_ref[6:7, :] += fold(shift)
        return carry
    lax.fori_loop(0, TILE // chunk_rows, chunk, 0)
    rows = lax.broadcasted_iota(jnp.int32, (16, WIDTH), 0)
    gv_ref[0:16, :] += jnp.where(rows < 5, mm(hot[:, 0:TILE], low_ref[...]), 0.0)


def clean_latent(latent_ref, lat_ref, rows_dev):
    lat_ref[...] = latent_ref[...]
    steps = -(-rows_dev // TILE)
    tail = rows_dev - (steps - 1) * TILE
    if tail < TILE:
        @pl.when(pl.program_id(0) == steps - 1)
        def _():
            lat_ref[tail:TILE, :] = jnp.zeros((TILE - tail, WIDTH), BF16)


def split_low(x):
    high = x.astype(BF16)
    return high, (x - high.astype(F32)).astype(BF16)


def put_pieces(out_refs, spot, at, matrix):
    rows = out_refs[0].shape[1]
    if len(out_refs) == 1:
        out_refs[0][at] = matrix(pl.ds(0, rows))
    else:
        for k, ref in enumerate(out_refs):
            ref[at] = matrix(pl.ds(pl.multiple_of((spot ^ k) * rows, rows), rows))


def assemble_kernel(pieces, first, spots_ref, *refs):
    ins, (front_ref, own_ref) = refs[:pieces], refs[pieces:]
    rows = ins[0].shape[1]
    for k, ref in enumerate(ins):
        span = pl.ds(pl.multiple_of((spots_ref[1] ^ k) * rows, rows), rows)
        for m in range(ref.shape[0]):
            if m < first:
                front_ref[m, span, :] = ref[m]
            else:
                own_ref[m - first, span, :] = ref[m]


def first_kernel(layers, rows_dev, latent_ref, ints_ref, w_ref, act_ref, n_ref, slope_ref, r_ref, s_ref, vec_ref, lat_ref, hot_ref):
    @pl.when(pl.program_id(0) == 0)
    def _():
        unpack_vec(w_ref[0], vec_ref)

    clean_latent(latent_ref, lat_ref, rows_dev)
    hot_ref[...] = moves_hot(ints_ref[0]).T[0:TILE]
    stem_forward(720, lat_ref, hot_ref, vec_ref, w_ref[1], s_ref, n_ref, slope_ref, r_ref, SPLIT)
    forward_layers(1440, 0, SPLIT, layers, s_ref, (act_ref, n_ref, slope_ref, r_ref), vec_ref, w_ref, -2, 0)


def middle_kernel(
    layers, nq, sources, pieces, spots_ref, s_in_ref, ints_ref, vec_ref, hb_ref, *refs
):
    src = refs[:sources]
    latents_ref, value_ref, chance_ref, ds_ref, gv_ref, rep_ref = refs[sources:sources + 6]
    outs = refs[sources + 6:sources + 6 + pieces]
    w_ref, col_ref, act_ref, n_ref, slope_ref, r_ref, low_ref, dlog_ref, gw_ref, ghb_ref, loss_ref = refs[sources + 6 + pieces:]
    blocks = layers - SPLIT
    step = pl.program_id(0)

    @pl.when(step == 0)
    def _():
        for ref in (gw_ref, gv_ref, ghb_ref, loss_ref):
            ref[...] = jnp.zeros_like(ref)
        each = src[0].shape[0]
        for d, ref in enumerate(src):
            for m in range(each):
                w_ref[(spots_ref[0] ^ d) * each + m if sources > 1 else m] = ref[m]

    spread_columns(ints_ref[0], col_ref)
    ds_ref[...] = s_in_ref[...]
    save = (act_ref, n_ref, slope_ref, r_ref)
    forward_layers(1440, SPLIT, layers, layers, ds_ref, save, vec_ref, w_ref, SPLIT, SPLIT)

    def head(c, carry):
        base = pl.multiple_of(c * HEAD_CHUNK, UNIT)
        heads_chunk(base, nq, ds_ref, low_ref, col_ref, w_ref, blocks, hb_ref, latents_ref, value_ref, chance_ref, dlog_ref, loss_ref, ghb_ref)
        return carry

    lax.fori_loop(0, TILE // HEAD_CHUNK, head, 0)

    def head_grad(k, carry):
        gw_ref[blocks + k] += mm_tn(latents_ref[...], dlog_ref[k])
        return carry

    lax.fori_loop(0, 3, head_grad, 0)
    backward_layers(1440, SPLIT, layers, layers, ds_ref, low_ref, save, w_ref, SPLIT, SPLIT, gw_ref, gv_ref, SPLIT)

    @pl.when(step == pl.num_programs(0) - 1)
    def _():
        def put(m, carry):
            put_pieces(outs, spots_ref[1], m, lambda rows: gw_ref[m, rows, :].astype(BF16))
            return carry

        lax.fori_loop(0, blocks + 3, put, 0)
        sums = fold(ghb_ref[...])
        row = lax.broadcasted_iota(jnp.int32, (8, WIDTH), 0)
        total = jnp.where(row == 3, jnp.concatenate([fold(loss_ref[...]), jnp.zeros((1, 128), F32)], axis=1), 0.0)
        for k in range(3):
            total = jnp.where(row == k, sums[:, k * 256:(k + 1) * 256], total)
        high, low = split_low(total)
        rep_ref[...] = jnp.concatenate([high, low], axis=0)


def last_kernel(
    layers, pieces, rows_dev, spots_ref, latent_ref, ints_ref, ds_in_ref, act_ref, n_ref, slope_ref, r_ref, w_ref, gv_in_ref, *refs
):
    lgrad_ref = refs[0]
    outs = refs[1:1 + pieces]
    lat_ref, ds_ref, low_ref, gw_ref, gv_ref = refs[1 + pieces:]
    step = pl.program_id(0)

    @pl.when(step == 0)
    def _():
        gw_ref[...] = jnp.zeros_like(gw_ref)
        gv_ref[...] = gv_in_ref[...]

    clean_latent(latent_ref, lat_ref, rows_dev)
    ds_ref[...] = ds_in_ref[...]
    low_ref[...] = ds_in_ref[...].astype(BF16)
    backward_layers(1440, 0, SPLIT, layers, ds_ref, low_ref, (act_ref, n_ref, slope_ref, r_ref), w_ref, -2, 0, gw_ref, gv_ref, -1)
    stem_backward(720, lat_ref, moves_hot(ints_ref[0]), ds_ref, low_ref, n_ref, slope_ref, r_ref, SPLIT, w_ref[1], lgrad_ref, gw_ref, 0, gv_ref)

    @pl.when(step == pl.num_programs(0) - 1)
    def _():
        for m in range(SPLIT + 1):
            put_pieces(outs, spots_ref[1], m, lambda rows: gw_ref[m, rows, :].astype(BF16))
        wide = jnp.concatenate([gv_ref[...], jnp.zeros((128 - gv_ref.shape[0], WIDTH), F32)], axis=0).T
        high, low = split_low(wide)
        gw_ref[0] = jnp.concatenate([high, low], axis=1).astype(F32)
        put_pieces(outs, spots_ref[1], SPLIT + 1, lambda rows: gw_ref[0, rows, :].astype(BF16))


def sum_kernel(count, split, *refs):
    ins, out_ref = refs[:count], refs[count]
    for m in range(out_ref.shape[0]):
        total = ins[0][m].astype(F32)
        for ref in ins[1:]:
            total = total + ref[m].astype(F32)
        if m == split:
            high, low = split_low(total[:, 0:128] + total[:, 128:256])
            out_ref[m] = jnp.concatenate([high, low], axis=1)
        else:
            out_ref[m] = total.astype(BF16)


def sum_rep_kernel(count, *refs):
    ins, out_ref = refs[:count], refs[count]
    total = ins[0][...].astype(F32)
    for ref in ins[1:]:
        total = total + ref[...].astype(F32)
    high, low = split_low(total[0:8] + total[8:16])
    out_ref[...] = jnp.concatenate([high, low], axis=0)


SMEM = pl.BlockSpec(memory_space=pltpu.SMEM)
VMEM = pl.BlockSpec(memory_space=pltpu.VMEM)


def params(mib):
    return pltpu.CompilerParams(vmem_limit_bytes=mib << 20)


def tiled(shape, dim):
    block = shape[:dim] + (TILE,) + shape[dim + 1:]
    return pl.BlockSpec(block, lambda i: (0,) * dim + (i,) + (0,) * (len(shape) - dim - 1))


def whole(shape):
    return pl.BlockSpec(shape, lambda i: (0,) * len(shape))


def once(shape):
    return pl.BlockSpec(shape, lambda i: (0,) * len(shape), pipeline_mode=pl.Buffered(1))


def struct(shape, dtype):
    return jax.ShapeDtypeStruct(shape, dtype)


def exchange(x, axis, size):
    return [lax.ppermute(x, axis, [(i, i ^ k) for i in range(size)]) for k in range(1, size)]


def send_pieces(pieces, axis):
    size = len(pieces)
    return [lax.ppermute(pieces[k], axis, [(i, i ^ k) for i in range(size)]) for k in range(1, size)]


def per_device(
    latent, actions, value_bins, chance_codes, step_mask, stem_weight, action_table, stem_bias, stem_gain, stem_shift,
    block_weight, block_gain, block_shift, block_bias, value_weight, value_bias, chance_weight, chance_bias,
):
    n_dp, n_fsdp = lax.axis_size("dp"), lax.axis_size("fsdp")
    rows_dev = latent.shape[0]
    layers, shard = block_weight.shape[0], block_weight.shape[1]
    nq, nc = value_weight.shape[1], chance_weight.shape[1]
    moves = action_table.shape[0]
    steps = -(-rows_dev // TILE)
    padded = steps * TILE
    fast = shard % 16 == 0 and n_dp & (n_dp - 1) == 0 and n_fsdp & (n_fsdp - 1) == 0
    dp, fsdp = lax.axis_index("dp"), lax.axis_index("fsdp")
    spots = jnp.stack([dp, fsdp]).astype(jnp.int32)

    vectors = jnp.concatenate(
        [action_table, stem_bias[None], stem_gain[None], stem_shift[None], block_gain, block_shift, block_bias], axis=0
    )
    vectors = jnp.pad(vectors.T, ((0, 0), (0, WIDTH - vectors.shape[0])))
    head = jnp.concatenate(
        [value_weight, jnp.zeros((shard, 640 - nq), BF16), chance_weight, jnp.zeros((shard, 128 - nc), BF16)], axis=1
    )
    head = jnp.stack([head[:, k * WIDTH:(k + 1) * WIDTH] for k in range(3)])
    front = jnp.concatenate([vectors[None], stem_weight[None], block_weight[:SPLIT]], axis=0)
    back = jnp.concatenate([block_weight[SPLIT:], head], axis=0)
    n_front, n_back = front.shape[0], back.shape[0]
    if fast:
        each = -(-n_back // n_dp)
        back = jnp.pad(back, ((0, each * n_dp - n_back), (0, 0), (0, 0)))
        mine = jnp.concatenate([front, lax.dynamic_slice_in_dim(back, dp * each, each, 0)], axis=0)
        got = [mine] + exchange(mine, "fsdp", n_fsdp)
        w_front, own = pl.pallas_call(
            functools.partial(assemble_kernel, n_fsdp, n_front),
            in_specs=[SMEM] + [VMEM] * n_fsdp,
            out_specs=[VMEM] * 2,
            out_shape=[struct((n_front, WIDTH, WIDTH), BF16), struct((each, WIDTH, WIDTH), BF16)],
            name="assemble",
        )(spots, *got)
        sources = [own] + exchange(own, "dp", n_dp)
        pieces, piece_rows = n_fsdp, shard
    else:
        w_front = lax.all_gather(front, "fsdp", axis=1, tiled=True)
        sources = [lax.all_gather(back, "fsdp", axis=1, tiled=True)]
        pieces, piece_rows = 1, WIDTH

    ints = jnp.stack([actions, value_bins >> 5, value_bins & 31, chance_codes, step_mask])
    ints = jnp.pad(ints.astype(BF16), ((0, 11), (0, padded - rows_dev))).reshape(16, steps, TILE).transpose(1, 0, 2)
    width = -(-TILE // 128) * 128
    ints = jnp.pad(ints, ((0, 0), (0, 0), (0, width - TILE)))
    ints_spec = pl.BlockSpec((1, 16, width), lambda i: (i, 0, 0))
    low = lambda n: jnp.full((n,), -1e30, F32)
    head_bias = jnp.concatenate([value_bias.astype(F32), low(640 - nq), chance_bias.astype(F32), low(128 - nc)])
    head_bias = jnp.broadcast_to(head_bias[None], (8, 3 * WIDTH))

    saved = [
        struct((SPLIT, padded, WIDTH), BF16),
        struct((SPLIT + 1, padded, WIDTH), BF16),
        struct((SPLIT + 1, padded, WIDTH), BF16),
        struct((SPLIT + 1, padded, 128), F32),
    ]
    stream = struct((padded, WIDTH), F32)
    scratch = pltpu.VMEM
    *held, s_mid, vec = pl.pallas_call(
        functools.partial(first_kernel, layers, rows_dev),
        grid=(steps,),
        in_specs=[tiled((rows_dev, WIDTH), 0), ints_spec, once(w_front.shape)],
        out_specs=[tiled(x.shape, 1) for x in saved] + [tiled(stream.shape, 0), whole((128, WIDTH))],
        out_shape=saved + [stream, struct((128, WIDTH), F32)],
        scratch_shapes=[scratch((TILE, WIDTH), BF16), scratch((TILE, 16), BF16)],
        compiler_params=params(60),
        cost_estimate=pl.CostEstimate(flops=4 * rows_dev * WIDTH * WIDTH * 40, bytes_accessed=60 << 20, transcendentals=0),
        name="first",
    )(latent, ints, w_front)

    blocks = layers - SPLIT
    latents, value_logits, chance_logits, ds_mid, gv_mid, rep, *parts_mid = pl.pallas_call(
        functools.partial(middle_kernel, layers, nq, len(sources), pieces),
        grid=(steps,),
        in_specs=[SMEM, tiled(stream.shape, 0), ints_spec, once(vec.shape), once(head_bias.shape)]
        + [once(x.shape) for x in sources],
        out_specs=[
            tiled((rows_dev, WIDTH), 0), tiled((rows_dev, nq), 0), tiled((rows_dev, nc), 0), tiled(stream.shape, 0),
            whole((48, WIDTH)), whole((16, WIDTH)),
        ] + [whole((blocks + 3, piece_rows, WIDTH))] * pieces,
        out_shape=[
            struct((rows_dev, WIDTH), BF16), struct((rows_dev, nq), BF16), struct((rows_dev, nc), BF16), stream,
            struct((48, WIDTH), F32), struct((16, WIDTH), BF16),
        ] + [struct((blocks + 3, piece_rows, WIDTH), BF16)] * pieces,
        scratch_shapes=[
            scratch((sources[0].shape[0] * len(sources), WIDTH, WIDTH), BF16),
            scratch((3, TILE, 128), F32),
            scratch((blocks, TILE, WIDTH), BF16),
            scratch((blocks, TILE, WIDTH), BF16),
            scratch((blocks, TILE, WIDTH), BF16),
            scratch((blocks, TILE, 128), F32),
            scratch((TILE, WIDTH), BF16),
            scratch((3, TILE, WIDTH), BF16),
            scratch((blocks + 3, WIDTH, WIDTH), F32),
            scratch((UNIT, 3 * WIDTH), F32),
            scratch((UNIT, 128), F32),
        ],
        compiler_params=params(62),
        cost_estimate=pl.CostEstimate(flops=4 * rows_dev * WIDTH * WIDTH * 200, bytes_accessed=40 << 20, transcendentals=0),
        name="middle",
    )(spots, s_mid, ints, vec, head_bias, *sources)

    latent_grad, *parts_end = pl.pallas_call(
        functools.partial(last_kernel, layers, pieces, rows_dev),
        grid=(steps,),
        in_specs=[SMEM, tiled((rows_dev, WIDTH), 0), ints_spec, tiled(stream.shape, 0)]
        + [tiled(x.shape, 1) for x in saved]
        + [once(w_front.shape), once((48, WIDTH))],
        out_specs=[tiled((rows_dev, WIDTH), 0)] + [whole((SPLIT + 2, piece_rows, WIDTH))] * pieces,
        out_shape=[struct((rows_dev, WIDTH), BF16)] + [struct((SPLIT + 2, piece_rows, WIDTH), BF16)] * pieces,
        scratch_shapes=[
            scratch((TILE, WIDTH), BF16),
            scratch((TILE, WIDTH), F32),
            scratch((TILE, WIDTH), BF16),
            scratch((SPLIT + 1, WIDTH, WIDTH), F32),
            scratch((48, WIDTH), F32),
        ],
        compiler_params=params(60),
        cost_estimate=pl.CostEstimate(flops=4 * rows_dev * WIDTH * WIDTH * 40, bytes_accessed=60 << 20, transcendentals=0),
        name="last",
    )(spots, latent, ints, ds_mid, *held, w_front, gv_mid)

    if fast:
        def add(arrays, split, name):
            return pl.pallas_call(
                functools.partial(sum_kernel, len(arrays), split),
                in_specs=[VMEM] * len(arrays), out_specs=VMEM,
                out_shape=struct(arrays[0].shape, BF16), name=name,
            )(*arrays)

        def add_rep(arrays, name):
            return pl.pallas_call(
                functools.partial(sum_rep_kernel, len(arrays)),
                in_specs=[VMEM] * len(arrays), out_specs=VMEM,
                out_shape=struct(arrays[0].shape, BF16), name=name,
            )(*arrays)

        mid = add([parts_mid[0]] + send_pieces(parts_mid, "fsdp"), -1, "sum_mid")
        rep = add_rep([rep] + exchange(rep, "fsdp", n_fsdp), "sum_rep")
        end = add([parts_end[0]] + send_pieces(parts_end, "fsdp"), SPLIT + 1, "sum_end")
        total = lambda x: sum((y.astype(F32) for y in exchange(x, "dp", n_dp)), x.astype(F32))
        mid, rep, end = total(mid), total(rep), total(end)
    else:
        scatter = lambda x: lax.psum(
            lax.psum_scatter(x, "fsdp", scatter_dimension=1, tiled=True).astype(F32), "dp"
        )
        mid, end = scatter(parts_mid[0]), scatter(parts_end[0])
        rep = lax.psum(rep.astype(F32), ("dp", "fsdp"))

    scale = 1.0 / (rows_dev * n_dp * n_fsdp)
    rep = (rep[0:8] + rep[8:16]) * scale
    head_grad = jnp.concatenate([mid[blocks + k] for k in range(3)], axis=1) * scale
    small = (end[SPLIT + 1, :, 0:128] + end[SPLIT + 1, :, 128:256]).T * scale
    bias_sums = rep[0:3].reshape(3 * WIDTH)
    at = moves + 3
    gain = block_gain.astype(F32)
    return (
        latents,
        value_logits,
        chance_logits,
        jnp.sum(rep[3]),
        latent_grad,
        end[0] * scale,
        small[0:moves],
        small[moves],
        small[moves + 1] / stem_gain.astype(F32),
        small[moves + 2] / (16.0 * stem_gain.astype(F32)),
        jnp.concatenate([end[1:SPLIT + 1], mid[:blocks]], axis=0) * scale,
        small[at:at + layers] / gain,
        small[at + layers:at + 2 * layers] / (16.0 * gain),
        small[at + 2 * layers:at + 3 * layers],
        head_grad[:, 0:nq],
        bias_sums[0:nq],
        head_grad[:, 640:640 + nc],
        bias_sums[640:640 + nc],
    )


def solution(mesh):
    placed = (
        P(("dp", "fsdp"), None),
        P(("dp", "fsdp")),
        P(("dp", "fsdp")),
        P(("dp", "fsdp")),
        P(("dp", "fsdp")),
        P("fsdp", None),
        P(None, "fsdp"),
        P("fsdp"),
        P("fsdp"),
        P("fsdp"),
        P(None, "fsdp", None),
        P(None, "fsdp"),
        P(None, "fsdp"),
        P(None, "fsdp"),
        P("fsdp", None),
        P(),
        P("fsdp", None),
        P(),
    )
    return jax.shard_map(
        per_device,
        mesh=mesh,
        in_specs=placed,
        out_specs=(
            P(("dp", "fsdp"), None),
            P(("dp", "fsdp"), None),
            P(("dp", "fsdp"), None),
            P(),
            P(("dp", "fsdp"), None),
            P("fsdp", None),
            P(None, "fsdp"),
            P("fsdp"),
            P("fsdp"),
            P("fsdp"),
            P(None, "fsdp", None),
            P(None, "fsdp"),
            P(None, "fsdp"),
            P(None, "fsdp"),
            P("fsdp", None),
            P(),
            P("fsdp", None),
            P(),
        ),
        check_vma=False,
    )
```

```python
import functools
import jax
import jax.numpy as jnp
from jax import lax
from jax.experimental import pallas as pl
from jax.experimental.pallas import tpu as pltpu
from jax.sharding import PartitionSpec as P

F32 = jnp.float32
BF16 = jnp.bfloat16
WIDTH = 256
UNIT = 16
TILE = 1920
CHUNK = 640
PARTS = TILE // CHUNK
HEAD_CHUNK = 384
SPLIT = 4
K0 = 2 * 0.7978845608028654
K1 = 8 * 0.7978845608028654 * 0.044715


def mm(a, b):
    return lax.dot_general(a, b, (((1,), (0,)), ((), ())), preferred_element_type=F32)


def mm_nt(a, b):
    return lax.dot_general(a, b, (((1,), (1,)), ((), ())), preferred_element_type=F32)


def mm_tn(a, b):
    return lax.dot_general(a, b, (((0,), (0,)), ((), ())), preferred_element_type=F32)


def norm_gelu(s, gain8, gain_slope, shift_half):
    mean = jnp.sum(s, axis=1, keepdims=True) * (1.0 / WIDTH)
    center = s - mean
    r = lax.rsqrt(jnp.sum(center * center, axis=1, keepdims=True) + WIDTH * 1e-5)
    n = center * r
    h = n * gain8 + shift_half
    y = h * h
    t = jnp.tanh(h * (K0 + K1 * y))
    e1 = 1.0 + t
    bend = (h * (y + K0 / (3 * K1))) * (1.0 - t)
    slope = (e1 * gain_slope) * (1.0 / (3 * K1) + bend)
    return h * e1, n.astype(BF16), slope.astype(BF16), jnp.broadcast_to(r, (UNIT, 128))


def scales(vec_ref, at, layers):
    gain = vec_ref[pl.ds(at, 1), :]
    return gain * 8.0, gain * (8.0 * 3 * K1), vec_ref[pl.ds(at + layers, 1), :] * 0.5


def norm_back(da, slope, n, r):
    w = da * slope.astype(F32)
    m1 = jnp.sum(w, axis=1, keepdims=True) * (1.0 / WIDTH)
    w16 = w.astype(BF16)
    wn = w16 * n
    wide = (wn[:, 0:128] + wn[:, 128:256]).astype(F32)
    m2 = jnp.sum(wide, axis=1, keepdims=True)
    m1 = jnp.broadcast_to(m1, (UNIT, 128)).astype(BF16)
    m2 = jnp.broadcast_to(m2, (UNIT, 128)).astype(BF16)
    halves = [
        (w[:, k:k + 128] - (m1 + n[:, k:k + 128] * m2).astype(F32)) * r for k in (0, 128)
    ]
    return jnp.concatenate(halves, axis=1), w, wn


def rows_of(c):
    return pl.multiple_of(c * CHUNK, UNIT)


def activate(base, s_ref, save, i, scale):
    act_ref, n_ref, slope_ref, r_ref = save
    for u in range(0, CHUNK, UNIT):
        rows = pl.ds(base + u, UNIT)
        act, n, slope, r = norm_gelu(s_ref[rows, :], *scale)
        act_ref[i, rows, :] = act.astype(BF16)
        n_ref[i, rows, :] = n
        slope_ref[i, rows, :] = slope
        r_ref[i, rows, :] = r


def forward_layers(first, last, layers, s_ref, save, vec_ref, w_ref, w_at, save_at):
    act_ref = save[0]

    def product(t):
        i, c = first + lax.div(t, PARTS), lax.rem(t, PARTS)
        return mm(act_ref[i - save_at, pl.ds(rows_of(c), CHUNK), :], w_ref[i - w_at])

    def activation(t):
        i, c = first + lax.div(t, PARTS), lax.rem(t, PARTS)
        activate(rows_of(c), s_ref, save, i - save_at, scales(vec_ref, 7 + i, layers))

    def residual(t, out):
        i, c = first + lax.div(t, PARTS), lax.rem(t, PARTS)
        bias = vec_ref[pl.ds(7 + 2 * layers + i, 1), :]
        for u in range(0, CHUNK, UNIT):
            rows = pl.ds(rows_of(c) + u, UNIT)
            s_ref[rows, :] = s_ref[rows, :] + (out[u:u + UNIT, :] + bias)

    def body(t, carry):
        out = product(t - 1)
        activation(t)
        residual(t - 1, out)
        return carry

    steps = (last - first) * PARTS
    activation(jnp.int32(0))
    lax.fori_loop(1, steps, body, 0)
    end = jnp.int32(steps - 1)
    residual(end, product(end))


def column_sums(parts):
    total = parts[0]
    for part in parts[1:]:
        total = total + part
    return total.astype(F32)


GROUP = 4


def fold(x):
    return jnp.sum(x, axis=0, keepdims=True)


def backward_layers(first, last, layers, s_ref, low_ref, da_ref, save, w_ref, w_at, save_at, gw_ref, gv_ref, g_at):
    act_ref, n_ref, slope_ref, r_ref = save
    steps = (last - first) * PARTS

    def place(t):
        return last - 1 - lax.div(t, PARTS), rows_of(lax.rem(t, PARTS))

    def product(t):
        i, base = place(t)
        return mm_nt(low_ref[pl.ds(base, CHUNK), :], w_ref[i - w_at])

    def body(t, carry):
        i, base = place(t)
        following = product(jnp.minimum(t + 1, steps - 1))
        gw_ref[i - g_at] += mm_tn(act_ref[i - save_at, pl.ds(base, CHUNK), :], low_ref[pl.ds(base, CHUNK), :])
        zero = jnp.zeros((UNIT, WIDTH), F32)
        shift, gain, bias = zero, zero, zero
        held = []
        for u in range(0, CHUNK, UNIT):
            rows = pl.ds(base + u, UNIT)
            at = (i - save_at, rows, slice(None))
            d_in, wf, wn = norm_back(da_ref[u:u + UNIT, :], slope_ref[at], n_ref[at], r_ref[at])
            shift = shift + wf
            held.append(wn)
            if len(held) == GROUP:
                gain = gain + column_sums(held)
                held = []
            ds = s_ref[rows, :]
            bias = bias + ds
            ds = ds + d_in
            s_ref[rows, :] = ds
            low_ref[rows, :] = ds.astype(BF16)
        da_ref[...] = following
        for k, x in enumerate((gain, shift, bias)):
            gv_ref[pl.ds(7 + k * layers + i, 1), :] += fold(x)
        return carry

    da_ref[...] = product(jnp.int32(0))
    lax.fori_loop(0, steps, body, 0)


def cross(logits, target, mask, lanes):
    top = functools.reduce(jnp.maximum, logits)
    shifted = [x - jnp.max(top, axis=1, keepdims=True) for x in logits]
    expon = [jnp.exp(x) for x in shifted]
    total = jnp.sum(functools.reduce(jnp.add, expon), axis=1, keepdims=True)
    weight = mask * (1.0 / total)
    hits = jnp.zeros_like(mask)
    grads = []
    for x, e, lane in zip(shifted, expon, lanes):
        hit = lane == target
        hits = jnp.where(hit, x, hits)
        grads.append(e * weight - jnp.where(hit, mask, 0.0))
    return jnp.log(total), hits, grads


def heads_chunk(c, nq, s_ref, low_ref, col_ref, w_ref, w_at, hb_ref, latents_ref, value_ref, chance_ref, dlog_ref, wide_ref, loss_ref, ghb_ref):
    size = HEAD_CHUNK
    base = pl.multiple_of(c * size, 128)
    span = pl.ds(base, size)
    lane = lax.broadcasted_iota(jnp.int32, (1, 128), 1).astype(F32)
    lanes = [lane + 128.0 * k for k in range(5)]
    bias = [hb_ref[0:1, k * 128:(k + 1) * 128] for k in range(6)]
    lat = s_ref[span, :].astype(BF16)
    latents_ref[span, :] = lat
    full = [mm(lat, w_ref[w_at + k]) for k in range(3)]
    loss = jnp.zeros((UNIT, 128), F32)
    sums = [jnp.zeros((UNIT, 128), F32)] * 6
    for u in range(0, size, UNIT):
        rows = pl.ds(base + u, UNIT)
        logits = [full[k // 2][u:u + UNIT, (k % 2) * 128:(k % 2 + 1) * 128] + bias[k] for k in range(6)]
        for k in range(6):
            wide_ref[k, u:u + UNIT, :] = logits[k].astype(BF16)
        bins, codes, mask = (col_ref[k, rows, :] for k in range(3))
        log_v, at_v, grad_v = cross(logits[:5], bins, mask, lanes)
        log_c, at_c, grad_c = cross(logits[5:], codes, mask, lanes[:1])
        loss = loss + mask * ((log_v + log_c) * (1.0 / 128) - (at_v + at_c))
        for k, grad in enumerate(grad_v + grad_c):
            sums[k] = sums[k] + grad
            dlog_ref[k // 2, rows, (k % 2) * 128:(k % 2 + 1) * 128] = grad.astype(BF16)
    loss_ref[...] += loss
    for k in range(6):
        ghb_ref[:, k * 128:(k + 1) * 128] += sums[k]
    for k in range(5):
        height = min(128, nq - k * 128)
        value_ref[k * 128:k * 128 + height, span] = wide_ref[k].T[0:height, :]
    chance_ref[:, span] = wide_ref[5].T[0:chance_ref.shape[0], :]
    ds = mm_nt(dlog_ref[0, span, :], w_ref[w_at])
    ds += mm_nt(dlog_ref[1, span, :], w_ref[w_at + 1])
    ds += mm_nt(dlog_ref[2, span, :], w_ref[w_at + 2])
    s_ref[span, :] = ds
    low_ref[span, :] = ds.astype(BF16)


def spread_columns(ints, col_ref):
    k = lax.broadcasted_iota(jnp.int32, (16, 384), 0)
    j = lax.broadcasted_iota(jnp.int32, (16, 384), 1) >> 7
    pick = jnp.where((j == 0) & (k == 1), 32.0, 0.0) + jnp.where(
        ((j == 0) & (k == 2)) | ((j == 1) & (k == 3)) | ((j == 2) & (k == 4)), 1.0, 0.0
    )
    cols = mm_tn(ints, pick.astype(BF16))
    for c in range(3):
        col_ref[c] = cols[:, c * 128:(c + 1) * 128]


def unpack_vec(w, vec_ref):
    vec_ref[...] = w[:, 0:128].astype(F32).T


def moves_hot(ints):
    rows = lax.broadcasted_iota(jnp.int32, ints.shape, 0).astype(F32)
    return jnp.where((rows == ints[0:1, :].astype(F32)) | (rows == 4.0), 1.0, 0.0).astype(BF16)


def table_of(vec_ref):
    rows = lax.broadcasted_iota(jnp.int32, (16, WIDTH), 0)
    return jnp.where(rows < 5, vec_ref[0:16, :], 0.0).astype(BF16)


def stem_forward(latent_ref, hot_ref, vec_ref, w, s_ref, n_ref, slope_ref, r_ref, n_at):
    table = table_of(vec_ref)
    scale = scales(vec_ref, 5, 1)

    def chunk(c, carry):
        base = rows_of(c)
        span = pl.ds(base, CHUNK)
        pre = mm(latent_ref[span, :], w) + mm(hot_ref[span, :], table)
        for u in range(0, CHUNK, UNIT):
            rows = pl.ds(base + u, UNIT)
            act, n, slope, r = norm_gelu(pre[u:u + UNIT, :], *scale)
            s_ref[rows, :] = act
            n_ref[n_at, rows, :] = n
            slope_ref[n_at, rows, :] = slope
            r_ref[n_at, rows, :] = r
        return carry

    lax.fori_loop(0, PARTS, chunk, 0)


def stem_backward(latent_ref, hot_ref, s_ref, low_ref, n_ref, slope_ref, r_ref, n_at, w, lgrad_ref, gw_ref, g_at, gv_ref):
    def chunk(c, carry):
        base = rows_of(c)
        span = pl.ds(base, CHUNK)
        shift = jnp.zeros((UNIT, WIDTH), F32)
        gain = shift
        held = []
        for u in range(0, CHUNK, UNIT):
            rows = pl.ds(base + u, UNIT)
            d_in, wf, wn = norm_back(s_ref[rows, :], slope_ref[n_at, rows, :], n_ref[n_at, rows, :], r_ref[n_at, rows, :])
            shift = shift + wf
            held.append(wn)
            if len(held) == GROUP:
                gain = gain + column_sums(held)
                held = []
            low_ref[rows, :] = d_in.astype(BF16)
        low = low_ref[span, :]
        lgrad_ref[span, :] = mm_nt(low, w).astype(BF16)
        gw_ref[g_at] += mm_tn(latent_ref[span, :], low)
        gv_ref[0:16, :] += mm_tn(hot_ref[span, :], low)
        gv_ref[5:6, :] += fold(gain)
        gv_ref[6:7, :] += fold(shift)
        return carry

    lax.fori_loop(0, PARTS, chunk, 0)


def clean_latent(latent_ref, lat_ref, rows_dev):
    lat_ref[...] = latent_ref[...]
    steps = -(-rows_dev // TILE)
    tail = rows_dev - (steps - 1) * TILE
    if tail < TILE:
        @pl.when(pl.program_id(0) == steps - 1)
        def _():
            lat_ref[tail:TILE, :] = jnp.zeros((TILE - tail, WIDTH), BF16)


def split_low(x):
    high = x.astype(BF16)
    return high, (x - high.astype(F32)).astype(BF16)


def join_pieces(pieces_ref, w_ref):
    rows = pieces_ref.shape[2]
    for f in range(pieces_ref.shape[0]):
        for m in range(pieces_ref.shape[1]):
            w_ref[m, f * rows:(f + 1) * rows, :] = pieces_ref[f, m]


def cut_pieces(out_ref, m, source_ref, at):
    rows = out_ref.shape[2]
    for f in range(out_ref.shape[0]):
        out_ref[f, m] = source_ref[at, f * rows:(f + 1) * rows, :].astype(BF16)


def first_kernel(layers, rows_dev, latent_ref, ints_ref, front_ref, act_ref, n_ref, slope_ref, r_ref, s_ref, vec_ref, w_ref, lat_ref, hot_ref):
    @pl.when(pl.program_id(0) == 0)
    def _():
        join_pieces(front_ref, w_ref)
        unpack_vec(w_ref[0], vec_ref)

    clean_latent(latent_ref, lat_ref, rows_dev)
    hot_ref[...] = moves_hot(ints_ref[0]).T
    stem_forward(lat_ref, hot_ref, vec_ref, w_ref[1], s_ref, n_ref, slope_ref, r_ref, SPLIT)
    forward_layers(0, SPLIT, layers, s_ref, (act_ref, n_ref, slope_ref, r_ref), vec_ref, w_ref, -2, 0)


def middle_kernel(
    layers, nq, s_in_ref, ints_ref, vec_ref, hb_ref, w_ref,
    latents_ref, value_ref, chance_ref, ds_ref, gv_ref, rep_ref, out_ref,
    col_ref, act_ref, n_ref, slope_ref, r_ref, low_ref, da_ref, dlog_ref, wide_ref, gw_ref, ghb_ref, loss_ref,
):
    blocks = layers - SPLIT
    step = pl.program_id(0)

    @pl.when(step == 0)
    def _():
        for ref in (gw_ref, gv_ref, ghb_ref, loss_ref):
            ref[...] = jnp.zeros_like(ref)

    spread_columns(ints_ref[0], col_ref)
    ds_ref[...] = s_in_ref[...]
    save = (act_ref, n_ref, slope_ref, r_ref)
    forward_layers(SPLIT, layers, layers, ds_ref, save, vec_ref, w_ref, SPLIT, SPLIT)

    def head(c, carry):
        heads_chunk(c, nq, ds_ref, low_ref, col_ref, w_ref, blocks, hb_ref, latents_ref, value_ref, chance_ref, dlog_ref, wide_ref, loss_ref, ghb_ref)
        return carry

    lax.fori_loop(0, TILE // HEAD_CHUNK, head, 0)

    def head_grad(k, carry):
        gw_ref[blocks + k] += mm_tn(latents_ref[...], dlog_ref[k])
        return carry

    lax.fori_loop(0, 3, head_grad, 0)
    backward_layers(SPLIT, layers, layers, ds_ref, low_ref, da_ref, save, w_ref, SPLIT, SPLIT, gw_ref, gv_ref, SPLIT)

    @pl.when(step == pl.num_programs(0) - 1)
    def _():
        def put(m, carry):
            cut_pieces(out_ref, m, gw_ref, m)
            return carry

        lax.fori_loop(0, blocks + 3, put, 0)
        sums = fold(ghb_ref[...])
        row = lax.broadcasted_iota(jnp.int32, (8, WIDTH), 0)
        total = jnp.where(row == 3, jnp.concatenate([fold(loss_ref[...]), jnp.zeros((1, 128), F32)], axis=1), 0.0)
        for k in range(3):
            total = jnp.where(row == k, sums[:, k * 256:(k + 1) * 256], total)
        rep_ref[...] = total


def last_kernel(
    layers, rows_dev, latent_ref, ints_ref, ds_in_ref, act_ref, n_ref, slope_ref, r_ref, front_ref, gv_in_ref,
    lgrad_ref, out_ref, w_ref, lat_ref, hot_ref, ds_ref, low_ref, da_ref, gw_ref, gv_ref,
):
    step = pl.program_id(0)

    @pl.when(step == 0)
    def _():
        join_pieces(front_ref, w_ref)
        gw_ref[...] = jnp.zeros_like(gw_ref)
        gv_ref[...] = gv_in_ref[...]

    clean_latent(latent_ref, lat_ref, rows_dev)
    hot_ref[...] = moves_hot(ints_ref[0]).T
    ds_ref[...] = ds_in_ref[...]
    low_ref[...] = ds_in_ref[...].astype(BF16)
    backward_layers(0, SPLIT, layers, ds_ref, low_ref, da_ref, (act_ref, n_ref, slope_ref, r_ref), w_ref, -2, 0, gw_ref, gv_ref, -1)
    stem_backward(lat_ref, hot_ref, ds_ref, low_ref, n_ref, slope_ref, r_ref, SPLIT, w_ref[1], lgrad_ref, gw_ref, 0, gv_ref)

    @pl.when(step == pl.num_programs(0) - 1)
    def _():
        for m in range(SPLIT + 1):
            cut_pieces(out_ref, m, gw_ref, m)
        wide = jnp.concatenate([gv_ref[...], jnp.zeros((128 - gv_ref.shape[0], WIDTH), F32)], axis=0).T
        high, low = split_low(wide)
        gw_ref[0] = jnp.concatenate([high, low], axis=1).astype(F32)
        cut_pieces(out_ref, SPLIT + 1, gw_ref, 0)


def sum_kernel(split, in_ref, out_ref):
    for m in range(out_ref.shape[0]):
        total = in_ref[0, m].astype(F32)
        for f in range(1, in_ref.shape[0]):
            total = total + in_ref[f, m].astype(F32)
        if m == split:
            high, low = split_low(total[:, 0:128] + total[:, 128:256])
            out_ref[m] = jnp.concatenate([high, low], axis=1)
        else:
            out_ref[m] = total.astype(BF16)


VMEM = pl.BlockSpec(memory_space=pltpu.VMEM)


def params(mib):
    return pltpu.CompilerParams(vmem_limit_bytes=mib << 20)


def tiled(shape, dim):
    block = shape[:dim] + (TILE,) + shape[dim + 1:]
    return pl.BlockSpec(block, lambda i: (0,) * dim + (i,) + (0,) * (len(shape) - dim - 1))


def whole(shape):
    return pl.BlockSpec(shape, lambda i: (0,) * len(shape))


def once(shape):
    return pl.BlockSpec(shape, lambda i: (0,) * len(shape), pipeline_mode=pl.Buffered(1))


def struct(shape, dtype):
    return jax.ShapeDtypeStruct(shape, dtype)


def exchange(x, axis, size):
    return [lax.ppermute(x, axis, [(i, i ^ k) for i in range(size)]) for k in range(1, size)]


def per_device(
    latent, actions, value_bins, chance_codes, step_mask, stem_weight, action_table, stem_bias, stem_gain, stem_shift,
    block_weight, block_gain, block_shift, block_bias, value_weight, value_bias, chance_weight, chance_bias,
):
    n_dp, n_fsdp = lax.axis_size("dp"), lax.axis_size("fsdp")
    rows_dev = latent.shape[0]
    layers, shard = block_weight.shape[0], block_weight.shape[1]
    nq, nc = value_weight.shape[1], chance_weight.shape[1]
    moves = action_table.shape[0]
    steps = -(-rows_dev // TILE)
    padded = steps * TILE
    fast = shard % 16 == 0 and n_dp & (n_dp - 1) == 0

    vectors = jnp.concatenate(
        [action_table, stem_bias[None], stem_gain[None], stem_shift[None], block_gain, block_shift, block_bias], axis=0
    )
    vectors = jnp.pad(vectors.T, ((0, 0), (0, WIDTH - vectors.shape[0])))
    head = jnp.concatenate(
        [value_weight, jnp.zeros((shard, 640 - nq), BF16), chance_weight, jnp.zeros((shard, 128 - nc), BF16)], axis=1
    )
    head = jnp.stack([head[:, k * WIDTH:(k + 1) * WIDTH] for k in range(3)])
    front = jnp.concatenate([vectors[None], stem_weight[None], block_weight[:SPLIT]], axis=0)
    back = jnp.concatenate([block_weight[SPLIT:], head], axis=0)
    if fast:
        pieces, piece_rows = n_fsdp, shard
        w_front = lax.all_to_all(jnp.broadcast_to(front[None], (n_fsdp,) + front.shape), "fsdp", 0, 0)
    else:
        pieces, piece_rows = 1, WIDTH
        w_front = lax.all_gather(front, "fsdp", axis=1, tiled=True)[None]
    w_back = lax.all_gather(back, "fsdp", axis=1, tiled=True)

    ints = jnp.stack([actions, value_bins >> 5, value_bins & 31, chance_codes, step_mask])
    ints = jnp.pad(ints.astype(BF16), ((0, 11), (0, padded - rows_dev))).reshape(16, steps, TILE).transpose(1, 0, 2)
    ints_spec = pl.BlockSpec((1, 16, TILE), lambda i: (i, 0, 0))
    low = lambda n: jnp.full((n,), -1e30, F32)
    head_bias = jnp.concatenate([value_bias.astype(F32), low(640 - nq), chance_bias.astype(F32), low(128 - nc)])
    head_bias = jnp.broadcast_to(head_bias[None], (8, 3 * WIDTH))

    saved = [
        struct((SPLIT, padded, WIDTH), BF16),
        struct((SPLIT + 1, padded, WIDTH), BF16),
        struct((SPLIT + 1, padded, WIDTH), BF16),
        struct((SPLIT + 1, padded, 128), F32),
    ]
    stream = struct((padded, WIDTH), F32)
    scratch = pltpu.VMEM
    front_shape = w_front.shape[1:2] + (WIDTH, WIDTH)
    *held, s_mid, vec = pl.pallas_call(
        functools.partial(first_kernel, layers, rows_dev),
        grid=(steps,),
        in_specs=[tiled((rows_dev, WIDTH), 0), ints_spec, once(w_front.shape)],
        out_specs=[tiled(x.shape, 1) for x in saved] + [tiled(stream.shape, 0), whole((128, WIDTH))],
        out_shape=saved + [stream, struct((128, WIDTH), F32)],
        scratch_shapes=[scratch(front_shape, BF16), scratch((TILE, WIDTH), BF16), scratch((TILE, 16), BF16)],
        compiler_params=params(62),
        cost_estimate=pl.CostEstimate(flops=rows_dev * WIDTH * WIDTH * 200, bytes_accessed=60 << 20, transcendentals=0),
        name="first",
    )(latent, ints, w_front)

    blocks = layers - SPLIT
    latents, value_logits, chance_logits, ds_mid, gv_mid, rep, parts_mid = pl.pallas_call(
        functools.partial(middle_kernel, layers, nq),
        grid=(steps,),
        in_specs=[tiled(stream.shape, 0), ints_spec, once(vec.shape), once(head_bias.shape), once(w_back.shape)],
        out_specs=[
            tiled((rows_dev, WIDTH), 0), tiled((nq, rows_dev), 1), tiled((nc, rows_dev), 1), tiled(stream.shape, 0),
            whole((48, WIDTH)), whole((8, WIDTH)), whole((pieces, blocks + 3, piece_rows, WIDTH)),
        ],
        out_shape=[
            struct((rows_dev, WIDTH), BF16), struct((nq, rows_dev), BF16), struct((nc, rows_dev), BF16), stream,
            struct((48, WIDTH), F32), struct((8, WIDTH), F32), struct((pieces, blocks + 3, piece_rows, WIDTH), BF16),
        ],
        scratch_shapes=[
            scratch((3, TILE, 128), F32),
            scratch((blocks, TILE, WIDTH), BF16),
            scratch((blocks, TILE, WIDTH), BF16),
            scratch((blocks, TILE, WIDTH), BF16),
            scratch((blocks, TILE, 128), F32),
            scratch((TILE, WIDTH), BF16),
            scratch((CHUNK, WIDTH), F32),
            scratch((3, TILE, WIDTH), BF16),
            scratch((6, HEAD_CHUNK, 128), BF16),
            scratch((blocks + 3, WIDTH, WIDTH), F32),
            scratch((UNIT, 3 * WIDTH), F32),
            scratch((UNIT, 128), F32),
        ],
        compiler_params=params(62),
        cost_estimate=pl.CostEstimate(flops=rows_dev * WIDTH * WIDTH * 600, bytes_accessed=40 << 20, transcendentals=0),
        name="middle",
    )(s_mid, ints, vec, head_bias, w_back)

    latent_grad, parts_end = pl.pallas_call(
        functools.partial(last_kernel, layers, rows_dev),
        grid=(steps,),
        in_specs=[tiled((rows_dev, WIDTH), 0), ints_spec, tiled(stream.shape, 0)]
        + [tiled(x.shape, 1) for x in saved]
        + [once(w_front.shape), once((48, WIDTH))],
        out_specs=[tiled((rows_dev, WIDTH), 0), whole((pieces, SPLIT + 2, piece_rows, WIDTH))],
        out_shape=[struct((rows_dev, WIDTH), BF16), struct((pieces, SPLIT + 2, piece_rows, WIDTH), BF16)],
        scratch_shapes=[
            scratch(front_shape, BF16),
            scratch((TILE, WIDTH), BF16),
            scratch((TILE, 16), BF16),
            scratch((TILE, WIDTH), F32),
            scratch((TILE, WIDTH), BF16),
            scratch((CHUNK, WIDTH), F32),
            scratch((SPLIT + 1, WIDTH, WIDTH), F32),
            scratch((48, WIDTH), F32),
        ],
        compiler_params=params(62),
        cost_estimate=pl.CostEstimate(flops=rows_dev * WIDTH * WIDTH * 150, bytes_accessed=60 << 20, transcendentals=0),
        name="last",
    )(latent, ints, ds_mid, *held, w_front, gv_mid)

    rep = lax.psum(rep, ("dp", "fsdp"))
    if fast:
        def reduce(parts, split, name):
            got = lax.all_to_all(parts, "fsdp", 0, 0)
            mine = pl.pallas_call(
                functools.partial(sum_kernel, split), in_specs=[VMEM], out_specs=VMEM,
                out_shape=struct(parts.shape[1:], BF16), name=name,
            )(got)
            return sum((y.astype(F32) for y in exchange(mine, "dp", n_dp)), mine.astype(F32))

        mid, end = reduce(parts_mid, -1, "sum_mid"), reduce(parts_end, SPLIT + 1, "sum_end")
    else:
        scatter = lambda x: lax.psum(
            lax.psum_scatter(x[0], "fsdp", scatter_dimension=1, tiled=True).astype(F32), "dp"
        )
        mid, end = scatter(parts_mid), scatter(parts_end)

    scale = 1.0 / (rows_dev * n_dp * n_fsdp)
    rep = rep * scale
    head_grad = jnp.concatenate([mid[blocks + k] for k in range(3)], axis=1) * scale
    small = (end[SPLIT + 1, :, 0:128] + end[SPLIT + 1, :, 128:256]).T * scale
    bias_sums = rep[0:3].reshape(3 * WIDTH)
    at = moves + 3
    gain = block_gain.astype(F32)
    return (
        latents,
        value_logits.T,
        chance_logits.T,
        jnp.sum(rep[3]),
        latent_grad,
        end[0] * scale,
        small[0:moves],
        small[moves],
        small[moves + 1] / stem_gain.astype(F32),
        small[moves + 2] / (16.0 * stem_gain.astype(F32)),
        jnp.concatenate([end[1:SPLIT + 1], mid[:blocks]], axis=0) * scale,
        small[at:at + layers] / gain,
        small[at + layers:at + 2 * layers] / (16.0 * gain),
        small[at + 2 * layers:at + 3 * layers],
        head_grad[:, 0:nq],
        bias_sums[0:nq],
        head_grad[:, 640:640 + nc],
        bias_sums[640:640 + nc],
    )


def solution(mesh):
    placed = (
        P(("dp", "fsdp"), None),
        P(("dp", "fsdp")),
        P(("dp", "fsdp")),
        P(("dp", "fsdp")),
        P(("dp", "fsdp")),
        P("fsdp", None),
        P(None, "fsdp"),
        P("fsdp"),
        P("fsdp"),
        P("fsdp"),
        P(None, "fsdp", None),
        P(None, "fsdp"),
        P(None, "fsdp"),
        P(None, "fsdp"),
        P("fsdp", None),
        P(),
        P("fsdp", None),
        P(),
    )
    return jax.shard_map(
        per_device,
        mesh=mesh,
        in_specs=placed,
        out_specs=(
            P(("dp", "fsdp"), None),
            P(("dp", "fsdp"), None),
            P(("dp", "fsdp"), None),
            P(),
            P(("dp", "fsdp"), None),
            P("fsdp", None),
            P(None, "fsdp"),
            P("fsdp"),
            P("fsdp"),
            P("fsdp"),
            P(None, "fsdp", None),
            P(None, "fsdp"),
            P(None, "fsdp"),
            P(None, "fsdp"),
            P("fsdp", None),
            P(),
            P("fsdp", None),
            P(),
        ),
        check_vma=False,
    )
```

```python
import functools
import jax
import jax.numpy as jnp
from jax import lax
from jax.experimental import pallas as pl
from jax.experimental.pallas import tpu as pltpu
from jax.sharding import PartitionSpec as P

F32 = jnp.float32
BF16 = jnp.bfloat16
WIDTH = 256
UNIT = 16
TILE = 1920
CHUNK = 640
PARTS = TILE // CHUNK
HEAD_CHUNK = 384
SPLIT = 4
K0 = 2 * 0.7978845608028654
K1 = 8 * 0.7978845608028654 * 0.044715


def mm(a, b):
    return lax.dot_general(a, b, (((1,), (0,)), ((), ())), preferred_element_type=F32)


def mm_nt(a, b):
    return lax.dot_general(a, b, (((1,), (1,)), ((), ())), preferred_element_type=F32)


def mm_tn(a, b):
    return lax.dot_general(a, b, (((0,), (0,)), ((), ())), preferred_element_type=F32)


def norm_gelu(s, gain8, gain_slope, shift_half):
    mean = jnp.sum(s, axis=1, keepdims=True) * (1.0 / WIDTH)
    center = s - mean
    r = lax.rsqrt(jnp.sum(center * center, axis=1, keepdims=True) + WIDTH * 1e-5)
    n = center * r
    h = n * gain8 + shift_half
    y = h * h
    t = jnp.tanh(h * (K0 + K1 * y))
    e1 = 1.0 + t
    bend = (h * (y + K0 / (3 * K1))) * (1.0 - t)
    slope = (e1 * gain_slope) * (1.0 / (3 * K1) + bend)
    return h * e1, n.astype(BF16), slope.astype(BF16), jnp.broadcast_to(r, (UNIT, 128))


def scales(vec_ref, at, layers):
    gain = vec_ref[pl.ds(at, 1), :]
    return gain * 8.0, gain * (8.0 * 3 * K1), vec_ref[pl.ds(at + layers, 1), :] * 0.5


def norm_back(da, slope, n, r):
    w = da * slope.astype(F32)
    m1 = jnp.sum(w, axis=1, keepdims=True) * (1.0 / WIDTH)
    w16 = w.astype(BF16)
    wn = w16 * n
    wide = (wn[:, 0:128] + wn[:, 128:256]).astype(F32)
    m2 = jnp.sum(wide, axis=1, keepdims=True)
    m1 = jnp.broadcast_to(m1, (UNIT, 128)).astype(BF16)
    m2 = jnp.broadcast_to(m2, (UNIT, 128)).astype(BF16)
    halves = [
        (w[:, k:k + 128] - (m1 + n[:, k:k + 128] * m2).astype(F32)) * r for k in (0, 128)
    ]
    return jnp.concatenate(halves, axis=1), w, wn


def rows_of(c):
    return pl.multiple_of(c * CHUNK, UNIT)


def activate(base, s_ref, save, i, scale):
    act_ref, n_ref, slope_ref, r_ref = save
    for u in range(0, CHUNK, UNIT):
        rows = pl.ds(base + u, UNIT)
        act, n, slope, r = norm_gelu(s_ref[rows, :], *scale)
        act_ref[i, rows, :] = act.astype(BF16)
        n_ref[i, rows, :] = n
        slope_ref[i, rows, :] = slope
        r_ref[i, rows, :] = r


def forward_layers(first, last, layers, s_ref, save, vec_ref, w_ref, w_at, save_at, after=None):
    act_ref = save[0]

    def product(t):
        i, c = first + lax.div(t, PARTS), lax.rem(t, PARTS)
        return mm(act_ref[i - save_at, pl.ds(rows_of(c), CHUNK), :], w_ref[i - w_at])

    def activation(t):
        i, c = first + lax.div(t, PARTS), lax.rem(t, PARTS)
        activate(rows_of(c), s_ref, save, i - save_at, scales(vec_ref, 7 + i, layers))

    def residual(t, out):
        i, c = first + lax.div(t, PARTS), lax.rem(t, PARTS)
        bias = vec_ref[pl.ds(7 + 2 * layers + i, 1), :]
        for u in range(0, CHUNK, UNIT):
            rows = pl.ds(rows_of(c) + u, UNIT)
            s_ref[rows, :] = s_ref[rows, :] + (out[u:u + UNIT, :] + bias)

    def body(t, carry):
        out = product(t - 1)
        activation(t)
        residual(t - 1, out)
        if after is not None:
            after(first + lax.div(t, PARTS), lax.rem(t, PARTS))
        return carry

    steps = (last - first) * PARTS
    activation(jnp.int32(0))
    lax.fori_loop(1, steps, body, 0)
    end = jnp.int32(steps - 1)
    residual(end, product(end))


def column_sums(parts):
    total = parts[0]
    for part in parts[1:]:
        total = total + part
    return total.astype(F32)


GROUP = 4


def fold(x):
    return jnp.sum(x, axis=0, keepdims=True)


def backward_layers(first, last, layers, s_ref, low_ref, da_ref, save, w_ref, w_at, save_at, gw_ref, gv_ref, g_at, after=None):
    act_ref, n_ref, slope_ref, r_ref = save
    steps = (last - first) * PARTS

    def place(t):
        return last - 1 - lax.div(t, PARTS), rows_of(lax.rem(t, PARTS))

    def product(t):
        i, base = place(t)
        return mm_nt(low_ref[pl.ds(base, CHUNK), :], w_ref[i - w_at])

    def body(t, carry):
        i, base = place(t)
        following = product(jnp.minimum(t + 1, steps - 1))
        gw_ref[i - g_at] += mm_tn(act_ref[i - save_at, pl.ds(base, CHUNK), :], low_ref[pl.ds(base, CHUNK), :])
        zero = jnp.zeros((UNIT, WIDTH), F32)
        shift, gain, bias = zero, zero, zero
        held = []
        for u in range(0, CHUNK, UNIT):
            rows = pl.ds(base + u, UNIT)
            at = (i - save_at, rows, slice(None))
            d_in, wf, wn = norm_back(da_ref[u:u + UNIT, :], slope_ref[at], n_ref[at], r_ref[at])
            shift = shift + wf
            held.append(wn)
            if len(held) == GROUP:
                gain = gain + column_sums(held)
                held = []
            ds = s_ref[rows, :]
            bias = bias + ds
            ds = ds + d_in
            s_ref[rows, :] = ds
            low_ref[rows, :] = ds.astype(BF16)
        da_ref[...] = following
        for k, x in enumerate((gain, shift, bias)):
            gv_ref[pl.ds(7 + k * layers + i, 1), :] += fold(x)
        if after is not None:
            after(i, lax.rem(t, PARTS))
        return carry

    da_ref[...] = product(jnp.int32(0))
    lax.fori_loop(0, steps, body, 0)


def cross(logits, target, mask, lanes):
    top = functools.reduce(jnp.maximum, logits)
    shifted = [x - jnp.max(top, axis=1, keepdims=True) for x in logits]
    expon = [jnp.exp(x) for x in shifted]
    total = jnp.sum(functools.reduce(jnp.add, expon), axis=1, keepdims=True)
    weight = mask * (1.0 / total)
    hits = jnp.zeros_like(mask)
    grads = []
    for x, e, lane in zip(shifted, expon, lanes):
        hit = lane == target
        hits = jnp.where(hit, x, hits)
        grads.append(e * weight - jnp.where(hit, mask, 0.0))
    return jnp.log(total), hits, grads


def heads_chunk(c, nq, s_ref, low_ref, col_ref, w_ref, w_at, hb_ref, latents_ref, value_ref, chance_ref, dlog_ref, wide_ref, loss_ref, ghb_ref):
    size = HEAD_CHUNK
    base = pl.multiple_of(c * size, 128)
    span = pl.ds(base, size)
    lane = lax.broadcasted_iota(jnp.int32, (1, 128), 1).astype(F32)
    lanes = [lane + 128.0 * k for k in range(5)]
    bias = [hb_ref[0:1, k * 128:(k + 1) * 128] for k in range(6)]
    lat = s_ref[span, :].astype(BF16)
    latents_ref[span, :] = lat
    full = [mm(lat, w_ref[w_at + k]) for k in range(3)]
    loss = jnp.zeros((UNIT, 128), F32)
    sums = [jnp.zeros((UNIT, 128), F32)] * 6
    for u in range(0, size, UNIT):
        rows = pl.ds(base + u, UNIT)
        logits = [full[k // 2][u:u + UNIT, (k % 2) * 128:(k % 2 + 1) * 128] + bias[k] for k in range(6)]
        for k in range(6):
            wide_ref[k, u:u + UNIT, :] = logits[k].astype(BF16)
        bins, codes, mask = (col_ref[k, rows, :] for k in range(3))
        log_v, at_v, grad_v = cross(logits[:5], bins, mask, lanes)
        log_c, at_c, grad_c = cross(logits[5:], codes, mask, lanes[:1])
        loss = loss + mask * ((log_v + log_c) * (1.0 / 128) - (at_v + at_c))
        for k, grad in enumerate(grad_v + grad_c):
            sums[k] = sums[k] + grad
            dlog_ref[k // 2, rows, (k % 2) * 128:(k % 2 + 1) * 128] = grad.astype(BF16)
    loss_ref[...] += loss
    for k in range(6):
        ghb_ref[:, k * 128:(k + 1) * 128] += sums[k]
    for k in range(5):
        height = min(128, nq - k * 128)
        value_ref[k * 128:k * 128 + height, span] = wide_ref[k].T[0:height, :]
    chance_ref[:, span] = wide_ref[5].T[0:chance_ref.shape[0], :]
    ds = mm_nt(dlog_ref[0, span, :], w_ref[w_at])
    ds += mm_nt(dlog_ref[1, span, :], w_ref[w_at + 1])
    ds += mm_nt(dlog_ref[2, span, :], w_ref[w_at + 2])
    s_ref[span, :] = ds
    low_ref[span, :] = ds.astype(BF16)


def spread_columns(ints, col_ref):
    k = lax.broadcasted_iota(jnp.int32, (16, 384), 0)
    j = lax.broadcasted_iota(jnp.int32, (16, 384), 1) >> 7
    pick = jnp.where((j == 0) & (k == 1), 32.0, 0.0) + jnp.where(
        ((j == 0) & (k == 2)) | ((j == 1) & (k == 3)) | ((j == 2) & (k == 4)), 1.0, 0.0
    )
    cols = mm_tn(ints, pick.astype(BF16))
    for c in range(3):
        col_ref[c] = cols[:, c * 128:(c + 1) * 128]


def unpack_vec(w, vec_ref):
    vec_ref[...] = w[:, 0:128].astype(F32).T


def moves_hot(ints):
    rows = lax.broadcasted_iota(jnp.int32, ints.shape, 0).astype(F32)
    return jnp.where((rows == ints[0:1, :].astype(F32)) | (rows == 4.0), 1.0, 0.0).astype(BF16)


def table_of(vec_ref):
    rows = lax.broadcasted_iota(jnp.int32, (16, WIDTH), 0)
    return jnp.where(rows < 5, vec_ref[0:16, :], 0.0).astype(BF16)


def stem_forward(latent_ref, hot_ref, vec_ref, w, s_ref, n_ref, slope_ref, r_ref, n_at):
    table = table_of(vec_ref)
    scale = scales(vec_ref, 5, 1)

    def chunk(c, carry):
        base = rows_of(c)
        span = pl.ds(base, CHUNK)
        pre = mm(latent_ref[span, :], w) + mm(hot_ref[span, :], table)
        for u in range(0, CHUNK, UNIT):
            rows = pl.ds(base + u, UNIT)
            act, n, slope, r = norm_gelu(pre[u:u + UNIT, :], *scale)
            s_ref[rows, :] = act
            n_ref[n_at, rows, :] = n
            slope_ref[n_at, rows, :] = slope
            r_ref[n_at, rows, :] = r
        return carry

    lax.fori_loop(0, PARTS, chunk, 0)


def stem_backward(latent_ref, hot_ref, s_ref, low_ref, n_ref, slope_ref, r_ref, n_at, w, lgrad_ref, gw_ref, g_at, gv_ref):
    def chunk(c, carry):
        base = rows_of(c)
        span = pl.ds(base, CHUNK)
        shift = jnp.zeros((UNIT, WIDTH), F32)
        gain = shift
        held = []
        for u in range(0, CHUNK, UNIT):
            rows = pl.ds(base + u, UNIT)
            d_in, wf, wn = norm_back(s_ref[rows, :], slope_ref[n_at, rows, :], n_ref[n_at, rows, :], r_ref[n_at, rows, :])
            shift = shift + wf
            held.append(wn)
            if len(held) == GROUP:
                gain = gain + column_sums(held)
                held = []
            low_ref[rows, :] = d_in.astype(BF16)
        low = low_ref[span, :]
        lgrad_ref[span, :] = mm_nt(low, w).astype(BF16)
        gw_ref[g_at] += mm_tn(latent_ref[span, :], low)
        gv_ref[0:16, :] += mm_tn(hot_ref[span, :], low)
        gv_ref[5:6, :] += fold(gain)
        gv_ref[6:7, :] += fold(shift)
        return carry

    lax.fori_loop(0, PARTS, chunk, 0)


def clean_latent(latent_ref, lat_ref, rows_dev):
    lat_ref[...] = latent_ref[...]
    steps = -(-rows_dev // TILE)
    tail = rows_dev - (steps - 1) * TILE
    if tail < TILE:
        @pl.when(pl.program_id(0) == steps - 1)
        def _():
            lat_ref[tail:TILE, :] = jnp.zeros((TILE - tail, WIDTH), BF16)


def split_low(x):
    high = x.astype(BF16)
    return high, (x - high.astype(F32)).astype(BF16)


def join_pieces(pieces_ref, w_ref):
    rows = pieces_ref.shape[2]
    for f in range(pieces_ref.shape[0]):
        for m in range(pieces_ref.shape[1]):
            w_ref[m, f * rows:(f + 1) * rows, :] = pieces_ref[f, m]


def cut_pieces(out_ref, m, source_ref, at):
    rows = out_ref.shape[2]
    for f in range(out_ref.shape[0]):
        out_ref[f, m] = source_ref[at, f * rows:(f + 1) * rows, :].astype(BF16)


def copies(refs, away, sems, i, span, inward):
    out = []
    for k, (near, far) in enumerate(zip(refs, away)):
        ends = (far.at[i, span, :], near.at[i]) if inward else (near.at[i], far.at[i, span, :])
        out.append(pltpu.make_async_copy(*ends, sems.at[i, k]))
    return out


def tile_span(step):
    return pl.ds(pl.multiple_of(step * TILE, 128), TILE)


def first_kernel(
    layers, rows_dev, latent_ref, ints_ref, front_ref, n_out, slope_out, r_out, act_out, s_ref, vec_ref,
    w_ref, lat_ref, hot_ref, n_ref, slope_ref, r_ref, act_ref, sems,
):
    step, steps = pl.program_id(0), pl.num_programs(0)
    span = tile_span(step)
    refs, away = (n_ref, slope_ref, r_ref, act_ref), (n_out, slope_out, r_out, act_out)

    def start(i, count=4):
        for copy in copies(refs[:count], away, sems, i, span, False):
            copy.start()

    def wait(i, count=4):
        for copy in copies(refs[:count], away, sems, i, span, False):
            copy.wait()

    @pl.when(step == 0)
    def _():
        join_pieces(front_ref, w_ref)
        unpack_vec(w_ref[0], vec_ref)

    clean_latent(latent_ref, lat_ref, rows_dev)
    hot_ref[...] = moves_hot(ints_ref[0]).T

    @pl.when(step > 0)
    def _():
        wait(SPLIT, 3)

    stem_forward(lat_ref, hot_ref, vec_ref, w_ref[1], s_ref, n_ref, slope_ref, r_ref, SPLIT)
    start(SPLIT, 3)

    def after(i, c):
        @pl.when(c == PARTS - 1)
        def _():
            start(i)

            @pl.when((step > 0) & (i < SPLIT - 1))
            def _():
                wait(i + 1)

    @pl.when(step > 0)
    def _():
        wait(0)

    save = (act_ref, n_ref, slope_ref, r_ref)
    forward_layers(0, SPLIT, layers, s_ref, save, vec_ref, w_ref, -2, 0, after)

    @pl.when(step == steps - 1)
    def _():
        wait(SPLIT, 3)
        for i in range(SPLIT):
            wait(i)


def middle_kernel(
    layers, nq, s_in_ref, ints_ref, vec_ref, hb_ref, w_ref,
    latents_ref, value_ref, chance_ref, ds_ref, gv_ref, rep_ref, out_ref,
    col_ref, act_ref, n_ref, slope_ref, r_ref, low_ref, da_ref, dlog_ref, wide_ref, gw_ref, ghb_ref, loss_ref,
):
    blocks = layers - SPLIT
    step = pl.program_id(0)

    @pl.when(step == 0)
    def _():
        for ref in (gw_ref, gv_ref, ghb_ref, loss_ref):
            ref[...] = jnp.zeros_like(ref)

    spread_columns(ints_ref[0], col_ref)
    ds_ref[...] = s_in_ref[...]
    save = (act_ref, n_ref, slope_ref, r_ref)
    forward_layers(SPLIT, layers, layers, ds_ref, save, vec_ref, w_ref, SPLIT, SPLIT)

    def head(c, carry):
        heads_chunk(c, nq, ds_ref, low_ref, col_ref, w_ref, blocks, hb_ref, latents_ref, value_ref, chance_ref, dlog_ref, wide_ref, loss_ref, ghb_ref)
        return carry

    lax.fori_loop(0, TILE // HEAD_CHUNK, head, 0)

    def head_grad(k, carry):
        gw_ref[blocks + k] += mm_tn(latents_ref[...], dlog_ref[k])
        return carry

    lax.fori_loop(0, 3, head_grad, 0)
    backward_layers(SPLIT, layers, layers, ds_ref, low_ref, da_ref, save, w_ref, SPLIT, SPLIT, gw_ref, gv_ref, SPLIT)

    @pl.when(step == pl.num_programs(0) - 1)
    def _():
        def put(m, carry):
            cut_pieces(out_ref, m, gw_ref, m)
            return carry

        lax.fori_loop(0, blocks + 3, put, 0)
        sums = fold(ghb_ref[...])
        row = lax.broadcasted_iota(jnp.int32, (8, WIDTH), 0)
        total = jnp.where(row == 3, jnp.concatenate([fold(loss_ref[...]), jnp.zeros((1, 128), F32)], axis=1), 0.0)
        for k in range(3):
            total = jnp.where(row == k, sums[:, k * 256:(k + 1) * 256], total)
        rep_ref[...] = total
        if out_ref.shape[1] > blocks + 3:
            high, low = split_low(total)
            halves = jnp.concatenate([high, low], axis=0)
            for f in range(out_ref.shape[0]):
                out_ref[f, blocks + 3, 0:16, :] = halves
                out_ref[f, blocks + 3, 16:, :] = jnp.zeros_like(out_ref[f, blocks + 3, 16:, :])


def last_kernel(
    layers, rows_dev, latent_ref, ints_ref, ds_in_ref, n_in, slope_in, r_in, act_in, front_ref, gv_in_ref,
    lgrad_ref, out_ref, w_ref, lat_ref, hot_ref, ds_ref, low_ref, da_ref, n_ref, slope_ref, r_ref, act_ref, gw_ref, gv_ref, sems,
):
    step, steps = pl.program_id(0), pl.num_programs(0)
    refs, away = (n_ref, slope_ref, r_ref, act_ref), (n_in, slope_in, r_in, act_in)

    def start(i, to, count=4):
        for copy in copies(refs[:count], away, sems, i, tile_span(to), True):
            copy.start()

    def wait(i, count=4):
        for copy in copies(refs[:count], away, sems, i, tile_span(step), True):
            copy.wait()

    @pl.when(step == 0)
    def _():
        for i in reversed(range(SPLIT)):
            start(i, 0)
        start(SPLIT, 0, 3)
        join_pieces(front_ref, w_ref)
        gw_ref[...] = jnp.zeros_like(gw_ref)
        gv_ref[...] = gv_in_ref[...]

    clean_latent(latent_ref, lat_ref, rows_dev)
    hot_ref[...] = moves_hot(ints_ref[0]).T
    ds_ref[...] = ds_in_ref[...]
    low_ref[...] = ds_in_ref[...].astype(BF16)

    def after(i, c):
        @pl.when(c == PARTS - 1)
        def _():
            @pl.when(step < steps - 1)
            def _():
                start(i, step + 1)

            @pl.when(i > 0)
            def _():
                wait(i - 1)

    wait(SPLIT - 1)
    save = (act_ref, n_ref, slope_ref, r_ref)
    backward_layers(0, SPLIT, layers, ds_ref, low_ref, da_ref, save, w_ref, -2, 0, gw_ref, gv_ref, -1, after)
    wait(SPLIT, 3)
    stem_backward(lat_ref, hot_ref, ds_ref, low_ref, n_ref, slope_ref, r_ref, SPLIT, w_ref[1], lgrad_ref, gw_ref, 0, gv_ref)

    @pl.when(step < steps - 1)
    def _():
        start(SPLIT, step + 1, 3)

    @pl.when(step == steps - 1)
    def _():
        for m in range(SPLIT + 1):
            cut_pieces(out_ref, m, gw_ref, m)
        wide = jnp.concatenate([gv_ref[...], jnp.zeros((128 - gv_ref.shape[0], WIDTH), F32)], axis=0).T
        high, low = split_low(wide)
        gw_ref[0] = jnp.concatenate([high, low], axis=1).astype(F32)
        cut_pieces(out_ref, SPLIT + 1, gw_ref, 0)


def pack_kernel(
    stem_ref, table_ref, stem_vec_ref, block_ref, gain_ref, shift_ref, bias_ref, value_ref, chance_ref, front_ref, back_ref, vec_ref
):
    layers, shard = block_ref.shape[0], block_ref.shape[1]
    moves = table_ref.shape[0]
    vec_ref[...] = jnp.zeros_like(vec_ref)
    at = 0
    for ref in (table_ref, stem_vec_ref, gain_ref, shift_ref, bias_ref):
        vec_ref[at:at + ref.shape[0], 0:shard] = ref[...].astype(F32)
        at += ref.shape[0]
    vectors = vec_ref[...].T[0:shard, :]
    vectors = jnp.concatenate([vectors, jnp.zeros_like(vectors)], axis=1).astype(BF16)
    for f in range(front_ref.shape[0]):
        front_ref[f, 0] = vectors
        front_ref[f, 1] = stem_ref[...]
        for i in range(SPLIT):
            front_ref[f, 2 + i] = block_ref[i]
    for i in range(SPLIT, layers):
        back_ref[i - SPLIT] = block_ref[i]
    at = layers - SPLIT
    back_ref[at:] = jnp.zeros_like(back_ref[at:])
    nq, nc = value_ref.shape[1], chance_ref.shape[1]
    for k in range(3):
        width = min(WIDTH, nq - k * WIDTH)
        back_ref[at + k, :, 0:width] = value_ref[:, k * WIDTH:k * WIDTH + width]
    back_ref[at + 2, :, 128:128 + nc] = chance_ref[...]


def sum_kernel(mid, mid_ref, end_ref, out_ref):
    def total_of(ref, m):
        total = ref[0, m].astype(F32)
        for f in range(1, ref.shape[0]):
            total = total + ref[f, m].astype(F32)
        return total

    for m in range(mid):
        out_ref[m] = total_of(mid_ref, m).astype(BF16)
    total = total_of(mid_ref, mid)
    high, low = split_low(total[0:8] + total[8:16])
    out_ref[mid] = jnp.zeros_like(out_ref[mid])
    out_ref[mid, 0:16, :] = jnp.concatenate([high, low], axis=0)
    count = end_ref.shape[1]
    for m in range(count - 1):
        out_ref[mid + 1 + m] = total_of(end_ref, m).astype(BF16)
    total = total_of(end_ref, count - 1)
    high, low = split_low(total[:, 0:128] + total[:, 128:256])
    out_ref[mid + count] = jnp.concatenate([high, low], axis=1)


def finish_kernel(
    count, scale, stem_vec_ref, gain_ref, *refs
):
    ins = refs[:count]
    (
        loss_ref, stem_ref, table_ref, stem_bias_ref, stem_gain_ref, stem_shift_ref, block_ref, block_gain_ref, block_shift_ref,
        block_bias_ref, value_ref, value_bias_ref, chance_ref, chance_bias_ref,
    ) = refs[count:]
    layers, moves = block_ref.shape[0], table_ref.shape[0]
    nq, nc = value_ref.shape[1], chance_ref.shape[1]
    mid = layers - SPLIT + 3

    def total_of(m):
        total = ins[0][m].astype(F32)
        for ref in ins[1:]:
            total = total + ref[m].astype(F32)
        return total * scale

    for i in range(SPLIT, layers):
        block_ref[i] = total_of(i - SPLIT)
    for i in range(SPLIT):
        block_ref[i] = total_of(mid + 2 + i)
    stem_ref[...] = total_of(mid + 1)
    for k in range(3):
        width = min(WIDTH, nq - k * WIDTH)
        part = total_of(layers - SPLIT + k)
        value_ref[:, k * WIDTH:k * WIDTH + width] = part[:, 0:width]
    chance_ref[...] = part[:, 128:128 + nc]
    rep = total_of(mid)
    rep = rep[0:8] + rep[8:16] if rep.shape[0] >= 16 else rep
    bias = jnp.concatenate([rep[k:k + 1] for k in range(3)], axis=1)
    value_bias_ref[...] = bias[:, 0:nq]
    chance_bias_ref[...] = bias[:, 640:640 + nc]
    loss_ref[...] = jnp.sum(rep[3:4], axis=1, keepdims=True)
    small = total_of(mid + 2 + SPLIT)
    small = small[:, 0:128] + small[:, 128:256]
    shard = small.shape[0]
    if shard < 128:
        small = jnp.concatenate([small, jnp.zeros((128 - shard, 128), F32)], axis=0)
    small = small.T[:, 0:shard]
    table_ref[...] = small[0:moves]
    stem_gain = stem_vec_ref[1:2, :].astype(F32)
    stem_bias_ref[...] = small[moves:moves + 1]
    stem_gain_ref[...] = small[moves + 1:moves + 2] / stem_gain
    stem_shift_ref[...] = small[moves + 2:moves + 3] / (16.0 * stem_gain)
    at = moves + 3
    gain = gain_ref[...].astype(F32)
    block_gain_ref[...] = small[at:at + layers] / gain
    block_shift_ref[...] = small[at + layers:at + 2 * layers] / (16.0 * gain)
    block_bias_ref[...] = small[at + 2 * layers:at + 3 * layers]


VMEM = pl.BlockSpec(memory_space=pltpu.VMEM)
ANY = pl.BlockSpec(memory_space=pl.ANY)


def params(mib):
    return pltpu.CompilerParams(vmem_limit_bytes=mib << 20)


def tiled(shape, dim):
    block = shape[:dim] + (TILE,) + shape[dim + 1:]
    return pl.BlockSpec(block, lambda i: (0,) * dim + (i,) + (0,) * (len(shape) - dim - 1))


def whole(shape):
    return pl.BlockSpec(shape, lambda i: (0,) * len(shape))


def once(shape):
    return pl.BlockSpec(shape, lambda i: (0,) * len(shape), pipeline_mode=pl.Buffered(1))


def struct(shape, dtype):
    return jax.ShapeDtypeStruct(shape, dtype)


def exchange(x, axis, size):
    return [lax.ppermute(x, axis, [(i, i ^ k) for i in range(size)]) for k in range(1, size)]


def per_device(
    latent, actions, value_bins, chance_codes, step_mask, stem_weight, action_table, stem_bias, stem_gain, stem_shift,
    block_weight, block_gain, block_shift, block_bias, value_weight, value_bias, chance_weight, chance_bias,
):
    n_dp, n_fsdp = lax.axis_size("dp"), lax.axis_size("fsdp")
    rows_dev = latent.shape[0]
    layers, shard = block_weight.shape[0], block_weight.shape[1]
    nq, nc = value_weight.shape[1], chance_weight.shape[1]
    moves = action_table.shape[0]
    steps = -(-rows_dev // TILE)
    padded = steps * TILE
    fast = shard % 16 == 0 and n_dp & (n_dp - 1) == 0

    pieces, piece_rows = (n_fsdp, shard) if fast else (1, WIDTH)
    stem_vec = jnp.stack([stem_bias, stem_gain, stem_shift])
    front, back = pl.pallas_call(
        pack_kernel,
        in_specs=[VMEM] * 9,
        out_specs=[VMEM] * 2,
        out_shape=[
            struct((pieces, 2 + SPLIT, shard, WIDTH), BF16), struct((layers - SPLIT + 3, shard, WIDTH), BF16),
        ],
        scratch_shapes=[pltpu.VMEM((128, max(shard, 128)), F32)],
        name="pack",
    )(stem_weight, action_table, stem_vec, block_weight, block_gain, block_shift, block_bias, value_weight, chance_weight)
    if fast:
        w_front = lax.all_to_all(front, "fsdp", 0, 0)
    else:
        w_front = lax.all_gather(front, "fsdp", axis=2, tiled=True)
    w_back = lax.all_gather(back, "fsdp", axis=1, tiled=True)

    ints = jnp.stack([actions, value_bins >> 5, value_bins & 31, chance_codes, step_mask])
    ints = jnp.pad(ints.astype(BF16), ((0, 11), (0, padded - rows_dev))).reshape(16, steps, TILE).transpose(1, 0, 2)
    ints_spec = pl.BlockSpec((1, 16, TILE), lambda i: (i, 0, 0))
    low = lambda n: jnp.full((n,), -1e30, F32)
    head_bias = jnp.concatenate([value_bias.astype(F32), low(640 - nq), chance_bias.astype(F32), low(128 - nc)])
    head_bias = jnp.broadcast_to(head_bias[None], (8, 3 * WIDTH))

    saved = [
        struct((SPLIT + 1, padded, WIDTH), BF16),
        struct((SPLIT + 1, padded, WIDTH), BF16),
        struct((SPLIT + 1, padded, 128), F32),
        struct((SPLIT, padded, WIDTH), BF16),
    ]
    scratch = pltpu.VMEM
    kept = [scratch((x.shape[0], TILE, x.shape[2]), x.dtype) for x in saved] + [pltpu.SemaphoreType.DMA((SPLIT + 1, 4))]
    stream = struct((padded, WIDTH), F32)
    front_shape = w_front.shape[1:2] + (WIDTH, WIDTH)
    *held, s_mid, vec = pl.pallas_call(
        functools.partial(first_kernel, layers, rows_dev),
        grid=(steps,),
        in_specs=[tiled((rows_dev, WIDTH), 0), ints_spec, once(w_front.shape)],
        out_specs=[ANY] * 4 + [tiled(stream.shape, 0), whole((128, WIDTH))],
        out_shape=saved + [stream, struct((128, WIDTH), F32)],
        scratch_shapes=[scratch(front_shape, BF16), scratch((TILE, WIDTH), BF16), scratch((TILE, 16), BF16)] + kept,
        compiler_params=params(62),
        cost_estimate=pl.CostEstimate(flops=rows_dev * WIDTH * WIDTH * 200, bytes_accessed=60 << 20, transcendentals=0),
        name="first",
    )(latent, ints, w_front)

    blocks = layers - SPLIT
    mid_shape = (pieces, blocks + (4 if fast else 3), piece_rows, WIDTH)
    latents, value_logits, chance_logits, ds_mid, gv_mid, rep, parts_mid = pl.pallas_call(
        functools.partial(middle_kernel, layers, nq),
        grid=(steps,),
        in_specs=[tiled(stream.shape, 0), ints_spec, once(vec.shape), once(head_bias.shape), once(w_back.shape)],
        out_specs=[
            tiled((rows_dev, WIDTH), 0), tiled((nq, rows_dev), 1), tiled((nc, rows_dev), 1), tiled(stream.shape, 0),
            whole((48, WIDTH)), whole((8, WIDTH)), whole(mid_shape),
        ],
        out_shape=[
            struct((rows_dev, WIDTH), BF16), struct((nq, rows_dev), BF16), struct((nc, rows_dev), BF16), stream,
            struct((48, WIDTH), F32), struct((8, WIDTH), F32), struct(mid_shape, BF16),
        ],
        scratch_shapes=[
            scratch((3, TILE, 128), F32),
            scratch((blocks, TILE, WIDTH), BF16),
            scratch((blocks, TILE, WIDTH), BF16),
            scratch((blocks, TILE, WIDTH), BF16),
            scratch((blocks, TILE, 128), F32),
            scratch((TILE, WIDTH), BF16),
            scratch((CHUNK, WIDTH), F32),
            scratch((3, TILE, WIDTH), BF16),
            scratch((6, HEAD_CHUNK, 128), BF16),
            scratch((blocks + 3, WIDTH, WIDTH), F32),
            scratch((UNIT, 3 * WIDTH), F32),
            scratch((UNIT, 128), F32),
        ],
        compiler_params=params(62),
        cost_estimate=pl.CostEstimate(flops=rows_dev * WIDTH * WIDTH * 600, bytes_accessed=40 << 20, transcendentals=0),
        name="middle",
    )(s_mid, ints, vec, head_bias, w_back)

    latent_grad, parts_end = pl.pallas_call(
        functools.partial(last_kernel, layers, rows_dev),
        grid=(steps,),
        in_specs=[tiled((rows_dev, WIDTH), 0), ints_spec, tiled(stream.shape, 0)]
        + [ANY] * 4 + [once(w_front.shape), once((48, WIDTH))],
        out_specs=[tiled((rows_dev, WIDTH), 0), whole((pieces, SPLIT + 2, piece_rows, WIDTH))],
        out_shape=[struct((rows_dev, WIDTH), BF16), struct((pieces, SPLIT + 2, piece_rows, WIDTH), BF16)],
        scratch_shapes=[
            scratch(front_shape, BF16),
            scratch((TILE, WIDTH), BF16),
            scratch((TILE, 16), BF16),
            scratch((TILE, WIDTH), F32),
            scratch((TILE, WIDTH), BF16),
            scratch((CHUNK, WIDTH), F32),
        ] + kept[:4] + [
            scratch((SPLIT + 1, WIDTH, WIDTH), F32),
            scratch((48, WIDTH), F32),
        ] + kept[4:],
        compiler_params=params(62),
        cost_estimate=pl.CostEstimate(flops=rows_dev * WIDTH * WIDTH * 150, bytes_accessed=60 << 20, transcendentals=0),
        name="last",
    )(latent, ints, ds_mid, *held, w_front, gv_mid)

    count = blocks + 4 + SPLIT + 2
    if fast:
        got_mid = lax.all_to_all(parts_mid, "fsdp", 0, 0)
        parts_end, got_mid = lax.optimization_barrier((parts_end, got_mid))
        got_end = lax.all_to_all(parts_end, "fsdp", 0, 0)
        mine = pl.pallas_call(
            functools.partial(sum_kernel, blocks + 3),
            in_specs=[VMEM] * 2,
            out_specs=VMEM,
            out_shape=struct((count, shard, WIDTH), BF16),
            name="sum",
        )(got_mid, got_end)
        sums = [mine] + exchange(mine, "dp", n_dp)
    else:
        scatter = lambda x: lax.psum_scatter(x[0], "fsdp", scatter_dimension=1, tiled=True).astype(F32)
        sums = jnp.concatenate([scatter(parts_mid), jnp.zeros((1, shard, WIDTH), F32), scatter(parts_end)])
        rep = lax.psum(rep, ("dp", "fsdp"))
        sums = lax.psum(sums, "dp").at[blocks + 3, 0:8, :].set(rep)
        sums = [sums]

    shapes = [
        (1, 1), (shard, WIDTH), (moves, shard), (1, shard), (1, shard), (1, shard), (layers, shard, WIDTH), (layers, shard),
        (layers, shard), (layers, shard), (shard, nq), (1, nq), (shard, nc), (1, nc),
    ]
    (
        loss, stem_grad, table_grad, stem_bias_grad, stem_gain_grad, stem_shift_grad, block_grad, gain_grad, shift_grad, bias_grad,
        value_grad, value_bias_grad, chance_grad, chance_bias_grad,
    ) = pl.pallas_call(
        functools.partial(finish_kernel, len(sums), 1.0 / (rows_dev * n_dp * n_fsdp)),
        in_specs=[VMEM] * (2 + len(sums)),
        out_specs=[VMEM] * len(shapes),
        out_shape=[struct(x, F32) for x in shapes],
        name="finish",
    )(stem_vec, block_gain, *sums)
    return (
        latents,
        value_logits.T,
        chance_logits.T,
        loss.reshape(()),
        latent_grad,
        stem_grad,
        table_grad,
        stem_bias_grad.reshape(shard),
        stem_gain_grad.reshape(shard),
        stem_shift_grad.reshape(shard),
        block_grad,
        gain_grad,
        shift_grad,
        bias_grad,
        value_grad,
        value_bias_grad.reshape(nq),
        chance_grad,
        chance_bias_grad.reshape(nc),
    )


def solution(mesh):
    placed = (
        P(("dp", "fsdp"), None),
        P(("dp", "fsdp")),
        P(("dp", "fsdp")),
        P(("dp", "fsdp")),
        P(("dp", "fsdp")),
        P("fsdp", None),
        P(None, "fsdp"),
        P("fsdp"),
        P("fsdp"),
        P("fsdp"),
        P(None, "fsdp", None),
        P(None, "fsdp"),
        P(None, "fsdp"),
        P(None, "fsdp"),
        P("fsdp", None),
        P(),
        P("fsdp", None),
        P(),
    )
    return jax.shard_map(
        per_device,
        mesh=mesh,
        in_specs=placed,
        out_specs=(
            P(("dp", "fsdp"), None),
            P(("dp", "fsdp"), None),
            P(("dp", "fsdp"), None),
            P(),
            P(("dp", "fsdp"), None),
            P("fsdp", None),
            P(None, "fsdp"),
            P("fsdp"),
            P("fsdp"),
            P("fsdp"),
            P(None, "fsdp", None),
            P(None, "fsdp"),
            P(None, "fsdp"),
            P(None, "fsdp"),
            P("fsdp", None),
            P(),
            P("fsdp", None),
            P(),
        ),
        check_vma=False,
    )
```

```python
import functools
import jax
import jax.numpy as jnp
from jax import lax
from jax.experimental import pallas as pl
from jax.experimental.pallas import tpu as pltpu
from jax.sharding import PartitionSpec as P

F32 = jnp.float32
BF16 = jnp.bfloat16
WIDTH = 256
UNIT = 16
TILE = 1920
CHUNK = 640
PARTS = TILE // CHUNK
HEAD_CHUNK = 384
SPLIT = 4
K0 = 2 * 0.7978845608028654
K1 = 8 * 0.7978845608028654 * 0.044715


def mm(a, b):
    return lax.dot_general(a, b, (((1,), (0,)), ((), ())), preferred_element_type=F32)


def mm_nt(a, b):
    return lax.dot_general(a, b, (((1,), (1,)), ((), ())), preferred_element_type=F32)


def mm_tn(a, b):
    return lax.dot_general(a, b, (((0,), (0,)), ((), ())), preferred_element_type=F32)


def norm_gelu(s, gain8, gain_slope, shift_half):
    mean = jnp.sum(s, axis=1, keepdims=True) * (1.0 / WIDTH)
    center = s - mean
    r = lax.rsqrt(jnp.sum(center * center, axis=1, keepdims=True) + WIDTH * 1e-5)
    n = center * r
    h = n * gain8 + shift_half
    y = h * h
    t = jnp.tanh(h * (K0 + K1 * y))
    e1 = 1.0 + t
    bend = (h * (y + K0 / (3 * K1))) * (1.0 - t)
    slope = (e1 * gain_slope) * (1.0 / (3 * K1) + bend)
    return h * e1, n.astype(BF16), slope.astype(BF16), jnp.broadcast_to(r, (UNIT, 128))


def scales(vec_ref, at, layers):
    gain = vec_ref[pl.ds(at, 1), :]
    return gain * 8.0, gain * (8.0 * 3 * K1), vec_ref[pl.ds(at + layers, 1), :] * 0.5


def norm_back(da, slope, n, r):
    w = da * slope.astype(F32)
    m1 = jnp.sum(w, axis=1, keepdims=True) * (1.0 / WIDTH)
    w16 = w.astype(BF16)
    wn = w16 * n
    wide = (wn[:, 0:128] + wn[:, 128:256]).astype(F32)
    m2 = jnp.sum(wide, axis=1, keepdims=True)
    m1 = jnp.broadcast_to(m1, (UNIT, 128)).astype(BF16)
    m2 = jnp.broadcast_to(m2, (UNIT, 128)).astype(BF16)
    halves = [
        (w[:, k:k + 128] - (m1 + n[:, k:k + 128] * m2).astype(F32)) * r for k in (0, 128)
    ]
    return jnp.concatenate(halves, axis=1), w, wn


def rows_of(c):
    return pl.multiple_of(c * CHUNK, UNIT)


def activate(base, s_ref, save, i, scale):
    act_ref, n_ref, slope_ref, r_ref = save
    for u in range(0, CHUNK, UNIT):
        rows = pl.ds(base + u, UNIT)
        act, n, slope, r = norm_gelu(s_ref[rows, :], *scale)
        act_ref[i, rows, :] = act.astype(BF16)
        n_ref[i, rows, :] = n
        slope_ref[i, rows, :] = slope
        r_ref[i, rows, :] = r


def following(i, c, change):
    end = c == PARTS - 1
    return jnp.where(end, i + change, i), jnp.where(end, 0, c + 1)


def forward_layers(first, last, layers, s_ref, save, vec_ref, w_ref, w_at, save_at, after=None):
    act_ref = save[0]

    def product(i, c):
        return mm(act_ref[i - save_at, pl.ds(rows_of(c), CHUNK), :], w_ref[i - w_at])

    def activation(i, c):
        activate(rows_of(c), s_ref, save, i - save_at, scales(vec_ref, 7 + i, layers))

    def residual(i, base, out):
        bias = vec_ref[pl.ds(7 + 2 * layers + i, 1), :]
        for u in range(0, CHUNK, UNIT):
            rows = pl.ds(base + u, UNIT)
            s_ref[rows, :] = s_ref[rows, :] + (out[u:u + UNIT, :] + bias)

    def body(t, carry):
        before, now = carry
        out = product(*before)
        activation(*now)
        base = rows_of(before[1])
        if spare:
            base = pl.multiple_of(jnp.where(t == 0, TILE, base), UNIT)
        residual(before[0], base, out)
        if after is not None:
            after(*now)
        return now, following(*now, 1)

    spare = s_ref.shape[0] > TILE
    start = jnp.int32(first), jnp.int32(0)
    carry = start, start
    if not spare:
        activation(*start)
        carry = start, following(*start, 1)
    end, _ = lax.fori_loop(0 if spare else 1, (last - first) * PARTS, body, carry)
    residual(end[0], rows_of(end[1]), product(*end))


def column_sums(parts):
    total = parts[0]
    for part in parts[1:]:
        total = total + part
    return total.astype(F32)


GROUP = 4


def fold(x):
    return jnp.sum(x, axis=0, keepdims=True)


def backward_layers(first, last, layers, s_ref, low_ref, da_ref, save, w_ref, w_at, save_at, gw_ref, gv_ref, g_at, after=None):
    act_ref, n_ref, slope_ref, r_ref = save

    def product(i, c):
        return mm_nt(low_ref[pl.ds(rows_of(c), CHUNK), :], w_ref[i - w_at])

    def body(t, carry):
        i, c = carry
        base = rows_of(c)
        next_i, next_c = following(i, c, -1)
        next_i = jnp.maximum(next_i, first)
        next_da = product(next_i, next_c)
        gw_ref[i - g_at] += mm_tn(act_ref[i - save_at, pl.ds(base, CHUNK), :], low_ref[pl.ds(base, CHUNK), :])
        zero = jnp.zeros((UNIT, WIDTH), F32)
        shift, gain, bias = zero, zero, zero
        held = []
        for u in range(0, CHUNK, UNIT):
            rows = pl.ds(base + u, UNIT)
            at = (i - save_at, rows, slice(None))
            d_in, wf, wn = norm_back(da_ref[u:u + UNIT, :], slope_ref[at], n_ref[at], r_ref[at])
            shift = shift + wf
            held.append(wn)
            if len(held) == GROUP:
                gain = gain + column_sums(held)
                held = []
            ds = s_ref[rows, :]
            bias = bias + ds
            ds = ds + d_in
            s_ref[rows, :] = ds
            low_ref[rows, :] = ds.astype(BF16)
        da_ref[...] = next_da
        for k, x in enumerate((gain, shift, bias)):
            gv_ref[pl.ds(7 + k * layers + i, 1), :] += fold(x)
        if after is not None:
            after(i, c)
        return next_i, next_c

    start = jnp.int32(last - 1), jnp.int32(0)
    da_ref[...] = product(*start)
    lax.fori_loop(0, (last - first) * PARTS, body, start)


def columns_of(ints):
    row = lax.broadcasted_iota(jnp.int32, (16, ints.shape[1]), 0)
    parts = (ints[1:2] >> 5, ints[1:2] & 31, ints[2:3], ints[3:4])
    values = jnp.zeros_like(row)
    for k, part in enumerate(parts):
        values = jnp.where(row == k, part, values)
    k = lax.broadcasted_iota(jnp.int32, (16, 384), 0)
    j = lax.broadcasted_iota(jnp.int32, (16, 384), 1) >> 7
    pick = jnp.where((j == 0) & (k == 0), 32.0, 0.0) + jnp.where(
        ((j == 0) & (k == 1)) | ((j == 1) & (k == 2)) | ((j == 2) & (k == 3)), 1.0, 0.0
    )
    return mm_tn(values.astype(F32).astype(BF16), pick.astype(BF16))


def softmax(hb_ref, full_ref, col_ref, top_ref, total_ref, expon_ref, wide_ref, dlog_ref, at, loss_ref):
    units = [slice(u, u + UNIT) for u in range(0, HEAD_CHUNK, UNIT)]
    lane = lax.broadcasted_iota(jnp.int32, (1, 128), 1).astype(F32)
    spread = lambda x: jnp.broadcast_to(x, (UNIT, 128))
    cols = [slice(k * 128, (k + 1) * 128) for k in range(6)]
    for rows in units:
        logits = [full_ref[rows, cols[k]] + hb_ref[0:1, cols[k]].astype(F32) for k in range(6)]
        for k in range(6):
            full_ref[rows, cols[k]] = logits[k]
            wide_ref[k, rows, :] = logits[k].astype(BF16)
        top = functools.reduce(jnp.maximum, logits[:5])
        top_ref[0, rows, :] = spread(jnp.max(top, axis=1, keepdims=True))
        top_ref[1, rows, :] = spread(jnp.max(logits[5], axis=1, keepdims=True))
    for rows in units:
        expon = [jnp.exp(full_ref[rows, cols[k]] - top_ref[k // 5, rows, :]) for k in range(6)]
        for k in range(6):
            expon_ref[rows, cols[k]] = expon[k]
        total_ref[0, rows, :] = spread(jnp.sum(functools.reduce(jnp.add, expon[:5]), axis=1, keepdims=True))
        total_ref[1, rows, :] = spread(jnp.sum(expon[5], axis=1, keepdims=True))
    loss = jnp.zeros((UNIT, 128), F32)
    for rows in units:
        targets, mask = (col_ref[rows, cols[0]], col_ref[rows, cols[1]]), col_ref[rows, cols[2]]
        zero = jnp.zeros_like(mask)
        hits = [zero, zero]
        weights = [mask / total_ref[j, rows, :] for j in range(2)]
        for k in range(6):
            j = k // 5
            hit = lane + 128.0 * (k % 5) == targets[j]
            hits[j] = jnp.where(hit, full_ref[rows, cols[k]], hits[j])
            grad = expon_ref[rows, cols[k]] * weights[j] - jnp.where(hit, mask, zero)
            dlog_ref[pl.ds(at + rows.start, UNIT), cols[k]] = grad.astype(BF16)
        row = jnp.log(total_ref[0, rows, :]) + jnp.log(total_ref[1, rows, :]) + (top_ref[0, rows, :] + top_ref[1, rows, :])
        loss = loss + mask * (row * (1.0 / 128) - (hits[0] + hits[1]))
    loss_ref[...] += loss


def heads(
    nq, ints_ref, s_ref, ds_ref, low_ref, wh_ref, hb_ref, latents_ref, value_ref, chance_ref, turned_ref, dlog_ref, loss_ref, full_ref, col_ref,
    top_ref, total_ref, expon_ref, wide_ref, gw_ref, g_at,
):
    size = HEAD_CHUNK
    count = TILE // size

    def span_of(t):
        return pl.ds(pl.multiple_of(t * size, 128), size)

    def logits(t):
        lat = s_ref[span_of(t), :].astype(BF16)
        latents_ref[span_of(t), :] = lat
        return mm(lat, wh_ref[...]), columns_of(ints_ref[:, span_of(t)])

    def keep(parts):
        full_ref[...], col_ref[...] = parts

    def turn(t):
        for k in range(5):
            height = min(128, nq - k * 128)
            value_ref[k * 128:k * 128 + height, span_of(t)] = wide_ref[k].T[0:height, :]
        chance_ref[:, span_of(t)] = wide_ref[5].T[0:chance_ref.shape[0], :]
        turned_ref[0:WIDTH, span_of(t)] = latents_ref[span_of(t), :].T

    def product(t):
        return mm_nt(dlog_ref[span_of(t), :], wh_ref[...])

    def store(t, ds):
        ds_ref[span_of(t), :] = ds
        low_ref[span_of(t), :] = ds.astype(BF16)

    def body(t, carry):
        before = jnp.maximum(t - 1, 0)
        following = logits(jnp.minimum(t + 1, count - 1))
        turn(before)
        ds = product(before)
        softmax(
            hb_ref, full_ref, col_ref, top_ref, total_ref, expon_ref, wide_ref, dlog_ref, pl.multiple_of(t * size, 128), loss_ref
        )
        store(before, ds)
        keep(following)
        return carry

    keep(logits(jnp.int32(0)))
    lax.fori_loop(0, count, body, 0)
    end = jnp.int32(count - 1)
    turn(end)
    store(end, product(end))

    def grads(k, carry):
        gw_ref[g_at + k] += mm(turned_ref[...], dlog_ref[:, pl.ds(pl.multiple_of(k * WIDTH, WIDTH), WIDTH)])
        return carry

    lax.fori_loop(0, 3, grads, 0)


def unpack_vec(w, vec_ref):
    vec_ref[...] = w[:, 0:128].astype(F32).T


def moves_hot(ints):
    rows = lax.broadcasted_iota(jnp.int32, (16, ints.shape[1]), 0)
    return jnp.where((rows == ints[0:1]) | (rows == 4), 1.0, 0.0).astype(BF16)


def table_of(vec_ref):
    rows = lax.broadcasted_iota(jnp.int32, (16, WIDTH), 0)
    return jnp.where(rows < 5, vec_ref[0:16, :], 0.0).astype(BF16)


def stem_forward(latent_ref, hot_ref, vec_ref, w, s_ref, n_ref, slope_ref, r_ref, pre_ref, n_at):
    table = table_of(vec_ref)
    scale = scales(vec_ref, 5, 1)

    def product(c):
        span = pl.ds(rows_of(c), CHUNK)
        return mm(latent_ref[span, :], w) + mm(hot_ref[span, :], table)

    def body(c, carry):
        following = product(jnp.minimum(c + 1, PARTS - 1))
        for u in range(0, CHUNK, UNIT):
            rows = pl.ds(rows_of(c) + u, UNIT)
            act, n, slope, r = norm_gelu(pre_ref[u:u + UNIT, :], *scale)
            s_ref[rows, :] = act
            n_ref[n_at, rows, :] = n
            slope_ref[n_at, rows, :] = slope
            r_ref[n_at, rows, :] = r
        pre_ref[...] = following
        return carry

    pre_ref[...] = product(jnp.int32(0))
    lax.fori_loop(0, PARTS, body, 0)


def stem_backward(latent_ref, hot_ref, s_ref, low_ref, n_ref, slope_ref, r_ref, n_at, w, lgrad_ref, gw_ref, g_at, gv_ref):
    def products(c):
        span = pl.ds(rows_of(c), CHUNK)
        low = low_ref[...]
        lgrad_ref[span, :] = mm_nt(low, w).astype(BF16)
        gw_ref[g_at] += mm_tn(latent_ref[span, :], low)
        gv_ref[0:16, :] += mm_tn(hot_ref[span, :], low)

    def body(c, carry):
        products(jnp.maximum(c - 1, 0))
        shift = jnp.zeros((UNIT, WIDTH), F32)
        gain = shift
        held = []
        for u in range(0, CHUNK, UNIT):
            rows = pl.ds(rows_of(c) + u, UNIT)
            d_in, wf, wn = norm_back(s_ref[rows, :], slope_ref[n_at, rows, :], n_ref[n_at, rows, :], r_ref[n_at, rows, :])
            shift = shift + wf
            held.append(wn)
            if len(held) == GROUP:
                gain = gain + column_sums(held)
                held = []
            low_ref[u:u + UNIT, :] = d_in.astype(BF16)
        gv_ref[5:6, :] += fold(gain)
        gv_ref[6:7, :] += fold(shift)
        return carry

    low_ref[...] = jnp.zeros_like(low_ref)
    lax.fori_loop(0, PARTS, body, 0)
    products(PARTS - 1)


def clean_latent(latent_ref, lat_ref, rows_dev):
    lat_ref[...] = latent_ref[...]
    steps = -(-rows_dev // TILE)
    tail = rows_dev - (steps - 1) * TILE
    if tail < TILE:
        @pl.when(pl.program_id(0) == steps - 1)
        def _():
            lat_ref[tail:TILE, :] = jnp.zeros((TILE - tail, WIDTH), BF16)


def split_low(x):
    high = x.astype(BF16)
    return high, (x - high.astype(F32)).astype(BF16)


def join_pieces(pieces_ref, w_ref, at):
    rows = WIDTH // pieces_ref.shape[0]
    for f in range(pieces_ref.shape[0]):
        for m in range(pieces_ref.shape[1] // rows):
            w_ref[at + m, f * rows:(f + 1) * rows, :] = pieces_ref[f, m * rows:(m + 1) * rows, :]


def join_front(core_ref, front_refs, w_ref):
    if len(front_refs) == 1:
        join_pieces(front_refs[0], w_ref, 0)
    else:
        half = w_ref.shape[0] // 2
        for core in range(2):
            @pl.when(core_ref[0] == core)
            def _():
                join_pieces(front_refs[core], w_ref, 0)
                join_pieces(front_refs[1 - core], w_ref, half)


def cut_pieces(out_ref, m, matrix):
    rows = WIDTH // out_ref.shape[0]
    at = m * rows if isinstance(m, int) else pl.multiple_of(m * rows, rows)
    for f in range(out_ref.shape[0]):
        out_ref[f, pl.ds(at, rows), :] = matrix[f * rows:(f + 1) * rows, :].astype(BF16)


def cut_vectors(out_ref, at, wide):
    rows = WIDTH // out_ref.shape[0]
    half = rows // 2
    for f in range(out_ref.shape[0]):
        part = wide[f * rows:(f + 1) * rows, :]
        out_ref[f, at:at + half, :] = jnp.concatenate([part[0:half], part[half:rows]], axis=1).astype(BF16)


def copies(refs, away, sems, i, span, inward):
    out = []
    for k, (near, far) in enumerate(zip(refs, away)):
        ends = (far.at[i, span, :], near.at[i]) if inward else (near.at[i], far.at[i, span, :])
        out.append(pltpu.make_async_copy(*ends, sems.at[i, k]))
    return out


def tile_span(step):
    return pl.ds(pl.multiple_of(step * TILE, 128), TILE)


def first_kernel(layers, rows_dev, fronts, core_ref, latent_ref, ints_ref, *refs):
    front_refs = refs[:fronts]
    (
        n_out, slope_out, r_out, act_out, s_ref, vec_ref, w_ref, lat_ref, hot_ref, pre_ref, n_ref, slope_ref, r_ref, act_ref, sems,
    ) = refs[fronts:]
    step, steps = pl.program_id(0), pl.num_programs(0)
    span = tile_span(step)
    refs, away = (n_ref, slope_ref, r_ref, act_ref), (n_out, slope_out, r_out, act_out)

    def start(i, count=4):
        for copy in copies(refs[:count], away, sems, i, span, False):
            copy.start()

    def wait(i, count=4):
        for copy in copies(refs[:count], away, sems, i, span, False):
            copy.wait()

    @pl.when(step == 0)
    def _():
        join_front(core_ref, front_refs, w_ref)
        unpack_vec(w_ref[0], vec_ref)

    clean_latent(latent_ref, lat_ref, rows_dev)
    hot_ref[...] = moves_hot(ints_ref[...]).T

    @pl.when(step > 0)
    def _():
        wait(SPLIT, 3)

    stem_forward(lat_ref, hot_ref, vec_ref, w_ref[1], s_ref, n_ref, slope_ref, r_ref, pre_ref, SPLIT)
    start(SPLIT, 3)

    def after(i, c):
        @pl.when(c == PARTS - 1)
        def _():
            start(i)

            @pl.when((step > 0) & (i < SPLIT - 1))
            def _():
                wait(i + 1)

    @pl.when(step > 0)
    def _():
        wait(0)

    save = (act_ref, n_ref, slope_ref, r_ref)
    forward_layers(0, SPLIT, layers, s_ref, save, vec_ref, w_ref, -2, 0, after)

    @pl.when(step == steps - 1)
    def _():
        wait(SPLIT, 3)
        for i in range(SPLIT):
            wait(i)


def middle_kernel(
    layers, nq, s_in_ref, ints_ref, vec_ref, hb_ref, w_ref,
    latents_ref, value_ref, chance_ref, ds_ref, gv_ref, rep_ref, out_ref,
    wh_ref, s_ref, act_ref, n_ref, slope_ref, r_ref, low_ref, da_ref, turned_ref, dlog_ref, gw_ref, gh_ref, loss_ref, *chunk_refs,
):
    blocks = layers - SPLIT
    step = pl.program_id(0)

    @pl.when(step == 0)
    def _():
        for ref in (gw_ref, gh_ref, gv_ref, loss_ref):
            ref[...] = jnp.zeros_like(ref)
        turned_ref[WIDTH:, :] = jnp.ones_like(turned_ref[WIDTH:, :])
        for k in range(3):
            wh_ref[:, k * WIDTH:(k + 1) * WIDTH] = w_ref[blocks + k]

    s_ref[0:TILE, :] = s_in_ref[...]
    save = (act_ref, n_ref, slope_ref, r_ref)
    forward_layers(SPLIT, layers, layers, s_ref, save, vec_ref, w_ref, SPLIT, SPLIT)
    heads(nq, ints_ref, s_ref, ds_ref, low_ref, wh_ref, hb_ref, latents_ref, value_ref, chance_ref, turned_ref, dlog_ref, loss_ref, *chunk_refs, gh_ref, 0)
    backward_layers(SPLIT, layers, layers, ds_ref, low_ref, da_ref, save, w_ref, SPLIT, SPLIT, gw_ref, gv_ref, SPLIT)

    @pl.when(step == pl.num_programs(0) - 1)
    def _():
        def put(m, carry):
            cut_pieces(out_ref, m, gw_ref.at[m])
            return carry

        lax.fori_loop(0, blocks, put, 0)
        for k in range(3):
            cut_pieces(out_ref, blocks + k, gh_ref.at[k])
        row = lax.broadcasted_iota(jnp.int32, (8, WIDTH), 0)
        total = jnp.where(row == 3, jnp.concatenate([fold(loss_ref[...]), jnp.zeros((1, 128), F32)], axis=1), 0.0)
        for k in range(3):
            total = jnp.where(row == k, gh_ref[k, WIDTH:WIDTH + 1, :], total)
        rep_ref[...] = total
        at = (blocks + 3) * WIDTH // out_ref.shape[0]
        high, low = split_low(total)
        for f in range(out_ref.shape[0]):
            out_ref[f, at:at + 16, :] = jnp.concatenate([high, low], axis=0)


def last_kernel(layers, rows_dev, fronts, core_ref, latent_ref, ints_ref, ds_in_ref, n_in, slope_in, r_in, act_in, gv_in_ref, *refs):
    front_refs = refs[:fronts]
    (
        lgrad_ref, out_ref, w_ref, lat_ref, hot_ref, ds_ref, low_ref, da_ref, chunk_ref, n_ref, slope_ref, r_ref, act_ref, gw_ref, gv_ref,
        sems,
    ) = refs[fronts:]
    step, steps = pl.program_id(0), pl.num_programs(0)
    refs, away = (n_ref, slope_ref, r_ref, act_ref), (n_in, slope_in, r_in, act_in)

    def start(i, to, count=4):
        for copy in copies(refs[:count], away, sems, i, tile_span(to), True):
            copy.start()

    def wait(i, count=4):
        for copy in copies(refs[:count], away, sems, i, tile_span(step), True):
            copy.wait()

    @pl.when(step == 0)
    def _():
        start(SPLIT - 1, 0)
        join_front(core_ref, front_refs, w_ref)
        gw_ref[...] = jnp.zeros_like(gw_ref)
        gv_ref[...] = gv_in_ref[...]

    clean_latent(latent_ref, lat_ref, rows_dev)
    hot_ref[...] = moves_hot(ints_ref[...]).T
    ds_ref[...] = ds_in_ref[...]
    low_ref[...] = ds_in_ref[...].astype(BF16)

    def after(i, c):
        @pl.when(c == PARTS - 1)
        def _():
            @pl.when(step < steps - 1)
            def _():
                start(i, step + 1)

            @pl.when(i > 0)
            def _():
                wait(i - 1)

    wait(SPLIT - 1)

    @pl.when(step == 0)
    def _():
        for i in reversed(range(SPLIT - 1)):
            start(i, 0)
        start(SPLIT, 0, 3)

    save = (act_ref, n_ref, slope_ref, r_ref)
    backward_layers(0, SPLIT, layers, ds_ref, low_ref, da_ref, save, w_ref, -2, 0, gw_ref, gv_ref, -1, after)
    wait(SPLIT, 3)
    stem_backward(lat_ref, hot_ref, ds_ref, chunk_ref, n_ref, slope_ref, r_ref, SPLIT, w_ref[1], lgrad_ref, gw_ref, 0, gv_ref)

    @pl.when(step < steps - 1)
    def _():
        start(SPLIT, step + 1, 3)

    @pl.when(step == steps - 1)
    def _():
        for m in range(SPLIT + 1):
            cut_pieces(out_ref, m, gw_ref[m])
        high, low = split_low(jnp.concatenate([gv_ref[...], jnp.zeros((64 - gv_ref.shape[0], WIDTH), F32)], axis=0))
        wide = jnp.concatenate([high, low], axis=0).astype(F32).T
        cut_vectors(out_ref, (SPLIT + 1) * WIDTH // out_ref.shape[0], wide)


def pack_kernel(
    fronts, core_ref, stem_ref, table_ref, stem_vec_ref, block_ref, gain_ref, shift_ref, bias_ref, value_ref, chance_ref, front_ref,
    back_ref, vec_ref,
):
    layers, shard = block_ref.shape[0], block_ref.shape[1]
    nq, nc = value_ref.shape[1], chance_ref.shape[1]
    vec_ref[...] = jnp.zeros_like(vec_ref)
    at = 0
    for ref in (table_ref, stem_vec_ref, gain_ref, shift_ref, bias_ref):
        vec_ref[at:at + ref.shape[0], 0:shard] = ref[...].astype(F32)
        at += ref.shape[0]
    vectors = vec_ref[...].T[0:shard, :]
    vectors = jnp.concatenate([vectors, jnp.zeros_like(vectors)], axis=1).astype(BF16)
    entries = [lambda: vectors, lambda: stem_ref[...]] + [functools.partial(block_ref.__getitem__, i) for i in range(SPLIT)]
    half = len(entries) // fronts
    for core in range(fronts):
        @pl.when(core_ref[0] == core if fronts > 1 else core_ref[0] >= 0)
        def _():
            for m in range(half):
                entry = entries[core * half + m]()
                for f in range(front_ref.shape[0]):
                    front_ref[f, m * shard:(m + 1) * shard, :] = entry
    for i in range(SPLIT, layers):
        back_ref[i - SPLIT] = block_ref[i]
    at = layers - SPLIT
    back_ref[at:] = jnp.zeros_like(back_ref[at:])
    for k in range(3):
        width = min(WIDTH, nq - k * WIDTH)
        back_ref[at + k, :, 0:width] = value_ref[:, k * WIDTH:k * WIDTH + width]
    back_ref[at + 2, :, 128:128 + nc] = chance_ref[...]


def total_rows(refs, rows):
    total = refs[0][rows, :].astype(F32)
    for ref in refs[1:]:
        total = total + ref[rows, :].astype(F32)
    return total


def sum_mid_kernel(in_ref, out_ref):
    refs = [in_ref.at[f] for f in range(in_ref.shape[0])]
    end = in_ref.shape[1]
    for at in range(0, end - 16, 32):
        out_ref[at:at + 32, :] = total_rows(refs, slice(at, at + 32)).astype(BF16)
    total = total_rows(refs, slice(end - 16, end))
    high, low = split_low(total[0:8] + total[8:16])
    out_ref[end - 16:end, :] = jnp.concatenate([high, low], axis=0)


def sum_end_kernel(in_ref, out_ref):
    refs = [in_ref.at[f] for f in range(in_ref.shape[0])]
    end, vec = in_ref.shape[1], WIDTH // in_ref.shape[0] // 2
    for at in range(0, end - vec, 32):
        out_ref[at:at + 32, :] = total_rows(refs, slice(at, at + 32)).astype(BF16)
    total = total_rows(refs, slice(end - vec, end))
    parts = []
    for k in (0, 128):
        parts += split_low(total[:, k:k + 64] + total[:, k + 64:k + 128])
    out_ref[end - vec:end, :] = jnp.concatenate(parts, axis=1)


def finish_kernel(count, compact, scale, stem_vec_ref, gain_ref, *refs):
    mids, ends = refs[:count], refs[count:2 * count]
    (
        loss_ref, stem_ref, table_ref, stem_bias_ref, stem_gain_ref, stem_shift_ref, block_ref, block_gain_ref, block_shift_ref,
        block_bias_ref, value_ref, value_bias_ref, chance_ref, chance_bias_ref,
    ) = refs[2 * count:]
    layers, shard, moves = block_ref.shape[0], block_ref.shape[1], table_ref.shape[0]
    nq, nc = value_ref.shape[1], chance_ref.shape[1]

    def mid_of(at, rows):
        return total_rows(mids, slice(at, at + rows)) * scale

    def end_of(at, rows):
        return total_rows(ends, slice(at, at + rows)) * scale

    for i in range(SPLIT, layers):
        block_ref[i] = mid_of((i - SPLIT) * shard, shard)
    for i in range(SPLIT):
        block_ref[i] = end_of((1 + i) * shard, shard)
    stem_ref[...] = end_of(0, shard)
    for k in range(3):
        width = min(WIDTH, nq - k * WIDTH)
        part = mid_of((layers - SPLIT + k) * shard, shard)
        value_ref[:, k * WIDTH:k * WIDTH + width] = part[:, 0:width]
    chance_ref[...] = part[:, 128:128 + nc]
    rep = mid_of((layers - SPLIT + 3) * shard, 16)
    rep = rep[0:8] + rep[8:16]
    bias = jnp.concatenate([rep[k:k + 1] for k in range(3)], axis=1)
    value_bias_ref[...] = bias[:, 0:nq]
    chance_bias_ref[...] = bias[:, 640:640 + nc]
    loss_ref[0] = jnp.sum(rep[3:4])
    at = (1 + SPLIT) * shard
    if compact:
        small = end_of(at, shard // 2)
        small = jnp.concatenate([small[:, 0:128], small[:, 128:256]], axis=0)
    else:
        small = end_of(at, shard)[:, 0:128]
    if shard % 128:
        small = jnp.concatenate([small, jnp.zeros((128 - shard, 128), F32)], axis=0)
    small = small.T[:, 0:shard]
    small = small[0:64] + small[64:128]
    table_ref[...] = small[0:moves]
    stem_gain = stem_vec_ref[1:2, :].astype(F32)
    stem_bias_ref[...] = small[moves:moves + 1]
    stem_gain_ref[...] = small[moves + 1:moves + 2] / stem_gain
    stem_shift_ref[...] = small[moves + 2:moves + 3] / (16.0 * stem_gain)
    at = moves + 3
    gain = gain_ref[...].astype(F32)
    block_gain_ref[...] = small[at:at + layers] / gain
    block_shift_ref[...] = small[at + layers:at + 2 * layers] / (16.0 * gain)
    block_bias_ref[...] = small[at + 2 * layers:at + 3 * layers]


SMEM = pl.BlockSpec(memory_space=pltpu.SMEM)
VMEM = pl.BlockSpec(memory_space=pltpu.VMEM)
ANY = pl.BlockSpec(memory_space=pl.ANY)


def params(mib):
    return pltpu.CompilerParams(vmem_limit_bytes=mib << 20)


def tiled(shape, dim):
    block = shape[:dim] + (TILE,) + shape[dim + 1:]
    return pl.BlockSpec(block, lambda i: (0,) * dim + (i,) + (0,) * (len(shape) - dim - 1))


def whole(shape):
    return pl.BlockSpec(shape, lambda i: (0,) * len(shape))


def once(shape):
    return pl.BlockSpec(shape, lambda i: (0,) * len(shape), pipeline_mode=pl.Buffered(1))


def struct(shape, dtype):
    return jax.ShapeDtypeStruct(shape, dtype)


def exchange(x, axis, size):
    return [lax.ppermute(x, axis, [(i, i ^ k) for i in range(size)]) for k in range(1, size)]


def per_device(
    latent, actions, value_bins, chance_codes, step_mask, stem_weight, action_table, stem_bias, stem_gain, stem_shift,
    block_weight, block_gain, block_shift, block_bias, value_weight, value_bias, chance_weight, chance_bias,
):
    n_dp, n_fsdp = lax.axis_size("dp"), lax.axis_size("fsdp")
    rows_dev = latent.shape[0]
    layers, shard = block_weight.shape[0], block_weight.shape[1]
    nq, nc = value_weight.shape[1], chance_weight.shape[1]
    moves = action_table.shape[0]
    steps = -(-rows_dev // TILE)
    padded = steps * TILE
    fast = shard % 16 == 0 and n_dp & (n_dp - 1) == 0

    pieces, piece_rows = (n_fsdp, shard) if fast else (1, WIDTH)
    fronts = 2 if fast and n_dp % 2 == 0 and SPLIT % 2 == 0 else 1
    core = (lax.axis_index("dp") % 2).astype(jnp.int32).reshape(1)
    stem_vec = jnp.stack([stem_bias, stem_gain, stem_shift])
    n_front = (2 + SPLIT) // fronts
    front, back = pl.pallas_call(
        functools.partial(pack_kernel, fronts),
        in_specs=[SMEM] + [VMEM] * 9,
        out_specs=[VMEM] * 2,
        out_shape=[struct((pieces, n_front * shard, WIDTH), BF16), struct((layers - SPLIT + 3, shard, WIDTH), BF16)],
        scratch_shapes=[pltpu.VMEM((128, max(shard, 128)), F32)],
        name="pack",
    )(core, stem_weight, action_table, stem_vec, block_weight, block_gain, block_shift, block_bias, value_weight, chance_weight)
    if fast:
        w_fronts = [lax.all_to_all(front, "fsdp", 0, 0)]
        if fronts > 1:
            w_fronts.append(lax.ppermute(w_fronts[0], "dp", [(i, i ^ 1) for i in range(n_dp)]))
    else:
        front = lax.all_gather(front.reshape(n_front, shard, WIDTH), "fsdp", axis=1, tiled=True)
        w_fronts = [front.reshape(1, n_front * WIDTH, WIDTH)]
    w_back = lax.all_gather(back, "fsdp", axis=1, tiled=True)

    ints = jnp.pad(jnp.stack([actions, value_bins, chance_codes, step_mask]), ((0, 4), (0, padded - rows_dev)))
    ints_spec = pl.BlockSpec((8, TILE), lambda i: (0, i))
    none = lambda n: jnp.full((n,), -1e30, BF16)
    head_bias = jnp.concatenate([value_bias, none(640 - nq), chance_bias, none(128 - nc)])[None]

    saved = [
        struct((SPLIT + 1, padded, WIDTH), BF16),
        struct((SPLIT + 1, padded, WIDTH), BF16),
        struct((SPLIT + 1, padded, 128), F32),
        struct((SPLIT, padded, WIDTH), BF16),
    ]
    scratch = pltpu.VMEM
    kept = [scratch((x.shape[0], TILE, x.shape[2]), x.dtype) for x in saved] + [pltpu.SemaphoreType.DMA((SPLIT + 1, 4))]
    stream = struct((padded, WIDTH), F32)
    front_shape = (2 + SPLIT, WIDTH, WIDTH)
    *held, s_mid, vec = pl.pallas_call(
        functools.partial(first_kernel, layers, rows_dev, fronts),
        grid=(steps,),
        in_specs=[SMEM, tiled((rows_dev, WIDTH), 0), ints_spec] + [once(x.shape) for x in w_fronts],
        out_specs=[ANY] * 4 + [tiled(stream.shape, 0), whole((128, WIDTH))],
        out_shape=saved + [stream, struct((128, WIDTH), F32)],
        scratch_shapes=[scratch(front_shape, BF16), scratch((TILE, WIDTH), BF16), scratch((TILE, 16), BF16), scratch((CHUNK, WIDTH), F32)] + kept,
        compiler_params=params(62),
        cost_estimate=pl.CostEstimate(flops=rows_dev * WIDTH * WIDTH * 200, bytes_accessed=60 << 20, transcendentals=0),
        name="first",
    )(core, latent, ints, *w_fronts)

    blocks = layers - SPLIT
    compact = piece_rows % 32 == 0 and fast
    mid_shape = (pieces, (blocks + 3) * piece_rows + 16, WIDTH)
    end_shape = (pieces, (SPLIT + 1) * piece_rows + piece_rows // 2, WIDTH)
    latents, value_logits, chance_logits, ds_mid, gv_mid, rep, parts_mid = pl.pallas_call(
        functools.partial(middle_kernel, layers, nq),
        grid=(steps,),
        in_specs=[tiled(stream.shape, 0), ints_spec, once(vec.shape), once(head_bias.shape), once(w_back.shape)],
        out_specs=[
            tiled((rows_dev, WIDTH), 0), tiled((nq, rows_dev), 1), tiled((nc, rows_dev), 1), tiled(stream.shape, 0),
            whole((48, WIDTH)), whole((8, WIDTH)), whole(mid_shape),
        ],
        out_shape=[
            struct((rows_dev, WIDTH), BF16), struct((nq, rows_dev), BF16), struct((nc, rows_dev), BF16), stream,
            struct((48, WIDTH), F32), struct((8, WIDTH), F32), struct(mid_shape, BF16),
        ],
        scratch_shapes=[
            scratch((WIDTH, 3 * WIDTH), BF16),
            scratch((TILE + CHUNK, WIDTH), F32),
            scratch((blocks, TILE, WIDTH), BF16),
            scratch((blocks, TILE, WIDTH), BF16),
            scratch((blocks, TILE, WIDTH), BF16),
            scratch((blocks, TILE, 128), F32),
            scratch((TILE, WIDTH), BF16),
            scratch((CHUNK, WIDTH), F32),
            scratch((WIDTH + 16, TILE), BF16),
            scratch((TILE, 3 * WIDTH), BF16),
            scratch((blocks, WIDTH, WIDTH), F32),
            scratch((3, WIDTH + 16, WIDTH), F32),
            scratch((UNIT, 128), F32),
            scratch((HEAD_CHUNK, 3 * WIDTH), F32),
            scratch((HEAD_CHUNK, 384), F32),
            scratch((2, HEAD_CHUNK, 128), F32),
            scratch((2, HEAD_CHUNK, 128), F32),
            scratch((HEAD_CHUNK, 3 * WIDTH), F32),
            scratch((6, HEAD_CHUNK, 128), BF16),
        ],
        compiler_params=params(62),
        cost_estimate=pl.CostEstimate(flops=rows_dev * WIDTH * WIDTH * 600, bytes_accessed=40 << 20, transcendentals=0),
        name="middle",
    )(s_mid, ints, vec, head_bias, w_back)

    latent_grad, parts_end = pl.pallas_call(
        functools.partial(last_kernel, layers, rows_dev, fronts),
        grid=(steps,),
        in_specs=[SMEM, tiled((rows_dev, WIDTH), 0), ints_spec, tiled(stream.shape, 0)]
        + [ANY] * 4 + [once((48, WIDTH))] + [once(x.shape) for x in w_fronts],
        out_specs=[tiled((rows_dev, WIDTH), 0), whole(end_shape)],
        out_shape=[struct((rows_dev, WIDTH), BF16), struct(end_shape, BF16)],
        scratch_shapes=[
            scratch(front_shape, BF16),
            scratch((TILE, WIDTH), BF16),
            scratch((TILE, 16), BF16),
            scratch((TILE, WIDTH), F32),
            scratch((TILE, WIDTH), BF16),
            scratch((CHUNK, WIDTH), F32),
            scratch((CHUNK, WIDTH), BF16),
        ] + kept[:4] + [
            scratch((SPLIT + 1, WIDTH, WIDTH), F32),
            scratch((48, WIDTH), F32),
        ] + kept[4:],
        compiler_params=params(62),
        cost_estimate=pl.CostEstimate(flops=rows_dev * WIDTH * WIDTH * 150, bytes_accessed=60 << 20, transcendentals=0),
        name="last",
    )(core, latent, ints, ds_mid, *held, gv_mid, *w_fronts)

    if fast:
        got_mid = lax.all_to_all(parts_mid, "fsdp", 0, 0)
        parts_end, got_mid = lax.optimization_barrier((parts_end, got_mid))
        got_end = lax.all_to_all(parts_end, "fsdp", 0, 0)

        def add(body, got, name):
            return pl.pallas_call(
                body, in_specs=[VMEM], out_specs=VMEM, out_shape=struct(got.shape[1:], BF16), name=name,
            )(got)

        mine_mid, mine_end = add(sum_mid_kernel, got_mid, "sum_mid"), add(sum_end_kernel, got_end, "sum_end")
        mids = [mine_mid] + exchange(mine_mid, "dp", n_dp)
        ends = [mine_end] + exchange(mine_end, "dp", n_dp)
    else:
        def scatter(x, count):
            x = x[0, :count * WIDTH].reshape(count, WIDTH, WIDTH)
            x = lax.psum_scatter(x, "fsdp", scatter_dimension=1, tiled=True).astype(F32)
            return lax.psum(x, "dp").reshape(count * shard, WIDTH)

        rep = lax.psum(rep, ("dp", "fsdp"))
        vectors = parts_end[0, (SPLIT + 1) * WIDTH:]
        vectors = jnp.concatenate([vectors[:, 0:128], vectors[:, 128:256]], axis=0)
        vectors = jnp.concatenate([vectors, jnp.zeros_like(vectors)], axis=1)
        parts_end = jnp.concatenate([parts_end[:, :(SPLIT + 1) * WIDTH], vectors[None]], axis=1)
        mids = [jnp.concatenate([scatter(parts_mid, blocks + 3), rep, jnp.zeros((8, WIDTH), F32)])]
        ends = [scatter(parts_end, SPLIT + 2)]

    shapes = [
        (1,), (shard, WIDTH), (moves, shard), (1, shard), (1, shard), (1, shard), (layers, shard, WIDTH), (layers, shard),
        (layers, shard), (layers, shard), (shard, nq), (1, nq), (shard, nc), (1, nc),
    ]
    (
        loss, stem_grad, table_grad, stem_bias_grad, stem_gain_grad, stem_shift_grad, block_grad, gain_grad, shift_grad, bias_grad,
        value_grad, value_bias_grad, chance_grad, chance_bias_grad,
    ) = pl.pallas_call(
        functools.partial(finish_kernel, len(mids), compact, 1.0 / (rows_dev * n_dp * n_fsdp)),
        in_specs=[VMEM] * (2 + 2 * len(mids)),
        out_specs=[SMEM] + [VMEM] * (len(shapes) - 1),
        out_shape=[struct(x, F32) for x in shapes],
        name="finish",
    )(stem_vec, block_gain, *mids, *ends)
    return (
        latents,
        value_logits.T,
        chance_logits.T,
        loss.reshape(()),
        latent_grad,
        stem_grad,
        table_grad,
        stem_bias_grad.reshape(shard),
        stem_gain_grad.reshape(shard),
        stem_shift_grad.reshape(shard),
        block_grad,
        gain_grad,
        shift_grad,
        bias_grad,
        value_grad,
        value_bias_grad.reshape(nq),
        chance_grad,
        chance_bias_grad.reshape(nc),
    )


def solution(mesh):
    placed = (
        P(("dp", "fsdp"), None),
        P(("dp", "fsdp")),
        P(("dp", "fsdp")),
        P(("dp", "fsdp")),
        P(("dp", "fsdp")),
        P("fsdp", None),
        P(None, "fsdp"),
        P("fsdp"),
        P("fsdp"),
        P("fsdp"),
        P(None, "fsdp", None),
        P(None, "fsdp"),
        P(None, "fsdp"),
        P(None, "fsdp"),
        P("fsdp", None),
        P(),
        P("fsdp", None),
        P(),
    )
    return jax.shard_map(
        per_device,
        mesh=mesh,
        in_specs=placed,
        out_specs=(
            P(("dp", "fsdp"), None),
            P(("dp", "fsdp"), None),
            P(("dp", "fsdp"), None),
            P(),
            P(("dp", "fsdp"), None),
            P("fsdp", None),
            P(None, "fsdp"),
            P("fsdp"),
            P("fsdp"),
            P("fsdp"),
            P(None, "fsdp", None),
            P(None, "fsdp"),
            P(None, "fsdp"),
            P(None, "fsdp"),
            P("fsdp", None),
            P(),
            P("fsdp", None),
            P(),
        ),
        check_vma=False,
    )
```

```python
import functools
import jax
import jax.numpy as jnp
from jax import lax
from jax.experimental import pallas as pl
from jax.experimental.pallas import tpu as pltpu
from jax.sharding import PartitionSpec as P

F32 = jnp.float32
BF16 = jnp.bfloat16
WIDTH = 256
UNIT = 16
TILE = 1920
BACK = 640
CHUNK = 640
PARTS = TILE // CHUNK
HEAD_CHUNK = 384
SPLIT = 4
K0 = 2 * 0.7978845608028654
K1 = 8 * 0.7978845608028654 * 0.044715


def mm(a, b):
    return lax.dot_general(a, b, (((1,), (0,)), ((), ())), preferred_element_type=F32)


def mm_nt(a, b):
    return lax.dot_general(a, b, (((1,), (1,)), ((), ())), preferred_element_type=F32)


def mm_tn(a, b):
    return lax.dot_general(a, b, (((0,), (0,)), ((), ())), preferred_element_type=F32)


def norm_gelu(s, gain8, gain_slope, shift_half):
    mean = jnp.sum(s, axis=1, keepdims=True) * (1.0 / WIDTH)
    center = s - mean
    r = lax.rsqrt(jnp.sum(center * center, axis=1, keepdims=True) + WIDTH * 1e-5)
    n = center * r
    h = n * gain8 + shift_half
    y = h * h
    t = jnp.tanh(h * (K0 + K1 * y))
    e1 = 1.0 + t
    bend = (h * (y + K0 / (3 * K1))) * (1.0 - t)
    slope = (e1 * gain_slope) * (1.0 / (3 * K1) + bend)
    return h * e1, n.astype(BF16), slope, jnp.broadcast_to(r, (UNIT, 128))


def scales(vec_ref, at, layers):
    gain = vec_ref[pl.ds(at, 1), :]
    return gain * 8.0, gain * (8.0 * 3 * K1), vec_ref[pl.ds(at + layers, 1), :] * 0.5


def lane_sums(x):
    total = lax.reduce_sum(x[:, 0:128] + x[:, 128:256], (1,))
    return jnp.broadcast_to(total[:, None], (UNIT, 128))


def norm_back(da, slope, n, r):
    w = da * slope.astype(F32)
    w16 = w.astype(BF16)
    wn = w16 * n
    m1 = lane_sums(w16) * BF16(1.0 / WIDTH)
    m2 = lane_sums(wn)
    halves = [
        (w[:, k:k + 128] - (m1 + n[:, k:k + 128] * m2).astype(F32)) * r for k in (0, 128)
    ]
    return jnp.concatenate(halves, axis=1), w, wn


def rows_of(c):
    return pl.multiple_of(c * CHUNK, UNIT)


def activate(base, s_ref, save, i, scale):
    act_ref, n_ref, slope_ref, r_ref = save
    for u in range(0, CHUNK, UNIT):
        rows = pl.ds(base + u, UNIT)
        act, n, slope, r = norm_gelu(s_ref[rows, :], *scale)
        act_ref[i, rows, :] = act.astype(BF16)
        n_ref[i, rows, :] = n
        slope_ref[i, rows, :] = slope.astype(slope_ref.dtype)
        r_ref[i, rows, :] = r


def following(i, c, parts, change):
    end = c == parts - 1
    return jnp.where(end, i + change, i), jnp.where(end, 0, c + 1)


def forward_layers(first, last, layers, s_ref, save, vec_ref, w_ref, w_at, save_at, before_block=None, after_block=None):
    act_ref = save[0]

    def product(i, c):
        return mm(act_ref[i - save_at, pl.ds(rows_of(c), CHUNK), :], w_ref[i - w_at])

    def residual(i, base, out):
        bias = vec_ref[pl.ds(7 + 2 * layers + i, 1), :]
        for u in range(0, CHUNK, UNIT):
            rows = pl.ds(base + u, UNIT)
            s_ref[rows, :] = s_ref[rows, :] + (out[u:u + UNIT, :] + bias)

    def block(i, carry):
        if before_block is not None:
            before_block(i)

        def chunk(c, carry):
            old_i, old_c, base = carry
            out = product(old_i, old_c)
            activate(rows_of(c), s_ref, save, i - save_at, scales(vec_ref, 7 + i, layers))
            residual(old_i, pl.multiple_of(base, UNIT), out)
            return i, c, c * CHUNK

        carry = lax.fori_loop(0, PARTS, chunk, carry)
        if after_block is not None:
            after_block(i)
        return carry

    start = jnp.int32(first), jnp.int32(0), jnp.int32(TILE)
    i, c, base = lax.fori_loop(first, last, block, start)
    residual(i, pl.multiple_of(base, UNIT), product(i, c))


def column_sums(parts):
    total = parts[0]
    for part in parts[1:]:
        total = total + part
    return total.astype(F32)


GROUP = 8


def fold(x):
    return jnp.sum(x, axis=0, keepdims=True)


def backward_layers(first, last, layers, s_ref, low_ref, da_ref, save, w_ref, w_at, save_at, gw_ref, gv_ref, g_at, after_block=None, beside=None):
    act_ref, n_ref, slope_ref, r_ref = save

    def product(i, c):
        return mm_nt(low_ref[pl.ds(pl.multiple_of(c * BACK, UNIT), BACK), :], w_ref[i - w_at])

    def chunk(i, c):
        base = pl.multiple_of(c * BACK, UNIT)
        next_i, next_c = following(i, c, TILE // BACK, -1)
        next_i = jnp.maximum(next_i, first)
        next_da = product(next_i, next_c)
        gw_ref[i - g_at] += mm_tn(act_ref[i - save_at, pl.ds(base, BACK), :], low_ref[pl.ds(base, BACK), :])
        if beside is not None:
            beside(last - 1 - i, c)
        zero = jnp.zeros((UNIT, WIDTH), F32)
        shift, gain, bias = zero, zero, zero
        held = []
        for u in range(0, BACK, UNIT):
            rows = pl.ds(base + u, UNIT)
            at = (i - save_at, rows, slice(None))
            d_in, wf, wn = norm_back(da_ref[u:u + UNIT, :], slope_ref[at], n_ref[at], r_ref[at])
            shift = shift + wf
            held.append(wn)
            if len(held) == GROUP:
                gain = gain + column_sums(held)
                held = []
            ds = s_ref[rows, :]
            bias = bias + ds
            ds = ds + d_in
            s_ref[rows, :] = ds
            low_ref[rows, :] = ds.astype(BF16)
        da_ref[...] = next_da
        for k, x in enumerate((gain, shift, bias)):
            gv_ref[pl.ds(7 + k * layers + i, 1), :] += fold(x)

    def block(j, carry):
        i = last - 1 - j
        lax.fori_loop(0, TILE // BACK, lambda c, carry: chunk(i, c) or carry, 0)
        if after_block is not None:
            after_block(i)
        return carry

    da_ref[...] = product(last - 1, 0)
    lax.fori_loop(0, last - first, block, 0)


def softmax(full_ref, col_ref, top_ref, total_ref, expon_ref, wide_ref, dlog_ref, at, loss_ref):
    units = [slice(u, u + UNIT) for u in range(0, HEAD_CHUNK, UNIT)]
    lane = lax.broadcasted_iota(jnp.int32, (1, 128), 1).astype(F32)
    spread = lambda x: jnp.broadcast_to(x, (UNIT, 128))
    cols = [slice(k * 128, (k + 1) * 128) for k in range(6)]
    for rows in units:
        logits = [full_ref[rows, cols[k]] for k in range(6)]
        for k in range(6):
            wide_ref[k, rows, :] = logits[k].astype(BF16)
        top = functools.reduce(jnp.maximum, logits[:5])
        top_ref[0, rows, :] = spread(jnp.max(top, axis=1, keepdims=True))
        top_ref[1, rows, :] = spread(jnp.max(logits[5], axis=1, keepdims=True))
    for rows in units:
        expon = [jnp.exp(full_ref[rows, cols[k]] - top_ref[k // 5, rows, :]) for k in range(6)]
        for k in range(6):
            expon_ref[rows, cols[k]] = expon[k]
        total_ref[0, rows, :] = spread(jnp.sum(functools.reduce(jnp.add, expon[:5]), axis=1, keepdims=True))
        total_ref[1, rows, :] = spread(jnp.sum(expon[5], axis=1, keepdims=True))
    loss = jnp.zeros((UNIT, 128), F32)
    for rows in units:
        _, *targets, mask = (spread(col_ref[pl.ds(at + rows.start, UNIT), k:k + 1]) for k in range(4))
        zero = jnp.zeros_like(mask)
        hits = [zero, zero]
        weights = [mask / total_ref[j, rows, :] for j in range(2)]
        for k in range(6):
            j = k // 5
            hit = lane + 128.0 * (k % 5) == targets[j]
            hits[j] = jnp.where(hit, full_ref[rows, cols[k]], hits[j])
            grad = expon_ref[rows, cols[k]] * weights[j] - jnp.where(hit, mask, zero)
            dlog_ref[pl.ds(at + rows.start, UNIT), cols[k]] = grad.astype(BF16)
        row = jnp.log(total_ref[0, rows, :]) + jnp.log(total_ref[1, rows, :]) + (top_ref[0, rows, :] + top_ref[1, rows, :])
        loss = loss + mask * (row * (1.0 / 128) - (hits[0] + hits[1]))
    loss_ref[...] += loss


def heads(
    nq, ints_ref, s_ref, ds_ref, low_ref, wh_ref, hb_ref, latents_ref, value_ref, chance_ref, turned_ref, dlog_ref, loss_ref, full_ref, col_ref,
    top_ref, total_ref, expon_ref, wide_ref,
):
    size = HEAD_CHUNK
    count = TILE // size

    def span_of(t):
        return pl.ds(pl.multiple_of(t * size, 128), size)

    def logits(t):
        lat = s_ref[span_of(t), :].astype(BF16)
        latents_ref[span_of(t), :] = lat
        return mm(lat, wh_ref[...])

    def keep(parts):
        full_ref[...] = parts + hb_ref[...].astype(F32)

    def turn(t):
        for k in range(5):
            height = min(128, nq - k * 128)
            value_ref[k * 128:k * 128 + height, span_of(t)] = wide_ref[k].T[0:height, :]
        chance_ref[:, span_of(t)] = wide_ref[5].T[0:chance_ref.shape[0], :]
        turned_ref[0:WIDTH, span_of(t)] = latents_ref[span_of(t), :].T

    def product(t):
        return mm_nt(dlog_ref[span_of(t), :], wh_ref[...])

    def store(t, ds):
        ds_ref[span_of(t), :] = ds
        low_ref[span_of(t), :] = ds.astype(BF16)

    def body(t, carry):
        before = jnp.maximum(t - 1, 0)
        following = logits(jnp.minimum(t + 1, count - 1))
        turn(before)
        ds = product(before)
        softmax(full_ref, col_ref, top_ref, total_ref, expon_ref, wide_ref, dlog_ref, pl.multiple_of(t * size, 128), loss_ref)
        store(before, ds)
        keep(following)
        return carry

    col_ref[...] = ints_ref[...].astype(F32).T
    keep(logits(jnp.int32(0)))
    lax.fori_loop(0, count, body, 0)
    end = jnp.int32(count - 1)
    turn(end)
    store(end, product(end))


def unpack_vec(w, vec_ref):
    vec_ref[...] = w[:, 0:128].astype(F32).T


def moves_hot(ints):
    rows = lax.broadcasted_iota(jnp.int32, (16, ints.shape[1]), 0)
    return jnp.where((rows == ints[0:1]) | (rows == 4), 1.0, 0.0).astype(BF16)


def table_of(vec_ref):
    rows = lax.broadcasted_iota(jnp.int32, (16, WIDTH), 0)
    return jnp.where(rows < 5, vec_ref[0:16, :], 0.0).astype(BF16)


def stem_forward(latent_ref, hot_ref, vec_ref, w, s_ref, n_ref, slope_ref, r_ref, pre_ref, n_at):
    table = table_of(vec_ref)
    scale = scales(vec_ref, 5, 1)

    def product(c):
        span = pl.ds(rows_of(c), CHUNK)
        return mm(latent_ref[span, :], w) + mm(hot_ref[span, :], table)

    def body(c, carry):
        following = product(jnp.minimum(c + 1, PARTS - 1))
        for u in range(0, CHUNK, UNIT):
            rows = pl.ds(rows_of(c) + u, UNIT)
            act, n, slope, r = norm_gelu(pre_ref[u:u + UNIT, :], *scale)
            s_ref[rows, :] = act
            n_ref[n_at, rows, :] = n
            slope_ref[n_at, rows, :] = slope.astype(slope_ref.dtype)
            r_ref[n_at, rows, :] = r
        pre_ref[...] = following
        return carry

    pre_ref[...] = product(jnp.int32(0))
    lax.fori_loop(0, PARTS, body, 0)


def stem_backward(latent_ref, hot_ref, s_ref, low_ref, n_ref, slope_ref, r_ref, n_at, w, lgrad_ref, gw_ref, g_at, gv_ref):
    def products(c):
        span = pl.ds(rows_of(c), CHUNK)
        low = low_ref[...]
        lgrad_ref[span, :] = mm_nt(low, w).astype(BF16)
        gw_ref[g_at] += mm_tn(latent_ref[span, :], low)
        gv_ref[0:16, :] += mm(hot_ref[:, span], low)

    def body(c, carry):
        products(jnp.maximum(c - 1, 0))
        shift = jnp.zeros((UNIT, WIDTH), F32)
        gain = shift
        held = []
        for u in range(0, CHUNK, UNIT):
            rows = pl.ds(rows_of(c) + u, UNIT)
            d_in, wf, wn = norm_back(s_ref[rows, :], slope_ref[n_at, rows, :], n_ref[n_at, rows, :], r_ref[n_at, rows, :])
            shift = shift + wf
            held.append(wn)
            if len(held) == GROUP:
                gain = gain + column_sums(held)
                held = []
            low_ref[u:u + UNIT, :] = d_in.astype(BF16)
        gv_ref[5:6, :] += fold(gain)
        gv_ref[6:7, :] += fold(shift)
        return carry

    low_ref[...] = jnp.zeros_like(low_ref)
    lax.fori_loop(0, PARTS, body, 0)
    products(PARTS - 1)


def clean_latent(latent_ref, lat_ref, rows_dev):
    lat_ref[...] = latent_ref[...]
    steps = -(-rows_dev // TILE)
    tail = rows_dev - (steps - 1) * TILE
    if tail < TILE:
        @pl.when(pl.program_id(0) == steps - 1)
        def _():
            lat_ref[tail:TILE, :] = jnp.zeros((TILE - tail, WIDTH), BF16)


def split_low(x):
    high = x.astype(BF16)
    return high, (x - high.astype(F32)).astype(BF16)


def join_pieces(pieces_ref, w_ref, at):
    rows = WIDTH // pieces_ref.shape[0]
    for f in range(pieces_ref.shape[0]):
        for m in range(pieces_ref.shape[1] // rows):
            w_ref[at + m, f * rows:(f + 1) * rows, :] = pieces_ref[f, m * rows:(m + 1) * rows, :]


def join_front(core_ref, front_refs, w_ref):
    if len(front_refs) == 1:
        join_pieces(front_refs[0], w_ref, 0)
    else:
        half = w_ref.shape[0] // 2
        for core in range(2):
            @pl.when(core_ref[0] == core)
            def _():
                join_pieces(front_refs[core], w_ref, 0)
                join_pieces(front_refs[1 - core], w_ref, half)


def cut_pieces(out_ref, m, matrix):
    rows = WIDTH // out_ref.shape[0]
    at = m * rows if isinstance(m, int) else pl.multiple_of(m * rows, rows)
    for f in range(out_ref.shape[0]):
        out_ref[f, pl.ds(at, rows), :] = matrix[f * rows:(f + 1) * rows, :].astype(BF16)


def cut_vectors(out_ref, at, wide):
    rows = WIDTH // out_ref.shape[0]
    half = rows // 2
    for f in range(out_ref.shape[0]):
        part = wide[f * rows:(f + 1) * rows, :]
        out_ref[f, at:at + half, :] = jnp.concatenate([part[0:half], part[half:rows]], axis=1).astype(BF16)


def copies(refs, away, sems, i, span, inward):
    out = []
    for k, (near, far) in enumerate(zip(refs, away)):
        ends = (far.at[i, span, :], near.at[i]) if inward else (near.at[i], far.at[i, span, :])
        out.append(pltpu.make_async_copy(*ends, sems.at[i, k]))
    return out


def tile_span(step):
    return pl.ds(pl.multiple_of(step * TILE, 128), TILE)


def first_kernel(layers, rows_dev, fronts, core_ref, latent_ref, ints_ref, *refs):
    front_refs = refs[:fronts]
    (
        n_out, slope_out, r_out, act_out, s_out_ref, vec_ref, w_ref, lat_ref, hot_ref, pre_ref, s_ref, n_ref, slope_ref, r_ref, act_ref, sems,
    ) = refs[fronts:]
    step, steps = pl.program_id(0), pl.num_programs(0)
    span = tile_span(step)
    refs, away = (n_ref, slope_ref, r_ref, act_ref), (n_out, slope_out, r_out, act_out)

    def start(i, count=4):
        for copy in copies(refs[:count], away, sems, i, span, False):
            copy.start()

    def wait(i, count=4):
        for copy in copies(refs[:count], away, sems, i, span, False):
            copy.wait()

    @pl.when(step == 0)
    def _():
        join_front(core_ref, front_refs, w_ref)
        unpack_vec(w_ref[0], vec_ref)

    clean_latent(latent_ref, lat_ref, rows_dev)
    hot_ref[...] = moves_hot(ints_ref[...]).T

    @pl.when(step > 0)
    def _():
        wait(SPLIT, 3)

    stem_forward(lat_ref, hot_ref, vec_ref, w_ref[1], s_ref, n_ref, slope_ref, r_ref, pre_ref, SPLIT)
    start(SPLIT, 3)

    def before_block(i):
        @pl.when(step > 0)
        def _():
            wait(i)

    save = (act_ref, n_ref, slope_ref, r_ref)
    forward_layers(0, SPLIT, layers, s_ref, save, vec_ref, w_ref, -2, 0, before_block, start)
    s_out_ref[...] = s_ref[0:TILE, :]

    @pl.when(step == steps - 1)
    def _():
        wait(SPLIT, 3)
        for i in range(SPLIT):
            wait(i)


def middle_kernel(
    layers, nq, s_in_ref, ints_ref, vec_ref, hb_ref, w_ref,
    latents_ref, value_ref, chance_ref, ds_ref, gv_ref, rep_ref, out_ref,
    wh_ref, s_ref, act_ref, n_ref, slope_ref, r_ref, low_ref, da_ref, turned_ref, dlog_ref, gw_ref, gh_ref, loss_ref, *chunk_refs,
):
    blocks = layers - SPLIT
    step = pl.program_id(0)

    @pl.when(step == 0)
    def _():
        for ref in (gw_ref, gh_ref, gv_ref, loss_ref):
            ref[...] = jnp.zeros_like(ref)
        turned_ref[...] = jnp.ones_like(turned_ref)
        dlog_ref[TILE:, :] = jnp.zeros_like(dlog_ref[TILE:, :])
        for k in range(3):
            wh_ref[:, k * WIDTH:(k + 1) * WIDTH] = w_ref[blocks + k]

    s_ref[0:TILE, :] = s_in_ref[...]
    save = (act_ref, n_ref, slope_ref, r_ref)
    forward_layers(SPLIT, layers, layers, s_ref, save, vec_ref, w_ref, SPLIT, SPLIT)
    heads(nq, ints_ref, s_ref, ds_ref, low_ref, wh_ref, hb_ref, latents_ref, value_ref, chance_ref, turned_ref, dlog_ref, loss_ref, *chunk_refs)

    def beside(j, k):
        rows = pl.ds(pl.multiple_of(j * HEAD_CHUNK, 128), HEAD_CHUNK)
        columns = pl.ds(pl.multiple_of(k * WIDTH, WIDTH), WIDTH)
        gh_ref[k] += mm(turned_ref[:, rows], dlog_ref[rows, columns])

    backward_layers(SPLIT, layers, layers, ds_ref, low_ref, da_ref, save, w_ref, SPLIT, SPLIT, gw_ref, gv_ref, SPLIT, None, beside)

    @pl.when(step == pl.num_programs(0) - 1)
    def _():
        def put(m, carry):
            cut_pieces(out_ref, m, gw_ref.at[m])
            return carry

        lax.fori_loop(0, blocks, put, 0)
        for k in range(3):
            cut_pieces(out_ref, blocks + k, gh_ref.at[k])
        row = lax.broadcasted_iota(jnp.int32, (8, WIDTH), 0)
        total = jnp.where(row == 3, jnp.concatenate([fold(loss_ref[...]), jnp.zeros((1, 128), F32)], axis=1), 0.0)
        for k in range(3):
            total = jnp.where(row == k, gh_ref[k, WIDTH:WIDTH + 1, :], total)
        rep_ref[...] = total
        at = (blocks + 3) * WIDTH // out_ref.shape[0]
        high, low = split_low(total)
        for f in range(out_ref.shape[0]):
            out_ref[f, at:at + 16, :] = jnp.concatenate([high, low], axis=0)


def last_kernel(layers, rows_dev, fronts, core_ref, latent_ref, ints_ref, ds_in_ref, n_in, slope_in, r_in, act_in, gv_in_ref, *refs):
    front_refs = refs[:fronts]
    (
        lgrad_ref, out_ref, w_ref, lat_ref, hot_ref, ds_ref, low_ref, da_ref, chunk_ref, n_ref, slope_ref, r_ref, act_ref, gw_ref, gv_ref,
        sems,
    ) = refs[fronts:]
    step, steps = pl.program_id(0), pl.num_programs(0)
    refs, away = (n_ref, slope_ref, r_ref, act_ref), (n_in, slope_in, r_in, act_in)

    def start(i, to, count=4):
        for copy in copies(refs[:count], away, sems, i, tile_span(to), True):
            copy.start()

    def wait(i, count=4):
        for copy in copies(refs[:count], away, sems, i, tile_span(step), True):
            copy.wait()

    @pl.when(step == 0)
    def _():
        start(SPLIT - 1, 0)
        join_front(core_ref, front_refs, w_ref)
        gw_ref[...] = jnp.zeros_like(gw_ref)
        gv_ref[...] = gv_in_ref[...]

    clean_latent(latent_ref, lat_ref, rows_dev)
    hot_ref[...] = moves_hot(ints_ref[...])
    ds_ref[...] = ds_in_ref[...]
    low_ref[...] = ds_in_ref[...].astype(BF16)

    def after_block(i):
        @pl.when(step < steps - 1)
        def _():
            start(i, step + 1)

        @pl.when(i > 0)
        def _():
            wait(i - 1)

    wait(SPLIT - 1)

    @pl.when(step == 0)
    def _():
        for i in reversed(range(SPLIT - 1)):
            start(i, 0)
        start(SPLIT, 0, 3)

    save = (act_ref, n_ref, slope_ref, r_ref)
    backward_layers(0, SPLIT, layers, ds_ref, low_ref, da_ref, save, w_ref, -2, 0, gw_ref, gv_ref, -1, after_block)
    wait(SPLIT, 3)
    stem_backward(lat_ref, hot_ref, ds_ref, chunk_ref, n_ref, slope_ref, r_ref, SPLIT, w_ref[1], lgrad_ref, gw_ref, 0, gv_ref)

    @pl.when(step < steps - 1)
    def _():
        start(SPLIT, step + 1, 3)

    @pl.when(step == steps - 1)
    def _():
        for m in range(SPLIT + 1):
            cut_pieces(out_ref, m, gw_ref[m])
        high, low = split_low(jnp.concatenate([gv_ref[...], jnp.zeros((64 - gv_ref.shape[0], WIDTH), F32)], axis=0))
        wide = jnp.concatenate([high, low], axis=0).astype(F32).T
        cut_vectors(out_ref, (SPLIT + 1) * WIDTH // out_ref.shape[0], wide)


def pack_kernel(
    fronts, core_ref, stem_ref, table_ref, stem_bias_ref, stem_gain_ref, stem_shift_ref, block_ref, gain_ref, shift_ref, bias_ref, value_ref, chance_ref, front_ref,
    back_ref, vec_ref,
):
    layers, shard = block_ref.shape[0], block_ref.shape[1]
    nq, nc = value_ref.shape[1], chance_ref.shape[1]
    vec_ref[...] = jnp.zeros_like(vec_ref)
    at = 0
    for ref in (table_ref, stem_bias_ref, stem_gain_ref, stem_shift_ref, gain_ref, shift_ref, bias_ref):
        rows = ref[...].astype(F32)
        rows = rows[None] if len(ref.shape) == 1 else rows
        vec_ref[at:at + rows.shape[0], 0:shard] = rows
        at += rows.shape[0]
    vectors = vec_ref[...].T[0:shard, :]
    vectors = jnp.concatenate([vectors, jnp.zeros_like(vectors)], axis=1).astype(BF16)
    entries = [lambda: vectors, lambda: stem_ref[...]] + [functools.partial(block_ref.__getitem__, i) for i in range(SPLIT)]
    half = len(entries) // fronts
    for core in range(fronts):
        @pl.when(core_ref[0] == core if fronts > 1 else core_ref[0] >= 0)
        def _():
            for m in range(half):
                entry = entries[core * half + m]()
                for f in range(front_ref.shape[0]):
                    front_ref[f, m * shard:(m + 1) * shard, :] = entry
    for i in range(SPLIT, layers):
        back_ref[i - SPLIT] = block_ref[i]
    at = layers - SPLIT
    back_ref[at:] = jnp.zeros_like(back_ref[at:])
    for k in range(3):
        width = min(WIDTH, nq - k * WIDTH)
        back_ref[at + k, :, 0:width] = value_ref[:, k * WIDTH:k * WIDTH + width]
    back_ref[at + 2, :, 128:128 + nc] = chance_ref[...]


def total_rows(refs, rows):
    total = refs[0][rows, :].astype(F32)
    for ref in refs[1:]:
        total = total + ref[rows, :].astype(F32)
    return total


def sum_mid_kernel(in_ref, out_ref):
    refs = [in_ref.at[f] for f in range(in_ref.shape[0])]
    end = in_ref.shape[1]
    for at in range(0, end - 16, 32):
        out_ref[at:at + 32, :] = total_rows(refs, slice(at, at + 32)).astype(BF16)
    total = total_rows(refs, slice(end - 16, end))
    high, low = split_low(total[0:8] + total[8:16])
    out_ref[end - 16:end, :] = jnp.concatenate([high, low], axis=0)


def sum_end_kernel(in_ref, out_ref):
    refs = [in_ref.at[f] for f in range(in_ref.shape[0])]
    end, vec = in_ref.shape[1], WIDTH // in_ref.shape[0] // 2
    for at in range(0, end - vec, 32):
        out_ref[at:at + 32, :] = total_rows(refs, slice(at, at + 32)).astype(BF16)
    total = total_rows(refs, slice(end - vec, end))
    parts = []
    for k in (0, 128):
        parts += split_low(total[:, k:k + 64] + total[:, k + 64:k + 128])
    out_ref[end - vec:end, :] = jnp.concatenate(parts, axis=1)


def finish_kernel(count, compact, scale, stem_scale_ref, gain_ref, *refs):
    mids, ends = refs[:count], refs[count:2 * count]
    (
        loss_ref, stem_ref, table_ref, stem_bias_ref, stem_gain_ref, stem_shift_ref, block_ref, block_gain_ref, block_shift_ref,
        block_bias_ref, value_ref, value_bias_ref, chance_ref, chance_bias_ref,
    ) = refs[2 * count:]
    layers, shard, moves = block_ref.shape[0], block_ref.shape[1], table_ref.shape[0]
    nq, nc = value_ref.shape[1], chance_ref.shape[1]

    def mid_of(at, rows):
        return total_rows(mids, slice(at, at + rows)) * scale

    def end_of(at, rows):
        return total_rows(ends, slice(at, at + rows)) * scale

    for i in range(SPLIT, layers):
        block_ref[i] = mid_of((i - SPLIT) * shard, shard)
    for i in range(SPLIT):
        block_ref[i] = end_of((1 + i) * shard, shard)
    stem_ref[...] = end_of(0, shard)
    for k in range(3):
        width = min(WIDTH, nq - k * WIDTH)
        part = mid_of((layers - SPLIT + k) * shard, shard)
        value_ref[:, k * WIDTH:k * WIDTH + width] = part[:, 0:width]
    chance_ref[...] = part[:, 128:128 + nc]
    rep = mid_of((layers - SPLIT + 3) * shard, 16)
    rep = rep[0:8] + rep[8:16]
    only = lax.broadcasted_iota(jnp.int32, rep.shape, 0)
    bias = jnp.concatenate([jnp.sum(jnp.where(only == k, rep, 0.0), axis=0) for k in range(3)])
    value_bias_ref[...] = bias[0:nq]
    chance_bias_ref[...] = bias[640:640 + nc]
    loss_ref[0] = jnp.sum(rep[3:4])
    at = (1 + SPLIT) * shard
    if compact:
        small = end_of(at, shard // 2)
        small = jnp.concatenate([small[:, 0:128], small[:, 128:256]], axis=0)
    else:
        small = end_of(at, shard)[:, 0:128]
    if shard % 128:
        small = jnp.concatenate([small, jnp.zeros((128 - shard, 128), F32)], axis=0)
    small = small.T[:, 0:shard]
    small = small[0:64] + small[64:128]
    table_ref[...] = small[0:moves]
    stem_gain = stem_scale_ref[...].astype(F32)[None]
    stem_bias_ref[...] = small[moves:moves + 1]
    stem_gain_ref[...] = small[moves + 1:moves + 2] / stem_gain
    stem_shift_ref[...] = small[moves + 2:moves + 3] / (16.0 * stem_gain)
    at = moves + 3
    gain = gain_ref[...].astype(F32)
    block_gain_ref[...] = small[at:at + layers] / gain
    block_shift_ref[...] = small[at + layers:at + 2 * layers] / (16.0 * gain)
    block_bias_ref[...] = small[at + 2 * layers:at + 3 * layers]


SMEM = pl.BlockSpec(memory_space=pltpu.SMEM)
VMEM = pl.BlockSpec(memory_space=pltpu.VMEM)
ANY = pl.BlockSpec(memory_space=pl.ANY)


def params(mib):
    return pltpu.CompilerParams(vmem_limit_bytes=mib << 20)


def tiled(shape, dim):
    block = shape[:dim] + (TILE,) + shape[dim + 1:]
    return pl.BlockSpec(block, lambda i: (0,) * dim + (i,) + (0,) * (len(shape) - dim - 1))


def whole(shape):
    return pl.BlockSpec(shape, lambda i: (0,) * len(shape))


def once(shape):
    return pl.BlockSpec(shape, lambda i: (0,) * len(shape), pipeline_mode=pl.Buffered(1))


def struct(shape, dtype):
    return jax.ShapeDtypeStruct(shape, dtype)


def exchange(x, axis, size):
    return [lax.ppermute(x, axis, [(i, i ^ k) for i in range(size)]) for k in range(1, size)]


def per_device(
    latent, actions, value_bins, chance_codes, step_mask, stem_weight, action_table, stem_bias, stem_gain, stem_shift,
    block_weight, block_gain, block_shift, block_bias, value_weight, value_bias, chance_weight, chance_bias,
):
    n_dp, n_fsdp = lax.axis_size("dp"), lax.axis_size("fsdp")
    rows_dev = latent.shape[0]
    layers, shard = block_weight.shape[0], block_weight.shape[1]
    nq, nc = value_weight.shape[1], chance_weight.shape[1]
    moves = action_table.shape[0]
    steps = -(-rows_dev // TILE)
    padded = steps * TILE
    fast = shard % 16 == 0 and n_dp & (n_dp - 1) == 0

    pieces, piece_rows = (n_fsdp, shard) if fast else (1, WIDTH)
    fronts = 2 if fast and n_dp % 2 == 0 and SPLIT % 2 == 0 else 1
    core = (lax.axis_index("dp") % 2).astype(jnp.int32).reshape(1)
    n_front = (2 + SPLIT) // fronts
    front, back = pl.pallas_call(
        functools.partial(pack_kernel, fronts),
        in_specs=[SMEM] + [VMEM] * 11,
        out_specs=[VMEM] * 2,
        out_shape=[struct((pieces, n_front * shard, WIDTH), BF16), struct((layers - SPLIT + 3, shard, WIDTH), BF16)],
        scratch_shapes=[pltpu.VMEM((128, max(shard, 128)), F32)],
        name="pack",
    )(
        core, stem_weight, action_table, stem_bias, stem_gain, stem_shift, block_weight, block_gain, block_shift, block_bias,
        value_weight, chance_weight,
    )
    if fast:
        w_fronts = [lax.all_to_all(front, "fsdp", 0, 0)]
        if fronts > 1:
            w_fronts.append(lax.ppermute(w_fronts[0], "dp", [(i, i ^ 1) for i in range(n_dp)]))
    else:
        front = lax.all_gather(front.reshape(n_front, shard, WIDTH), "fsdp", axis=1, tiled=True)
        w_fronts = [front.reshape(1, n_front * WIDTH, WIDTH)]
    w_back = lax.all_gather(back, "fsdp", axis=1, tiled=True)

    ints = jnp.pad(jnp.stack([actions, value_bins, chance_codes, step_mask]), ((0, 4), (0, padded - rows_dev)))
    ints_spec = pl.BlockSpec((8, TILE), lambda i: (0, i))
    none = lambda n: jnp.full((n,), -1e30, BF16)
    head_bias = jnp.concatenate([value_bias, none(640 - nq), chance_bias, none(128 - nc)])[None]

    saved = [
        struct((SPLIT + 1, padded, WIDTH), BF16),
        struct((SPLIT + 1, padded, WIDTH), BF16),
        struct((SPLIT + 1, padded, 128), F32),
        struct((SPLIT, padded, WIDTH), BF16),
    ]
    scratch = pltpu.VMEM
    kept = [scratch((x.shape[0], TILE, x.shape[2]), x.dtype) for x in saved] + [pltpu.SemaphoreType.DMA((SPLIT + 1, 4))]
    stream = struct((padded, WIDTH), F32)
    front_shape = (2 + SPLIT, WIDTH, WIDTH)
    *held, s_mid, vec = pl.pallas_call(
        functools.partial(first_kernel, layers, rows_dev, fronts),
        grid=(steps,),
        in_specs=[SMEM, tiled((rows_dev, WIDTH), 0), ints_spec] + [once(x.shape) for x in w_fronts],
        out_specs=[ANY] * 4 + [tiled(stream.shape, 0), whole((128, WIDTH))],
        out_shape=saved + [stream, struct((128, WIDTH), F32)],
        scratch_shapes=[
            scratch(front_shape, BF16), scratch((TILE, WIDTH), BF16), scratch((TILE, 16), BF16), scratch((CHUNK, WIDTH), F32),
            scratch((TILE + CHUNK, WIDTH), F32),
        ] + kept,
        compiler_params=params(62),
        cost_estimate=pl.CostEstimate(flops=rows_dev * WIDTH * WIDTH * 200, bytes_accessed=60 << 20, transcendentals=0),
        name="first",
    )(core, latent, ints, *w_fronts)

    blocks = layers - SPLIT
    compact = piece_rows % 32 == 0 and fast
    mid_shape = (pieces, (blocks + 3) * piece_rows + 16, WIDTH)
    end_shape = (pieces, (SPLIT + 1) * piece_rows + piece_rows // 2, WIDTH)
    latents, value_logits, chance_logits, ds_mid, gv_mid, rep, parts_mid = pl.pallas_call(
        functools.partial(middle_kernel, layers, nq),
        grid=(steps,),
        in_specs=[tiled(stream.shape, 0), ints_spec, once(vec.shape), once(head_bias.shape), once(w_back.shape)],
        out_specs=[
            tiled((rows_dev, WIDTH), 0), tiled((nq, rows_dev), 1), tiled((nc, rows_dev), 1), tiled(stream.shape, 0),
            whole((48, WIDTH)), whole((8, WIDTH)), whole(mid_shape),
        ],
        out_shape=[
            struct((rows_dev, WIDTH), BF16), struct((nq, rows_dev), BF16), struct((nc, rows_dev), BF16), stream,
            struct((48, WIDTH), F32), struct((8, WIDTH), F32), struct(mid_shape, BF16),
        ],
        scratch_shapes=[
            scratch((WIDTH, 3 * WIDTH), BF16),
            scratch((TILE + CHUNK, WIDTH), F32),
            scratch((blocks, TILE, WIDTH), BF16),
            scratch((blocks, TILE, WIDTH), BF16),
            scratch((blocks, TILE, WIDTH), F32),
            scratch((blocks, TILE, 128), F32),
            scratch((TILE, WIDTH), BF16),
            scratch((BACK, WIDTH), F32),
            scratch((WIDTH + 16, max(blocks * HEAD_CHUNK, TILE)), BF16),
            scratch((max(blocks * HEAD_CHUNK, TILE), 3 * WIDTH), BF16),
            scratch((blocks, WIDTH, WIDTH), F32),
            scratch((3, WIDTH + 16, WIDTH), F32),
            scratch((UNIT, 128), F32),
            scratch((HEAD_CHUNK, 3 * WIDTH), F32),
            scratch((TILE, 8), F32),
            scratch((2, HEAD_CHUNK, 128), F32),
            scratch((2, HEAD_CHUNK, 128), F32),
            scratch((HEAD_CHUNK, 3 * WIDTH), F32),
            scratch((6, HEAD_CHUNK, 128), BF16),
        ],
        compiler_params=params(62),
        cost_estimate=pl.CostEstimate(flops=rows_dev * WIDTH * WIDTH * 600, bytes_accessed=40 << 20, transcendentals=0),
        name="middle",
    )(s_mid, ints, vec, head_bias, w_back)

    latent_grad, parts_end = pl.pallas_call(
        functools.partial(last_kernel, layers, rows_dev, fronts),
        grid=(steps,),
        in_specs=[SMEM, tiled((rows_dev, WIDTH), 0), ints_spec, tiled(stream.shape, 0)]
        + [ANY] * 4 + [once((48, WIDTH))] + [once(x.shape) for x in w_fronts],
        out_specs=[tiled((rows_dev, WIDTH), 0), whole(end_shape)],
        out_shape=[struct((rows_dev, WIDTH), BF16), struct(end_shape, BF16)],
        scratch_shapes=[
            scratch(front_shape, BF16),
            scratch((TILE, WIDTH), BF16),
            scratch((16, TILE), BF16),
            scratch((TILE, WIDTH), F32),
            scratch((TILE, WIDTH), BF16),
            scratch((BACK, WIDTH), F32),
            scratch((CHUNK, WIDTH), BF16),
        ] + kept[:4] + [
            scratch((SPLIT + 1, WIDTH, WIDTH), F32),
            scratch((48, WIDTH), F32),
        ] + kept[4:],
        compiler_params=params(62),
        cost_estimate=pl.CostEstimate(flops=rows_dev * WIDTH * WIDTH * 150, bytes_accessed=60 << 20, transcendentals=0),
        name="last",
    )(core, latent, ints, ds_mid, *held, gv_mid, *w_fronts)

    if fast:
        got_mid = lax.all_to_all(parts_mid, "fsdp", 0, 0)
        parts_end, got_mid = lax.optimization_barrier((parts_end, got_mid))
        got_end = lax.all_to_all(parts_end, "fsdp", 0, 0)

        def add(body, got, name):
            return pl.pallas_call(
                body, in_specs=[VMEM], out_specs=VMEM, out_shape=struct(got.shape[1:], BF16), name=name,
            )(got)

        mine_mid, mine_end = add(sum_mid_kernel, got_mid, "sum_mid"), add(sum_end_kernel, got_end, "sum_end")
        mids = [mine_mid] + exchange(mine_mid, "dp", n_dp)
        ends = [mine_end] + exchange(mine_end, "dp", n_dp)
    else:
        def scatter(x, count):
            x = x[0, :count * WIDTH].reshape(count, WIDTH, WIDTH)
            x = lax.psum_scatter(x, "fsdp", scatter_dimension=1, tiled=True).astype(F32)
            return lax.psum(x, "dp").reshape(count * shard, WIDTH)

        rep = lax.psum(rep, ("dp", "fsdp"))
        vectors = parts_end[0, (SPLIT + 1) * WIDTH:]
        vectors = jnp.concatenate([vectors[:, 0:128], vectors[:, 128:256]], axis=0)
        vectors = jnp.concatenate([vectors, jnp.zeros_like(vectors)], axis=1)
        parts_end = jnp.concatenate([parts_end[:, :(SPLIT + 1) * WIDTH], vectors[None]], axis=1)
        mids = [jnp.concatenate([scatter(parts_mid, blocks + 3), rep, jnp.zeros((8, WIDTH), F32)])]
        ends = [scatter(parts_end, SPLIT + 2)]

    shapes = [
        (1,), (shard, WIDTH), (moves, shard), (1, shard), (1, shard), (1, shard), (layers, shard, WIDTH), (layers, shard),
        (layers, shard), (layers, shard), (shard, nq), (nq,), (shard, nc), (nc,),
    ]
    (
        loss, stem_grad, table_grad, stem_bias_grad, stem_gain_grad, stem_shift_grad, block_grad, gain_grad, shift_grad, bias_grad,
        value_grad, value_bias_grad, chance_grad, chance_bias_grad,
    ) = pl.pallas_call(
        functools.partial(finish_kernel, len(mids), compact, 1.0 / (rows_dev * n_dp * n_fsdp)),
        in_specs=[VMEM] * (2 + 2 * len(mids)),
        out_specs=[SMEM] + [VMEM] * (len(shapes) - 1),
        out_shape=[struct(x, F32) for x in shapes],
        name="finish",
    )(stem_gain, block_gain, *mids, *ends)
    return (
        latents,
        value_logits.T,
        chance_logits.T,
        loss.reshape(()),
        latent_grad,
        stem_grad,
        table_grad,
        stem_bias_grad.reshape(shard),
        stem_gain_grad.reshape(shard),
        stem_shift_grad.reshape(shard),
        block_grad,
        gain_grad,
        shift_grad,
        bias_grad,
        value_grad,
        value_bias_grad,
        chance_grad,
        chance_bias_grad,
    )


def solution(mesh):
    placed = (
        P(("dp", "fsdp"), None),
        P(("dp", "fsdp")),
        P(("dp", "fsdp")),
        P(("dp", "fsdp")),
        P(("dp", "fsdp")),
        P("fsdp", None),
        P(None, "fsdp"),
        P("fsdp"),
        P("fsdp"),
        P("fsdp"),
        P(None, "fsdp", None),
        P(None, "fsdp"),
        P(None, "fsdp"),
        P(None, "fsdp"),
        P("fsdp", None),
        P(),
        P("fsdp", None),
        P(),
    )
    return jax.shard_map(
        per_device,
        mesh=mesh,
        in_specs=placed,
        out_specs=(
            P(("dp", "fsdp"), None),
            P(("dp", "fsdp"), None),
            P(("dp", "fsdp"), None),
            P(),
            P(("dp", "fsdp"), None),
            P("fsdp", None),
            P(None, "fsdp"),
            P("fsdp"),
            P("fsdp"),
            P("fsdp"),
            P(None, "fsdp", None),
            P(None, "fsdp"),
            P(None, "fsdp"),
            P(None, "fsdp"),
            P("fsdp", None),
            P(),
            P("fsdp", None),
            P(),
        ),
        check_vma=False,
    )
```

```python
import functools
import jax
import jax.numpy as jnp
from jax import lax
from jax.experimental import pallas as pl
from jax.experimental.pallas import tpu as pltpu
from jax.sharding import PartitionSpec as P

F32 = jnp.float32
BF16 = jnp.bfloat16
WIDTH = 256
UNIT = 16
TILE = 1920
BACK = 640
CHUNK = 640
PARTS = TILE // CHUNK
HEAD_CHUNK = 384
SPLIT = 4
K0 = 2 * 0.7978845608028654
K1 = 8 * 0.7978845608028654 * 0.044715


def mm(a, b):
    return lax.dot_general(a, b, (((1,), (0,)), ((), ())), preferred_element_type=F32)


def mm_nt(a, b):
    return lax.dot_general(a, b, (((1,), (1,)), ((), ())), preferred_element_type=F32)


def mm_tn(a, b):
    return lax.dot_general(a, b, (((0,), (0,)), ((), ())), preferred_element_type=F32)


def norm_gelu(s, gain8, gain_slope, shift_half):
    mean = jnp.sum(s, axis=1, keepdims=True) * (1.0 / WIDTH)
    center = s - mean
    r = lax.rsqrt(jnp.sum(center * center, axis=1, keepdims=True) + WIDTH * 1e-5)
    n = center * r
    h = n * gain8 + shift_half
    y = h * h
    t = jnp.tanh(h * (K0 + K1 * y))
    e1 = 1.0 + t
    bend = (h * (y + K0 / (3 * K1))) * (1.0 - t)
    slope = e1 * (1.0 / (3 * K1) + bend)
    if gain_slope is not None:
        slope = slope * gain_slope
    return h * e1, n.astype(BF16), slope, jnp.broadcast_to(r, (UNIT, 128))


def scales(vec_ref, at, layers, slope):
    gain = vec_ref[pl.ds(at, 1), :]
    return gain * 8.0, gain * (8.0 * 3 * K1) if slope else None, vec_ref[pl.ds(at + layers, 1), :] * 0.5


def gained(w, columns, at):
    lane = lax.broadcasted_iota(jnp.int32, columns.shape, 1)
    gain = jnp.sum(jnp.where(lane == at, columns, 0.0), axis=1, keepdims=True)
    return (w.astype(F32) * (gain * (8.0 * 3 * K1))).astype(BF16)


def lane_sums(x):
    total = lax.reduce_sum(x[:, 0:128] + x[:, 128:256], (1,))
    return jnp.broadcast_to(total[:, None], (UNIT, 128))


def norm_back(da, slope, n, r):
    w = da * slope.astype(F32)
    w16 = w.astype(BF16)
    wn = w16 * n
    m1 = lane_sums(w16) * BF16(1.0 / WIDTH)
    m2 = lane_sums(wn)
    halves = [
        (w[:, k:k + 128] - (m1 + n[:, k:k + 128] * m2).astype(F32)) * r for k in (0, 128)
    ]
    return jnp.concatenate(halves, axis=1), w, wn


def rows_of(c):
    return pl.multiple_of(c * CHUNK, UNIT)


def activate(base, s_ref, save, i, scale):
    act_ref, n_ref, slope_ref, r_ref = save
    for u in range(0, CHUNK, UNIT):
        rows = pl.ds(base + u, UNIT)
        act, n, slope, r = norm_gelu(s_ref[rows, :], *scale)
        act_ref[i, rows, :] = act.astype(BF16)
        n_ref[i, rows, :] = n
        slope_ref[i, rows, :] = slope.astype(slope_ref.dtype)
        r_ref[i, rows, :] = r


def following(i, c, parts, change):
    end = c == parts - 1
    return jnp.where(end, i + change, i), jnp.where(end, 0, c + 1)


def forward_layers(first, last, layers, s_ref, save, vec_ref, w_ref, w_at, save_at, before_block=None, after_block=None):
    act_ref = save[0]

    def product(i, c):
        return mm(act_ref[i - save_at, pl.ds(rows_of(c), CHUNK), :], w_ref[i - w_at])

    def residual(i, base, out):
        bias = vec_ref[pl.ds(7 + 2 * layers + i, 1), :]
        for u in range(0, CHUNK, UNIT):
            rows = pl.ds(base + u, UNIT)
            s_ref[rows, :] = s_ref[rows, :] + (out[u:u + UNIT, :] + bias)

    def block(i, carry):
        if before_block is not None:
            before_block(i)

        def chunk(c, carry):
            old_i, old_c, base = carry
            out = product(old_i, old_c)
            activate(rows_of(c), s_ref, save, i - save_at, scales(vec_ref, 7 + i, layers, False))
            residual(old_i, pl.multiple_of(base, UNIT), out)
            return i, c, c * CHUNK

        carry = lax.fori_loop(0, PARTS, chunk, carry)
        if after_block is not None:
            after_block(i)
        return carry

    start = jnp.int32(first), jnp.int32(0), jnp.int32(TILE)
    i, c, base = lax.fori_loop(first, last, block, start)
    residual(i, pl.multiple_of(base, UNIT), product(i, c))


def column_sums(parts):
    total = parts[0]
    for part in parts[1:]:
        total = total + part
    return total.astype(F32)


GROUP = 8


def fold(x):
    return jnp.sum(x, axis=0, keepdims=True)


def backward_layers(first, last, layers, s_ref, low_ref, da_ref, save, w_ref, w_at, save_at, gw_ref, gv_ref, g_at, after_block=None, beside=None):
    act_ref, n_ref, slope_ref, r_ref = save

    def product(i, c):
        return mm_nt(low_ref[pl.ds(pl.multiple_of(c * BACK, UNIT), BACK), :], w_ref[i - w_at])

    def chunk(i, c):
        base = pl.multiple_of(c * BACK, UNIT)
        next_i, next_c = following(i, c, TILE // BACK, -1)
        next_i = jnp.maximum(next_i, first)
        next_da = product(next_i, next_c)
        gw_ref[i - g_at] += mm_tn(act_ref[i - save_at, pl.ds(base, BACK), :], low_ref[pl.ds(base, BACK), :])
        if beside is not None:
            beside(last - 1 - i, c)
        zero = jnp.zeros((UNIT, WIDTH), F32)
        shift, gain, bias = zero, zero, zero
        held = []
        for u in range(0, BACK, UNIT):
            rows = pl.ds(base + u, UNIT)
            at = (i - save_at, rows, slice(None))
            d_in, wf, wn = norm_back(da_ref[u:u + UNIT, :], slope_ref[at], n_ref[at], r_ref[at])
            shift = shift + wf
            held.append(wn)
            if len(held) == GROUP:
                gain = gain + column_sums(held)
                held = []
            ds = s_ref[rows, :]
            bias = bias + ds
            ds = ds + d_in
            s_ref[rows, :] = ds
            low_ref[rows, :] = ds.astype(BF16)
        da_ref[...] = next_da
        for k, x in enumerate((gain, shift, bias)):
            gv_ref[pl.ds(7 + k * layers + i, 1), :] += fold(x)

    def block(j, carry):
        i = last - 1 - j
        lax.fori_loop(0, TILE // BACK, lambda c, carry: chunk(i, c) or carry, 0)
        if after_block is not None:
            after_block(i)
        return carry

    da_ref[...] = product(last - 1, 0)
    lax.fori_loop(0, last - first, block, 0)


def softmax(full_ref, col_ref, top_ref, total_ref, expon_ref, dlog_ref, at, loss_ref):
    units = [slice(u, u + UNIT) for u in range(0, HEAD_CHUNK, UNIT)]
    lane = lax.broadcasted_iota(jnp.int32, (1, 128), 1).astype(F32)
    spread = lambda x: jnp.broadcast_to(x, (UNIT, 128))
    cols = [slice(k * 128, (k + 1) * 128) for k in range(6)]
    for rows in units:
        logits = [full_ref[rows, cols[k]] for k in range(6)]
        top = functools.reduce(jnp.maximum, logits[:5])
        top_ref[0, rows, :] = spread(jnp.max(top, axis=1, keepdims=True))
        top_ref[1, rows, :] = spread(jnp.max(logits[5], axis=1, keepdims=True))
    for rows in units:
        expon = [jnp.exp(full_ref[rows, cols[k]] - top_ref[k // 5, rows, :]) for k in range(6)]
        for k in range(6):
            expon_ref[rows, cols[k]] = expon[k]
        total_ref[0, rows, :] = spread(jnp.sum(functools.reduce(jnp.add, expon[:5]), axis=1, keepdims=True))
        total_ref[1, rows, :] = spread(jnp.sum(expon[5], axis=1, keepdims=True))
    loss = jnp.zeros((UNIT, 128), F32)
    for rows in units:
        _, *targets, mask = (spread(col_ref[pl.ds(at + rows.start, UNIT), k:k + 1]) for k in range(4))
        zero = jnp.zeros_like(mask)
        hits = [zero, zero]
        weights = [mask / total_ref[j, rows, :] for j in range(2)]
        for k in range(6):
            j = k // 5
            hit = lane + 128.0 * (k % 5) == targets[j]
            hits[j] = jnp.where(hit, full_ref[rows, cols[k]], hits[j])
            grad = expon_ref[rows, cols[k]] * weights[j] - jnp.where(hit, mask, zero)
            dlog_ref[pl.ds(at + rows.start, UNIT), cols[k]] = grad.astype(BF16)
        row = jnp.log(total_ref[0, rows, :]) + jnp.log(total_ref[1, rows, :]) + (top_ref[0, rows, :] + top_ref[1, rows, :])
        loss = loss + mask * (row * (1.0 / 128) - (hits[0] + hits[1]))
    loss_ref[...] += loss


def heads(
    ints_ref, s_ref, ds_ref, low_ref, wh_ref, hb_ref, latents_ref, turned_ref, dlog_ref, loss_ref, full_ref, col_ref, top_ref, total_ref,
    expon_ref,
):
    size = HEAD_CHUNK
    count = TILE // size

    def span_of(t):
        return pl.ds(pl.multiple_of(t * size, 128), size)

    def logits(t):
        lat = s_ref[span_of(t), :].astype(BF16)
        latents_ref[span_of(t), :] = lat
        return mm(lat, wh_ref[...])

    def keep(parts):
        full_ref[...] = parts + hb_ref[...].astype(F32)

    def turn(t):
        turned_ref[0:WIDTH, span_of(t)] = latents_ref[span_of(t), :].T

    def product(t):
        return mm_nt(dlog_ref[span_of(t), :], wh_ref[...])

    def store(t, ds):
        ds_ref[span_of(t), :] = ds
        low_ref[span_of(t), :] = ds.astype(BF16)

    def body(t, carry):
        before = jnp.maximum(t - 1, 0)
        following = logits(jnp.minimum(t + 1, count - 1))
        turn(before)
        ds = product(before)
        softmax(full_ref, col_ref, top_ref, total_ref, expon_ref, dlog_ref, pl.multiple_of(t * size, 128), loss_ref)
        store(before, ds)
        keep(following)
        return carry

    col_ref[...] = ints_ref[...].astype(F32).T
    keep(logits(jnp.int32(0)))
    lax.fori_loop(0, count, body, 0)
    end = jnp.int32(count - 1)
    turn(end)
    store(end, product(end))


def unpack_vec(w, vec_ref):
    vec_ref[...] = w[:, 0:128].astype(F32).T


def moves_hot(ints):
    rows = lax.broadcasted_iota(jnp.int32, (16, ints.shape[1]), 0)
    return jnp.where((rows == ints[0:1]) | (rows == 4), 1.0, 0.0).astype(BF16)


def table_of(vec_ref):
    rows = lax.broadcasted_iota(jnp.int32, (16, WIDTH), 0)
    return jnp.where(rows < 5, vec_ref[0:16, :], 0.0).astype(BF16)


def stem_forward(latent_ref, hot_ref, vec_ref, w, s_ref, n_ref, slope_ref, r_ref, pre_ref, n_at):
    table = table_of(vec_ref)
    scale = scales(vec_ref, 5, 1, True)

    def product(c):
        span = pl.ds(rows_of(c), CHUNK)
        return mm(latent_ref[span, :], w) + mm(hot_ref[span, :], table)

    def body(c, carry):
        following = product(jnp.minimum(c + 1, PARTS - 1))
        for u in range(0, CHUNK, UNIT):
            rows = pl.ds(rows_of(c) + u, UNIT)
            act, n, slope, r = norm_gelu(pre_ref[u:u + UNIT, :], *scale)
            s_ref[rows, :] = act
            n_ref[n_at, rows, :] = n
            slope_ref[n_at, rows, :] = slope.astype(slope_ref.dtype)
            r_ref[n_at, rows, :] = r
        pre_ref[...] = following
        return carry

    pre_ref[...] = product(jnp.int32(0))
    lax.fori_loop(0, PARTS, body, 0)


def stem_backward(latent_ref, hot_ref, s_ref, low_ref, n_ref, slope_ref, r_ref, n_at, d_pre_ref, gw_ref, g_at, gv_ref):
    def products(c):
        span = pl.ds(rows_of(c), CHUNK)
        low = low_ref[...]
        gw_ref[g_at] += mm_tn(latent_ref[span, :], low)
        gv_ref[0:16, :] += mm(hot_ref[:, span], low)

    def body(c, carry):
        products(jnp.maximum(c - 1, 0))
        shift = jnp.zeros((UNIT, WIDTH), F32)
        gain = shift
        held = []
        for u in range(0, CHUNK, UNIT):
            rows = pl.ds(rows_of(c) + u, UNIT)
            d_in, wf, wn = norm_back(s_ref[rows, :], slope_ref[n_at, rows, :], n_ref[n_at, rows, :], r_ref[n_at, rows, :])
            shift = shift + wf
            held.append(wn)
            if len(held) == GROUP:
                gain = gain + column_sums(held)
                held = []
            low = d_in.astype(BF16)
            low_ref[u:u + UNIT, :] = low
            d_pre_ref[rows, :] = low
        gv_ref[5:6, :] += fold(gain)
        gv_ref[6:7, :] += fold(shift)
        return carry

    low_ref[...] = jnp.zeros_like(low_ref)
    lax.fori_loop(0, PARTS, body, 0)
    products(PARTS - 1)


def clean_latent(latent_ref, lat_ref, rows_dev):
    lat_ref[...] = latent_ref[...]
    steps = -(-rows_dev // TILE)
    tail = rows_dev - (steps - 1) * TILE
    if tail < TILE:
        @pl.when(pl.program_id(0) == steps - 1)
        def _():
            lat_ref[tail:TILE, :] = jnp.zeros((TILE - tail, WIDTH), BF16)


def split_low(x):
    high = x.astype(BF16)
    return high, (x - high.astype(F32)).astype(BF16)


def join_pieces(pieces_ref, w_ref, at):
    rows = WIDTH // pieces_ref.shape[0]
    for f in range(pieces_ref.shape[0]):
        for m in range(pieces_ref.shape[1] // rows):
            w_ref[at + m, f * rows:(f + 1) * rows, :] = pieces_ref[f, m * rows:(m + 1) * rows, :]


def join_front(core_ref, front_refs, w_ref):
    if len(front_refs) == 1:
        join_pieces(front_refs[0], w_ref, 0)
    else:
        half = w_ref.shape[0] // 2
        for core in range(2):
            @pl.when(core_ref[0] == core)
            def _():
                join_pieces(front_refs[core], w_ref, 0)
                join_pieces(front_refs[1 - core], w_ref, half)


def cut_pieces(out_ref, m, matrix):
    rows = WIDTH // out_ref.shape[0]
    at = m * rows if isinstance(m, int) else pl.multiple_of(m * rows, rows)
    for f in range(out_ref.shape[0]):
        out_ref[f, pl.ds(at, rows), :] = matrix[f * rows:(f + 1) * rows, :].astype(BF16)


def cut_vectors(out_ref, at, wide):
    rows = WIDTH // out_ref.shape[0]
    half = rows // 2
    for f in range(out_ref.shape[0]):
        part = wide[f * rows:(f + 1) * rows, :]
        out_ref[f, at:at + half, :] = jnp.concatenate([part[0:half], part[half:rows]], axis=1).astype(BF16)


def copies(refs, away, sems, i, span, inward):
    out = []
    for k, (near, far) in enumerate(zip(refs, away)):
        ends = (far.at[i, span, :], near.at[i]) if inward else (near.at[i], far.at[i, span, :])
        out.append(pltpu.make_async_copy(*ends, sems.at[i, k]))
    return out


def tile_span(step):
    return pl.ds(pl.multiple_of(step * TILE, 128), TILE)


def first_kernel(layers, rows_dev, fronts, core_ref, latent_ref, ints_ref, *refs):
    front_refs = refs[:fronts]
    (
        n_out, slope_out, r_out, act_out, s_out_ref, vec_ref, w_ref, lat_ref, hot_ref, pre_ref, s_ref, n_ref, slope_ref, r_ref, act_ref, sems,
    ) = refs[fronts:]
    step, steps = pl.program_id(0), pl.num_programs(0)
    span = tile_span(step)
    refs, away = (n_ref, slope_ref, r_ref, act_ref), (n_out, slope_out, r_out, act_out)

    def start(i, count=4):
        for copy in copies(refs[:count], away, sems, i, span, False):
            copy.start()

    def wait(i, count=4):
        for copy in copies(refs[:count], away, sems, i, span, False):
            copy.wait()

    @pl.when(step == 0)
    def _():
        join_front(core_ref, front_refs, w_ref)
        unpack_vec(w_ref[0], vec_ref)

    clean_latent(latent_ref, lat_ref, rows_dev)
    hot_ref[...] = moves_hot(ints_ref[...]).T

    @pl.when(step > 0)
    def _():
        wait(SPLIT, 3)

    stem_forward(lat_ref, hot_ref, vec_ref, w_ref[1], s_ref, n_ref, slope_ref, r_ref, pre_ref, SPLIT)
    start(SPLIT, 3)

    def before_block(i):
        @pl.when(step > 0)
        def _():
            wait(i)

    save = (act_ref, n_ref, slope_ref, r_ref)
    forward_layers(0, SPLIT, layers, s_ref, save, vec_ref, w_ref, -2, 0, before_block, start)
    s_out_ref[...] = s_ref[0:TILE, :]

    @pl.when(step == steps - 1)
    def _():
        wait(SPLIT, 3)
        for i in range(SPLIT):
            wait(i)


def middle_kernel(
    layers, s_in_ref, ints_ref, vec_ref, hb_ref, w_ref, latents_ref, ds_ref, gv_ref, rep_ref, out_ref,
    wh_ref, wg_ref, s_ref, act_ref, n_ref, slope_ref, r_ref, low_ref, da_ref, turned_ref, dlog_ref, gw_ref, gh_ref, loss_ref, *chunk_refs,
):
    blocks = layers - SPLIT
    step = pl.program_id(0)

    @pl.when(step == 0)
    def _():
        for ref in (gw_ref, gh_ref, gv_ref, loss_ref):
            ref[...] = jnp.zeros_like(ref)
        turned_ref[...] = jnp.ones_like(turned_ref)
        dlog_ref[TILE:, :] = jnp.zeros_like(dlog_ref[TILE:, :])
        for k in range(3):
            wh_ref[:, k * WIDTH:(k + 1) * WIDTH] = w_ref[blocks + k]
        columns = vec_ref[...].T

        def scale(i, carry):
            wg_ref[i] = gained(w_ref[i], columns, 7 + SPLIT + i)
            return carry

        lax.fori_loop(0, blocks, scale, 0)

    s_ref[0:TILE, :] = s_in_ref[...]
    save = (act_ref, n_ref, slope_ref, r_ref)
    forward_layers(SPLIT, layers, layers, s_ref, save, vec_ref, w_ref, SPLIT, SPLIT)
    heads(ints_ref, s_ref, ds_ref, low_ref, wh_ref, hb_ref, latents_ref, turned_ref, dlog_ref, loss_ref, *chunk_refs)

    def beside(j, k):
        rows = pl.ds(pl.multiple_of(j * HEAD_CHUNK, 128), HEAD_CHUNK)
        columns = pl.ds(pl.multiple_of(k * WIDTH, WIDTH), WIDTH)
        gh_ref[k] += mm(turned_ref[:, rows], dlog_ref[rows, columns])

    backward_layers(SPLIT, layers, layers, ds_ref, low_ref, da_ref, save, wg_ref, SPLIT, SPLIT, gw_ref, gv_ref, SPLIT, None, beside)

    @pl.when(step == pl.num_programs(0) - 1)
    def _():
        def put(m, carry):
            cut_pieces(out_ref, m, gw_ref.at[m])
            return carry

        lax.fori_loop(0, blocks, put, 0)
        for k in range(3):
            cut_pieces(out_ref, blocks + k, gh_ref.at[k])
        row = lax.broadcasted_iota(jnp.int32, (8, WIDTH), 0)
        total = jnp.where(row == 3, jnp.concatenate([fold(loss_ref[...]), jnp.zeros((1, 128), F32)], axis=1), 0.0)
        for k in range(3):
            total = jnp.where(row == k, gh_ref[k, WIDTH:WIDTH + 1, :], total)
        rep_ref[...] = total
        at = (blocks + 3) * WIDTH // out_ref.shape[0]
        high, low = split_low(total)
        for f in range(out_ref.shape[0]):
            out_ref[f, at:at + 16, :] = jnp.concatenate([high, low], axis=0)


def last_kernel(layers, rows_dev, fronts, core_ref, latent_ref, ints_ref, ds_in_ref, n_in, slope_in, r_in, act_in, gv_in_ref, *refs):
    front_refs = refs[:fronts]
    (
        d_pre_ref, out_ref, stem_ref, w_ref, lat_ref, hot_ref, ds_ref, low_ref, da_ref, chunk_ref, n_ref, slope_ref, r_ref, act_ref, gw_ref, gv_ref,
        sems,
    ) = refs[fronts:]
    step, steps = pl.program_id(0), pl.num_programs(0)
    refs, away = (n_ref, slope_ref, r_ref, act_ref), (n_in, slope_in, r_in, act_in)

    def start(i, to, count=4):
        for copy in copies(refs[:count], away, sems, i, tile_span(to), True):
            copy.start()

    def wait(i, count=4):
        for copy in copies(refs[:count], away, sems, i, tile_span(step), True):
            copy.wait()

    @pl.when(step == 0)
    def _():
        start(SPLIT - 1, 0)
        join_front(core_ref, front_refs, w_ref)
        stem_ref[...] = w_ref[1]
        columns = w_ref[0, :, 0:128].astype(F32)

        def scale(i, carry):
            w_ref[2 + i] = gained(w_ref[2 + i], columns, 7 + i)
            return carry

        lax.fori_loop(0, SPLIT, scale, 0)
        gw_ref[...] = jnp.zeros_like(gw_ref)
        gv_ref[...] = gv_in_ref[...]

    clean_latent(latent_ref, lat_ref, rows_dev)
    hot_ref[...] = moves_hot(ints_ref[...])
    ds_ref[...] = ds_in_ref[...]
    low_ref[...] = ds_in_ref[...].astype(BF16)

    def after_block(i):
        @pl.when(step < steps - 1)
        def _():
            start(i, step + 1)

        @pl.when(i > 0)
        def _():
            wait(i - 1)

    wait(SPLIT - 1)

    @pl.when(step == 0)
    def _():
        for i in reversed(range(SPLIT - 1)):
            start(i, 0)
        start(SPLIT, 0, 3)

    save = (act_ref, n_ref, slope_ref, r_ref)
    backward_layers(0, SPLIT, layers, ds_ref, low_ref, da_ref, save, w_ref, -2, 0, gw_ref, gv_ref, -1, after_block)
    wait(SPLIT, 3)
    stem_backward(lat_ref, hot_ref, ds_ref, chunk_ref, n_ref, slope_ref, r_ref, SPLIT, d_pre_ref, gw_ref, 0, gv_ref)

    @pl.when(step < steps - 1)
    def _():
        start(SPLIT, step + 1, 3)

    @pl.when(step == steps - 1)
    def _():
        for m in range(SPLIT + 1):
            cut_pieces(out_ref, m, gw_ref[m])
        high, low = split_low(jnp.concatenate([gv_ref[...], jnp.zeros((64 - gv_ref.shape[0], WIDTH), F32)], axis=0))
        wide = jnp.concatenate([high, low], axis=0).astype(F32).T
        cut_vectors(out_ref, (SPLIT + 1) * WIDTH // out_ref.shape[0], wide)


def pack_kernel(
    fronts, core_ref, stem_ref, table_ref, stem_bias_ref, stem_gain_ref, stem_shift_ref, block_ref, gain_ref, shift_ref, bias_ref, value_ref, chance_ref, front_ref,
    back_ref, vec_ref,
):
    layers, shard = block_ref.shape[0], block_ref.shape[1]
    nq, nc = value_ref.shape[1], chance_ref.shape[1]
    vec_ref[...] = jnp.zeros_like(vec_ref)
    at = 0
    for ref in (table_ref, stem_bias_ref, stem_gain_ref, stem_shift_ref, gain_ref, shift_ref, bias_ref):
        rows = ref[...].astype(F32)
        rows = rows[None] if len(ref.shape) == 1 else rows
        vec_ref[at:at + rows.shape[0], 0:shard] = rows
        at += rows.shape[0]
    vectors = vec_ref[...].T[0:shard, :]
    vectors = jnp.concatenate([vectors, jnp.zeros_like(vectors)], axis=1).astype(BF16)
    entries = [lambda: vectors, lambda: stem_ref[...]] + [functools.partial(block_ref.__getitem__, i) for i in range(SPLIT)]
    half = len(entries) // fronts
    for core in range(fronts):
        @pl.when(core_ref[0] == core if fronts > 1 else core_ref[0] >= 0)
        def _():
            for m in range(half):
                entry = entries[core * half + m]()
                for f in range(front_ref.shape[0]):
                    front_ref[f, m * shard:(m + 1) * shard, :] = entry
    for i in range(SPLIT, layers):
        back_ref[i - SPLIT] = block_ref[i]
    at = layers - SPLIT
    back_ref[at:] = jnp.zeros_like(back_ref[at:])
    for k in range(3):
        width = min(WIDTH, nq - k * WIDTH)
        back_ref[at + k, :, 0:width] = value_ref[:, k * WIDTH:k * WIDTH + width]
    back_ref[at + 2, :, 128:128 + nc] = chance_ref[...]


def outputs_kernel(latents_ref, d_pre_ref, w_ref, hb_ref, stem_ref, value_ref, chance_ref, lgrad_ref, turned_ref, bias_ref):
    count = turned_ref.shape[0] // WIDTH

    @pl.when(pl.program_id(0) == 0)
    def _():
        at = w_ref.shape[0] - count
        for k in range(count):
            turned_ref[k * WIDTH:(k + 1) * WIDTH, :] = w_ref[at + k].T
        columns = jnp.broadcast_to(hb_ref[...].astype(F32), (8, count * WIDTH)).T
        bias_ref[...] = jnp.broadcast_to(columns[:, 0:1], bias_ref.shape)

    nq, nc = value_ref.shape[0], chance_ref.shape[0]
    wide = [slice(k, k + 128) for k in range(0, HEAD_CHUNK, 128)]

    def chunk(c, carry):
        span = pl.ds(pl.multiple_of(c * HEAD_CHUNK, 128), HEAD_CHUNK)
        logits = mm_nt(turned_ref[...], latents_ref[span, :])
        logits = jnp.concatenate([logits[:, x] + bias_ref[...] for x in wide], axis=1).astype(BF16)
        value_ref[:, span] = logits[0:nq]
        chance_ref[:, span] = logits[640:640 + nc]
        lgrad_ref[span, :] = mm_nt(d_pre_ref[span, :], stem_ref[...]).astype(BF16)
        return carry

    lax.fori_loop(0, TILE // HEAD_CHUNK, chunk, 0)


def total_rows(refs, rows):
    total = refs[0][rows, :].astype(F32)
    for ref in refs[1:]:
        total = total + ref[rows, :].astype(F32)
    return total


def sum_mid_kernel(in_ref, out_ref):
    refs = [in_ref.at[f] for f in range(in_ref.shape[0])]
    end = in_ref.shape[1]
    for at in range(0, end - 16, 32):
        out_ref[at:at + 32, :] = total_rows(refs, slice(at, at + 32)).astype(BF16)
    total = total_rows(refs, slice(end - 16, end))
    high, low = split_low(total[0:8] + total[8:16])
    out_ref[end - 16:end, :] = jnp.concatenate([high, low], axis=0)


def sum_end_kernel(in_ref, out_ref):
    refs = [in_ref.at[f] for f in range(in_ref.shape[0])]
    end, vec = in_ref.shape[1], WIDTH // in_ref.shape[0] // 2
    for at in range(0, end - vec, 32):
        out_ref[at:at + 32, :] = total_rows(refs, slice(at, at + 32)).astype(BF16)
    total = total_rows(refs, slice(end - vec, end))
    parts = []
    for k in (0, 128):
        parts += split_low(total[:, k:k + 64] + total[:, k + 64:k + 128])
    out_ref[end - vec:end, :] = jnp.concatenate(parts, axis=1)


def finish_kernel(count, compact, scale, stem_scale_ref, gain_ref, *refs):
    mids, ends = refs[:count], refs[count:2 * count]
    (
        loss_ref, stem_ref, table_ref, stem_bias_ref, stem_gain_ref, stem_shift_ref, block_ref, block_gain_ref, block_shift_ref,
        block_bias_ref, value_ref, value_bias_ref, chance_ref, chance_bias_ref,
    ) = refs[2 * count:]
    layers, shard, moves = block_ref.shape[0], block_ref.shape[1], table_ref.shape[0]
    nq, nc = value_ref.shape[1], chance_ref.shape[1]

    def mid_of(at, rows):
        return total_rows(mids, slice(at, at + rows)) * scale

    def end_of(at, rows):
        return total_rows(ends, slice(at, at + rows)) * scale

    for i in range(SPLIT, layers):
        block_ref[i] = mid_of((i - SPLIT) * shard, shard)
    for i in range(SPLIT):
        block_ref[i] = end_of((1 + i) * shard, shard)
    stem_ref[...] = end_of(0, shard)
    for k in range(3):
        width = min(WIDTH, nq - k * WIDTH)
        part = mid_of((layers - SPLIT + k) * shard, shard)
        value_ref[:, k * WIDTH:k * WIDTH + width] = part[:, 0:width]
    chance_ref[...] = part[:, 128:128 + nc]
    rep = mid_of((layers - SPLIT + 3) * shard, 16)
    rep = rep[0:8] + rep[8:16]
    only = lax.broadcasted_iota(jnp.int32, rep.shape, 0)
    bias = jnp.concatenate([jnp.sum(jnp.where(only == k, rep, 0.0), axis=0) for k in range(3)])
    value_bias_ref[...] = bias[0:nq]
    chance_bias_ref[...] = bias[640:640 + nc]
    loss_ref[0] = jnp.sum(rep[3:4])
    at = (1 + SPLIT) * shard
    if compact:
        small = end_of(at, shard // 2)
        small = jnp.concatenate([small[:, 0:128], small[:, 128:256]], axis=0)
    else:
        small = end_of(at, shard)[:, 0:128]
    if shard % 128:
        small = jnp.concatenate([small, jnp.zeros((128 - shard, 128), F32)], axis=0)
    small = small.T[:, 0:shard]
    small = small[0:64] + small[64:128]
    table_ref[...] = small[0:moves]
    stem_gain = stem_scale_ref[...].astype(F32)[None]
    stem_bias_ref[...] = small[moves:moves + 1]
    stem_gain_ref[...] = small[moves + 1:moves + 2] / stem_gain
    stem_shift_ref[...] = small[moves + 2:moves + 3] / (16.0 * stem_gain)
    at = moves + 3
    gain = gain_ref[...].astype(F32)
    block_gain_ref[...] = small[at:at + layers] / gain
    block_shift_ref[...] = small[at + layers:at + 2 * layers] / (16.0 * gain)
    block_bias_ref[...] = small[at + 2 * layers:at + 3 * layers]


SMEM = pl.BlockSpec(memory_space=pltpu.SMEM)
VMEM = pl.BlockSpec(memory_space=pltpu.VMEM)
ANY = pl.BlockSpec(memory_space=pl.ANY)


def params(mib):
    return pltpu.CompilerParams(vmem_limit_bytes=mib << 20)


def tiled(shape, dim):
    block = shape[:dim] + (TILE,) + shape[dim + 1:]
    return pl.BlockSpec(block, lambda i: (0,) * dim + (i,) + (0,) * (len(shape) - dim - 1))


def whole(shape):
    return pl.BlockSpec(shape, lambda i: (0,) * len(shape))


def once(shape):
    return pl.BlockSpec(shape, lambda i: (0,) * len(shape), pipeline_mode=pl.Buffered(1))


def struct(shape, dtype):
    return jax.ShapeDtypeStruct(shape, dtype)


def exchange(x, axis, size):
    return [lax.ppermute(x, axis, [(i, i ^ k) for i in range(size)]) for k in range(1, size)]


def per_device(
    latent, actions, value_bins, chance_codes, step_mask, stem_weight, action_table, stem_bias, stem_gain, stem_shift,
    block_weight, block_gain, block_shift, block_bias, value_weight, value_bias, chance_weight, chance_bias,
):
    n_dp, n_fsdp = lax.axis_size("dp"), lax.axis_size("fsdp")
    rows_dev = latent.shape[0]
    layers, shard = block_weight.shape[0], block_weight.shape[1]
    nq, nc = value_weight.shape[1], chance_weight.shape[1]
    moves = action_table.shape[0]
    steps = -(-rows_dev // TILE)
    padded = steps * TILE
    fast = shard % 16 == 0 and n_dp & (n_dp - 1) == 0

    pieces, piece_rows = (n_fsdp, shard) if fast else (1, WIDTH)
    fronts = 2 if fast and n_dp % 2 == 0 and SPLIT % 2 == 0 else 1
    core = (lax.axis_index("dp") % 2).astype(jnp.int32).reshape(1)
    n_front = (2 + SPLIT) // fronts
    front, back = pl.pallas_call(
        functools.partial(pack_kernel, fronts),
        in_specs=[SMEM] + [VMEM] * 11,
        out_specs=[VMEM] * 2,
        out_shape=[struct((pieces, n_front * shard, WIDTH), BF16), struct((layers - SPLIT + 3, shard, WIDTH), BF16)],
        scratch_shapes=[pltpu.VMEM((128, max(shard, 128)), F32)],
        name="pack",
    )(
        core, stem_weight, action_table, stem_bias, stem_gain, stem_shift, block_weight, block_gain, block_shift, block_bias,
        value_weight, chance_weight,
    )
    ints = jnp.pad(jnp.stack([actions, value_bins, chance_codes, step_mask]), ((0, 4), (0, padded - rows_dev)))
    none = lambda n: jnp.full((n,), -1e30, BF16)
    head_bias = jnp.concatenate([value_bias, none(640 - nq), chance_bias, none(128 - nc)])[None]
    if fast:
        w_fronts = [lax.all_to_all(front, "fsdp", 0, 0)]
        if fronts > 1:
            w_fronts[0], ints, head_bias = lax.optimization_barrier((w_fronts[0], ints, head_bias))
            w_fronts.append(lax.ppermute(w_fronts[0], "dp", [(i, i ^ 1) for i in range(n_dp)]))
    else:
        front = lax.all_gather(front.reshape(n_front, shard, WIDTH), "fsdp", axis=1, tiled=True)
        w_fronts = [front.reshape(1, n_front * WIDTH, WIDTH)]
    w_back = lax.all_gather(back, "fsdp", axis=1, tiled=True)

    ints_spec = pl.BlockSpec((8, TILE), lambda i: (0, i))
    saved = [
        struct((SPLIT + 1, padded, WIDTH), BF16),
        struct((SPLIT + 1, padded, WIDTH), BF16),
        struct((SPLIT + 1, padded, 128), F32),
        struct((SPLIT, padded, WIDTH), BF16),
    ]
    scratch = pltpu.VMEM
    kept = [scratch((x.shape[0], TILE, x.shape[2]), x.dtype) for x in saved] + [pltpu.SemaphoreType.DMA((SPLIT + 1, 4))]
    stream = struct((padded, WIDTH), F32)
    front_shape = (2 + SPLIT, WIDTH, WIDTH)
    *held, s_mid, vec = pl.pallas_call(
        functools.partial(first_kernel, layers, rows_dev, fronts),
        grid=(steps,),
        in_specs=[SMEM, tiled((rows_dev, WIDTH), 0), ints_spec] + [once(x.shape) for x in w_fronts],
        out_specs=[ANY] * 4 + [tiled(stream.shape, 0), whole((128, WIDTH))],
        out_shape=saved + [stream, struct((128, WIDTH), F32)],
        scratch_shapes=[
            scratch(front_shape, BF16), scratch((TILE, WIDTH), BF16), scratch((TILE, 16), BF16), scratch((CHUNK, WIDTH), F32),
            scratch((TILE + CHUNK, WIDTH), F32),
        ] + kept,
        compiler_params=params(62),
        cost_estimate=pl.CostEstimate(flops=rows_dev * WIDTH * WIDTH * 200, bytes_accessed=60 << 20, transcendentals=0),
        name="first",
    )(core, latent, ints, *w_fronts)

    blocks = layers - SPLIT
    compact = piece_rows % 32 == 0 and fast
    mid_shape = (pieces, (blocks + 3) * piece_rows + 16, WIDTH)
    end_shape = (pieces, (SPLIT + 1) * piece_rows + piece_rows // 2, WIDTH)
    latents, ds_mid, gv_mid, rep, parts_mid = pl.pallas_call(
        functools.partial(middle_kernel, layers),
        grid=(steps,),
        in_specs=[tiled(stream.shape, 0), ints_spec, once(vec.shape), once(head_bias.shape), once(w_back.shape)],
        out_specs=[
            tiled((rows_dev, WIDTH), 0), tiled(stream.shape, 0), whole((48, WIDTH)), whole((8, WIDTH)), whole(mid_shape),
        ],
        out_shape=[
            struct((rows_dev, WIDTH), BF16), stream, struct((48, WIDTH), F32), struct((8, WIDTH), F32), struct(mid_shape, BF16),
        ],
        scratch_shapes=[
            scratch((WIDTH, 3 * WIDTH), BF16),
            scratch((blocks, WIDTH, WIDTH), BF16),
            scratch((TILE + CHUNK, WIDTH), F32),
            scratch((blocks, TILE, WIDTH), BF16),
            scratch((blocks, TILE, WIDTH), BF16),
            scratch((blocks, TILE, WIDTH), F32),
            scratch((blocks, TILE, 128), F32),
            scratch((TILE, WIDTH), BF16),
            scratch((BACK, WIDTH), F32),
            scratch((WIDTH + 16, max(blocks * HEAD_CHUNK, TILE)), BF16),
            scratch((max(blocks * HEAD_CHUNK, TILE), 3 * WIDTH), BF16),
            scratch((blocks, WIDTH, WIDTH), F32),
            scratch((3, WIDTH + 16, WIDTH), F32),
            scratch((UNIT, 128), F32),
            scratch((HEAD_CHUNK, 3 * WIDTH), F32),
            scratch((TILE, 8), F32),
            scratch((2, HEAD_CHUNK, 128), F32),
            scratch((2, HEAD_CHUNK, 128), F32),
            scratch((HEAD_CHUNK, 3 * WIDTH), F32),
        ],
        compiler_params=params(62),
        cost_estimate=pl.CostEstimate(flops=rows_dev * WIDTH * WIDTH * 600, bytes_accessed=40 << 20, transcendentals=0),
        name="middle",
    )(s_mid, ints, vec, head_bias, w_back)

    d_pre, parts_end, w_stem = pl.pallas_call(
        functools.partial(last_kernel, layers, rows_dev, fronts),
        grid=(steps,),
        in_specs=[SMEM, tiled((rows_dev, WIDTH), 0), ints_spec, tiled(stream.shape, 0)]
        + [ANY] * 4 + [once((48, WIDTH))] + [once(x.shape) for x in w_fronts],
        out_specs=[tiled((padded, WIDTH), 0), whole(end_shape), whole((WIDTH, WIDTH))],
        out_shape=[struct((padded, WIDTH), BF16), struct(end_shape, BF16), struct((WIDTH, WIDTH), BF16)],
        scratch_shapes=[
            scratch(front_shape, BF16),
            scratch((TILE, WIDTH), BF16),
            scratch((16, TILE), BF16),
            scratch((TILE, WIDTH), F32),
            scratch((TILE, WIDTH), BF16),
            scratch((BACK, WIDTH), F32),
            scratch((CHUNK, WIDTH), BF16),
        ] + kept[:4] + [
            scratch((SPLIT + 1, WIDTH, WIDTH), F32),
            scratch((48, WIDTH), F32),
        ] + kept[4:],
        compiler_params=params(62),
        cost_estimate=pl.CostEstimate(flops=rows_dev * WIDTH * WIDTH * 150, bytes_accessed=60 << 20, transcendentals=0),
        name="last",
    )(core, latent, ints, ds_mid, *held, gv_mid, *w_fronts)

    def outputs_of(states):
        return pl.pallas_call(
            outputs_kernel,
            grid=(steps,),
            in_specs=[tiled((rows_dev, WIDTH), 0), tiled((padded, WIDTH), 0)]
            + [once(x.shape) for x in (w_back, head_bias, w_stem)],
            out_specs=[tiled((nq, rows_dev), 1), tiled((nc, rows_dev), 1), tiled((rows_dev, WIDTH), 0)],
            out_shape=[struct((nq, rows_dev), BF16), struct((nc, rows_dev), BF16), struct((rows_dev, WIDTH), BF16)],
            scratch_shapes=[scratch((3 * WIDTH, WIDTH), BF16), scratch((3 * WIDTH, 128), F32)],
            compiler_params=params(48),
            cost_estimate=pl.CostEstimate(flops=rows_dev * WIDTH * WIDTH * 20, bytes_accessed=16 << 20, transcendentals=0),
            name="outputs",
        )(states, d_pre, w_back, head_bias, w_stem)

    if fast:
        got_mid = lax.all_to_all(parts_mid, "fsdp", 0, 0)
        parts_end, got_mid, states = lax.optimization_barrier((parts_end, got_mid, latents))
        got_end = lax.all_to_all(parts_end, "fsdp", 0, 0)
        outputs = outputs_of(states)
        got_end, outputs = lax.optimization_barrier((got_end, outputs))

        def add(body, got, name):
            return pl.pallas_call(
                body, in_specs=[VMEM], out_specs=VMEM, out_shape=struct(got.shape[1:], BF16), name=name,
            )(got)

        mine_mid, mine_end = add(sum_mid_kernel, got_mid, "sum_mid"), add(sum_end_kernel, got_end, "sum_end")
        mids = [mine_mid] + exchange(mine_mid, "dp", n_dp)
        ends = [mine_end] + exchange(mine_end, "dp", n_dp)
    else:
        outputs = outputs_of(latents)

        def scatter(x, count):
            x = x[0, :count * WIDTH].reshape(count, WIDTH, WIDTH)
            x = lax.psum_scatter(x, "fsdp", scatter_dimension=1, tiled=True).astype(F32)
            return lax.psum(x, "dp").reshape(count * shard, WIDTH)

        rep = lax.psum(rep, ("dp", "fsdp"))
        vectors = parts_end[0, (SPLIT + 1) * WIDTH:]
        vectors = jnp.concatenate([vectors[:, 0:128], vectors[:, 128:256]], axis=0)
        vectors = jnp.concatenate([vectors, jnp.zeros_like(vectors)], axis=1)
        parts_end = jnp.concatenate([parts_end[:, :(SPLIT + 1) * WIDTH], vectors[None]], axis=1)
        mids = [jnp.concatenate([scatter(parts_mid, blocks + 3), rep, jnp.zeros((8, WIDTH), F32)])]
        ends = [scatter(parts_end, SPLIT + 2)]

    value_logits, chance_logits, latent_grad = outputs
    shapes = [
        (1,), (shard, WIDTH), (moves, shard), (1, shard), (1, shard), (1, shard), (layers, shard, WIDTH), (layers, shard),
        (layers, shard), (layers, shard), (shard, nq), (nq,), (shard, nc), (nc,),
    ]
    (
        loss, stem_grad, table_grad, stem_bias_grad, stem_gain_grad, stem_shift_grad, block_grad, gain_grad, shift_grad, bias_grad,
        value_grad, value_bias_grad, chance_grad, chance_bias_grad,
    ) = pl.pallas_call(
        functools.partial(finish_kernel, len(mids), compact, 1.0 / (rows_dev * n_dp * n_fsdp)),
        in_specs=[VMEM] * (2 + 2 * len(mids)),
        out_specs=[SMEM] + [VMEM] * (len(shapes) - 1),
        out_shape=[struct(x, F32) for x in shapes],
        name="finish",
    )(stem_gain, block_gain, *mids, *ends)
    return (
        latents,
        value_logits.T,
        chance_logits.T,
        loss.reshape(()),
        latent_grad,
        stem_grad,
        table_grad,
        stem_bias_grad.reshape(shard),
        stem_gain_grad.reshape(shard),
        stem_shift_grad.reshape(shard),
        block_grad,
        gain_grad,
        shift_grad,
        bias_grad,
        value_grad,
        value_bias_grad,
        chance_grad,
        chance_bias_grad,
    )


def solution(mesh):
    placed = (
        P(("dp", "fsdp"), None),
        P(("dp", "fsdp")),
        P(("dp", "fsdp")),
        P(("dp", "fsdp")),
        P(("dp", "fsdp")),
        P("fsdp", None),
        P(None, "fsdp"),
        P("fsdp"),
        P("fsdp"),
        P("fsdp"),
        P(None, "fsdp", None),
        P(None, "fsdp"),
        P(None, "fsdp"),
        P(None, "fsdp"),
        P("fsdp", None),
        P(),
        P("fsdp", None),
        P(),
    )
    return jax.shard_map(
        per_device,
        mesh=mesh,
        in_specs=placed,
        out_specs=(
            P(("dp", "fsdp"), None),
            P(("dp", "fsdp"), None),
            P(("dp", "fsdp"), None),
            P(),
            P(("dp", "fsdp"), None),
            P("fsdp", None),
            P(None, "fsdp"),
            P("fsdp"),
            P("fsdp"),
            P("fsdp"),
            P(None, "fsdp", None),
            P(None, "fsdp"),
            P(None, "fsdp"),
            P(None, "fsdp"),
            P("fsdp", None),
            P(),
            P("fsdp", None),
            P(),
        ),
        check_vma=False,
    )
```

```python
import functools
import jax
import jax.numpy as jnp
from jax import lax
from jax.experimental import pallas as pl
from jax.experimental.pallas import tpu as pltpu
from jax.sharding import PartitionSpec as P

F32 = jnp.float32
BF16 = jnp.bfloat16
WIDTH = 256
UNIT = 16
WIDE = 32
TILE = 1920
BACK = 640
CHUNK = 640
PARTS = TILE // CHUNK
HEAD_CHUNK = 384
SPLIT = 4
K0 = 2 * 0.7978845608028654
K1 = 8 * 0.7978845608028654 * 0.044715


def mm(a, b):
    return lax.dot_general(a, b, (((1,), (0,)), ((), ())), preferred_element_type=F32)


def mm_nt(a, b):
    return lax.dot_general(a, b, (((1,), (1,)), ((), ())), preferred_element_type=F32)


def mm_tn(a, b):
    return lax.dot_general(a, b, (((0,), (0,)), ((), ())), preferred_element_type=F32)


def norm_gelu(s, gain8, gain_slope, shift_half):
    mean = jnp.sum(s, axis=1, keepdims=True) * (1.0 / WIDTH)
    center = s - mean
    r = lax.rsqrt(jnp.sum(center * center, axis=1, keepdims=True) + WIDTH * 1e-5)
    n = center * r
    h = n * gain8 + shift_half
    y = h * h
    t = jnp.tanh(h * (K0 + K1 * y))
    e1 = 1.0 + t
    bend = (h * (y + K0 / (3 * K1))) * (1.0 - t)
    slope = e1 * (1.0 / (3 * K1) + bend)
    if gain_slope is not None:
        slope = slope * gain_slope
    return h * e1, n.astype(BF16), slope, jnp.broadcast_to(r, (s.shape[0], 128))


def scales(vec_ref, at, layers, slope):
    gain = vec_ref[pl.ds(at, 1), :]
    return gain * 8.0, gain * (8.0 * 3 * K1) if slope else None, vec_ref[pl.ds(at + layers, 1), :] * 0.5


def gained(w, columns, at):
    lane = lax.broadcasted_iota(jnp.int32, columns.shape, 1)
    gain = jnp.sum(jnp.where(lane == at, columns, 0.0), axis=1, keepdims=True)
    return (w.astype(F32) * (gain * (8.0 * 3 * K1))).astype(BF16)


def lane_sums(x):
    total = lax.reduce_sum(x[:, 0:128] + x[:, 128:256], (1,))
    return jnp.broadcast_to(total[:, None], (x.shape[0], 128))


def norm_back(da, slope, n, r):
    w = da * slope.astype(F32)
    w16 = w.astype(BF16)
    wn = w16 * n
    m1 = lane_sums(w16) * BF16(1.0 / WIDTH)
    m2 = lane_sums(wn)
    halves = [
        (w[:, k:k + 128] - (m1 + n[:, k:k + 128] * m2).astype(F32)) * r for k in (0, 128)
    ]
    return jnp.concatenate(halves, axis=1), w, wn


def rows_of(c):
    return pl.multiple_of(c * CHUNK, UNIT)


def activate(base, s_ref, save, i, scale):
    act_ref, n_ref, slope_ref, r_ref = save
    for u in range(0, CHUNK, WIDE):
        rows = pl.ds(base + u, WIDE)
        act, n, slope, r = norm_gelu(s_ref[rows, :], *scale)
        act_ref[i, rows, :] = act.astype(BF16)
        n_ref[i, rows, :] = n
        slope_ref[i, rows, :] = slope.astype(slope_ref.dtype)
        r_ref[i, rows, :] = r


def following(i, c, parts, change):
    end = c == parts - 1
    return jnp.where(end, i + change, i), jnp.where(end, 0, c + 1)


def forward_layers(first, last, layers, s_ref, save, vec_ref, w_ref, w_at, save_at, before_block=None, after_block=None):
    act_ref = save[0]

    def product(i, c):
        return mm(act_ref[i - save_at, pl.ds(rows_of(c), CHUNK), :], w_ref[i - w_at])

    def residual(i, base, out):
        bias = vec_ref[pl.ds(7 + 2 * layers + i, 1), :]
        for u in range(0, CHUNK, WIDE):
            rows = pl.ds(base + u, WIDE)
            s_ref[rows, :] = s_ref[rows, :] + (out[u:u + WIDE, :] + bias)

    def block(i, carry):
        if before_block is not None:
            before_block(i)

        def chunk(c, carry):
            old_i, old_c, base = carry
            out = product(old_i, old_c)
            activate(rows_of(c), s_ref, save, i - save_at, scales(vec_ref, 7 + i, layers, False))
            residual(old_i, pl.multiple_of(base, UNIT), out)
            return i, c, c * CHUNK

        carry = lax.fori_loop(0, PARTS, chunk, carry)
        if after_block is not None:
            after_block(i)
        return carry

    start = jnp.int32(first), jnp.int32(0), jnp.int32(TILE)
    i, c, base = lax.fori_loop(first, last, block, start)
    residual(i, pl.multiple_of(base, UNIT), product(i, c))


def column_sums(parts):
    total = parts[0]
    for part in parts[1:]:
        total = total + part
    return total.astype(F32)


GROUP = 4


def fold(x):
    return jnp.sum(x, axis=0, keepdims=True)


def backward_layers(first, last, layers, s_ref, low_ref, da_ref, save, w_ref, w_at, save_at, gw_ref, gv_ref, g_at, after_block=None, beside=None):
    act_ref, n_ref, slope_ref, r_ref = save

    def product(i, c):
        return mm_nt(low_ref[pl.ds(pl.multiple_of(c * BACK, UNIT), BACK), :], w_ref[i - w_at])

    def chunk(i, c):
        base = pl.multiple_of(c * BACK, UNIT)
        next_i, next_c = following(i, c, TILE // BACK, -1)
        next_i = jnp.maximum(next_i, first)
        next_da = product(next_i, next_c)
        gw_ref[i - g_at] += mm_tn(act_ref[i - save_at, pl.ds(base, BACK), :], low_ref[pl.ds(base, BACK), :])
        if beside is not None:
            beside(last - 1 - i, c)
        zero = jnp.zeros((WIDE, WIDTH), F32)
        shift, gain, bias = zero, zero, zero
        held = []
        for u in range(0, BACK, WIDE):
            rows = pl.ds(base + u, WIDE)
            at = (i - save_at, rows, slice(None))
            d_in, wf, wn = norm_back(da_ref[u:u + WIDE, :], slope_ref[at], n_ref[at], r_ref[at])
            shift = shift + wf
            held.append(wn)
            if len(held) == GROUP:
                gain = gain + column_sums(held)
                held = []
            ds = s_ref[rows, :]
            bias = bias + ds
            ds = ds + d_in
            s_ref[rows, :] = ds
            low_ref[rows, :] = ds.astype(BF16)
        da_ref[...] = next_da
        for k, x in enumerate((gain, shift, bias)):
            gv_ref[pl.ds(7 + k * layers + i, 1), :] += fold(x)

    def block(j, carry):
        i = last - 1 - j
        lax.fori_loop(0, TILE // BACK, lambda c, carry: chunk(i, c) or carry, 0)
        if after_block is not None:
            after_block(i)
        return carry

    da_ref[...] = product(last - 1, 0)
    lax.fori_loop(0, last - first, block, 0)


def softmax(full_ref, col_ref, top_ref, total_ref, expon_ref, dlog_ref, at, loss_ref):
    units = [slice(u, u + UNIT) for u in range(0, HEAD_CHUNK, UNIT)]
    lane = lax.broadcasted_iota(jnp.int32, (1, 128), 1).astype(F32)
    spread = lambda x: jnp.broadcast_to(x, (UNIT, 128))
    cols = [slice(k * 128, (k + 1) * 128) for k in range(6)]
    for rows in units:
        logits = [full_ref[rows, cols[k]] for k in range(6)]
        top = functools.reduce(jnp.maximum, logits[:5])
        top_ref[0, rows, :] = spread(jnp.max(top, axis=1, keepdims=True))
        top_ref[1, rows, :] = spread(jnp.max(logits[5], axis=1, keepdims=True))
    for rows in units:
        expon = [jnp.exp(full_ref[rows, cols[k]] - top_ref[k // 5, rows, :]) for k in range(6)]
        for k in range(6):
            expon_ref[rows, cols[k]] = expon[k]
        total_ref[0, rows, :] = spread(jnp.sum(functools.reduce(jnp.add, expon[:5]), axis=1, keepdims=True))
        total_ref[1, rows, :] = spread(jnp.sum(expon[5], axis=1, keepdims=True))
    loss = jnp.zeros((UNIT, 128), F32)
    for rows in units:
        _, *targets, mask = (spread(col_ref[pl.ds(at + rows.start, UNIT), k:k + 1]) for k in range(4))
        zero = jnp.zeros_like(mask)
        hits = [zero, zero]
        weights = [mask / total_ref[j, rows, :] for j in range(2)]
        for k in range(6):
            j = k // 5
            hit = lane + 128.0 * (k % 5) == targets[j]
            hits[j] = jnp.where(hit, full_ref[rows, cols[k]], hits[j])
            grad = expon_ref[rows, cols[k]] * weights[j] - jnp.where(hit, mask, zero)
            dlog_ref[pl.ds(at + rows.start, UNIT), cols[k]] = grad.astype(BF16)
        row = jnp.log(total_ref[0, rows, :]) + jnp.log(total_ref[1, rows, :]) + (top_ref[0, rows, :] + top_ref[1, rows, :])
        loss = loss + mask * (row * (1.0 / 128) - (hits[0] + hits[1]))
    loss_ref[...] += loss


def heads(
    ints_ref, s_ref, ds_ref, low_ref, wh_ref, hb_ref, latents_ref, turned_ref, dlog_ref, loss_ref, full_ref, col_ref, top_ref, total_ref,
    expon_ref,
):
    size = HEAD_CHUNK
    count = TILE // size

    def span_of(t):
        return pl.ds(pl.multiple_of(t * size, 128), size)

    def logits(t):
        lat = s_ref[span_of(t), :].astype(BF16)
        latents_ref[span_of(t), :] = lat
        return mm(lat, wh_ref[...])

    def keep(parts):
        full_ref[...] = parts + hb_ref[...].astype(F32)

    def turn(t):
        turned_ref[0:WIDTH, span_of(t)] = latents_ref[span_of(t), :].T

    def product(t):
        return mm_nt(dlog_ref[span_of(t), :], wh_ref[...])

    def store(t, ds):
        ds_ref[span_of(t), :] = ds
        low_ref[span_of(t), :] = ds.astype(BF16)

    def body(t, carry):
        before = jnp.maximum(t - 1, 0)
        following = logits(jnp.minimum(t + 1, count - 1))
        turn(before)
        ds = product(before)
        softmax(full_ref, col_ref, top_ref, total_ref, expon_ref, dlog_ref, pl.multiple_of(t * size, 128), loss_ref)
        store(before, ds)
        keep(following)
        return carry

    col_ref[...] = ints_ref[...].astype(F32).T
    keep(logits(jnp.int32(0)))
    lax.fori_loop(0, count, body, 0)
    end = jnp.int32(count - 1)
    turn(end)
    store(end, product(end))


def unpack_vec(w, vec_ref):
    vec_ref[...] = w[:, 0:128].astype(F32).T


def moves_hot(ints):
    rows = lax.broadcasted_iota(jnp.int32, (16, ints.shape[1]), 0)
    return jnp.where((rows == ints[0:1]) | (rows == 4), 1.0, 0.0).astype(BF16)


def table_of(vec_ref):
    rows = lax.broadcasted_iota(jnp.int32, (16, WIDTH), 0)
    return jnp.where(rows < 5, vec_ref[0:16, :], 0.0).astype(BF16)


def stem_forward(latent_ref, hot_ref, vec_ref, w, s_ref, n_ref, slope_ref, r_ref, pre_ref, n_at):
    table = table_of(vec_ref)
    scale = scales(vec_ref, 5, 1, True)

    def product(c):
        span = pl.ds(rows_of(c), CHUNK)
        return mm(latent_ref[span, :], w) + mm(hot_ref[span, :], table)

    def body(c, carry):
        following = product(jnp.minimum(c + 1, PARTS - 1))
        for u in range(0, CHUNK, WIDE):
            rows = pl.ds(rows_of(c) + u, WIDE)
            act, n, slope, r = norm_gelu(pre_ref[u:u + WIDE, :], *scale)
            s_ref[rows, :] = act
            n_ref[n_at, rows, :] = n
            slope_ref[n_at, rows, :] = slope.astype(slope_ref.dtype)
            r_ref[n_at, rows, :] = r
        pre_ref[...] = following
        return carry

    pre_ref[...] = product(jnp.int32(0))
    lax.fori_loop(0, PARTS, body, 0)


def stem_backward(latent_ref, hot_ref, s_ref, low_ref, n_ref, slope_ref, r_ref, n_at, d_pre_ref, gw_ref, g_at, gv_ref):
    def products(c):
        span = pl.ds(rows_of(c), CHUNK)
        low = low_ref[...]
        gw_ref[g_at] += mm_tn(latent_ref[span, :], low)
        gv_ref[0:16, :] += mm(hot_ref[:, span], low)

    def body(c, carry):
        products(jnp.maximum(c - 1, 0))
        shift = jnp.zeros((WIDE, WIDTH), F32)
        gain = shift
        held = []
        for u in range(0, CHUNK, WIDE):
            rows = pl.ds(rows_of(c) + u, WIDE)
            d_in, wf, wn = norm_back(s_ref[rows, :], slope_ref[n_at, rows, :], n_ref[n_at, rows, :], r_ref[n_at, rows, :])
            shift = shift + wf
            held.append(wn)
            if len(held) == GROUP:
                gain = gain + column_sums(held)
                held = []
            low = d_in.astype(BF16)
            low_ref[u:u + WIDE, :] = low
            d_pre_ref[rows, :] = low
        gv_ref[5:6, :] += fold(gain)
        gv_ref[6:7, :] += fold(shift)
        return carry

    low_ref[...] = jnp.zeros_like(low_ref)
    lax.fori_loop(0, PARTS, body, 0)
    products(PARTS - 1)


def clean_latent(latent_ref, lat_ref, rows_dev):
    lat_ref[...] = latent_ref[...]
    steps = -(-rows_dev // TILE)
    tail = rows_dev - (steps - 1) * TILE
    if tail < TILE:
        @pl.when(pl.program_id(0) == steps - 1)
        def _():
            lat_ref[tail:TILE, :] = jnp.zeros((TILE - tail, WIDTH), BF16)


def split_low(x):
    high = x.astype(BF16)
    return high, (x - high.astype(F32)).astype(BF16)


def join_pieces(pieces_ref, w_ref, at):
    rows = WIDTH // pieces_ref.shape[0]
    for f in range(pieces_ref.shape[0]):
        for m in range(pieces_ref.shape[1] // rows):
            w_ref[at + m, f * rows:(f + 1) * rows, :] = pieces_ref[f, m * rows:(m + 1) * rows, :]


def join_front(core_ref, front_refs, w_ref):
    if len(front_refs) == 1:
        join_pieces(front_refs[0], w_ref, 0)
    else:
        half = w_ref.shape[0] // 2
        for core in range(2):
            @pl.when(core_ref[0] == core)
            def _():
                join_pieces(front_refs[core], w_ref, 0)
                join_pieces(front_refs[1 - core], w_ref, half)


def cut_pieces(out_ref, m, matrix):
    rows = WIDTH // out_ref.shape[0]
    at = m * rows if isinstance(m, int) else pl.multiple_of(m * rows, rows)
    for f in range(out_ref.shape[0]):
        out_ref[f, pl.ds(at, rows), :] = matrix[f * rows:(f + 1) * rows, :].astype(BF16)


def cut_vectors(out_ref, at, wide):
    rows = WIDTH // out_ref.shape[0]
    half = rows // 2
    for f in range(out_ref.shape[0]):
        part = wide[f * rows:(f + 1) * rows, :]
        out_ref[f, at:at + half, :] = jnp.concatenate([part[0:half], part[half:rows]], axis=1).astype(BF16)


def copies(refs, away, sems, i, span, inward):
    out = []
    for k, (near, far) in enumerate(zip(refs, away)):
        ends = (far.at[i, span, :], near.at[i]) if inward else (near.at[i], far.at[i, span, :])
        out.append(pltpu.make_async_copy(*ends, sems.at[i, k]))
    return out


def tile_span(step):
    return pl.ds(pl.multiple_of(step * TILE, 128), TILE)


def first_kernel(layers, rows_dev, fronts, core_ref, latent_ref, ints_ref, *refs):
    front_refs = refs[:fronts]
    (
        n_out, slope_out, r_out, act_out, s_out_ref, vec_ref, w_ref, lat_ref, hot_ref, pre_ref, s_ref, n_ref, slope_ref, r_ref, act_ref, sems,
    ) = refs[fronts:]
    step, steps = pl.program_id(0), pl.num_programs(0)
    span = tile_span(step)
    refs, away = (n_ref, slope_ref, r_ref, act_ref), (n_out, slope_out, r_out, act_out)

    def start(i, count=4):
        for copy in copies(refs[:count], away, sems, i, span, False):
            copy.start()

    def wait(i, count=4):
        for copy in copies(refs[:count], away, sems, i, span, False):
            copy.wait()

    @pl.when(step == 0)
    def _():
        join_front(core_ref, front_refs, w_ref)
        unpack_vec(w_ref[0], vec_ref)

    clean_latent(latent_ref, lat_ref, rows_dev)
    hot_ref[...] = moves_hot(ints_ref[...]).T

    @pl.when(step > 0)
    def _():
        wait(SPLIT, 3)

    stem_forward(lat_ref, hot_ref, vec_ref, w_ref[1], s_ref, n_ref, slope_ref, r_ref, pre_ref, SPLIT)
    start(SPLIT, 3)

    def before_block(i):
        @pl.when(step > 0)
        def _():
            wait(i)

    save = (act_ref, n_ref, slope_ref, r_ref)
    forward_layers(0, SPLIT, layers, s_ref, save, vec_ref, w_ref, -2, 0, before_block, start)
    s_out_ref[...] = s_ref[0:TILE, :]

    @pl.when(step == steps - 1)
    def _():
        wait(SPLIT, 3)
        for i in range(SPLIT):
            wait(i)


def middle_kernel(
    layers, s_in_ref, ints_ref, vec_ref, hb_ref, w_ref, latents_ref, ds_ref, gv_ref, rep_ref, out_ref,
    wh_ref, wg_ref, s_ref, act_ref, n_ref, slope_ref, r_ref, low_ref, da_ref, turned_ref, dlog_ref, gw_ref, gh_ref, loss_ref, *chunk_refs,
):
    blocks = layers - SPLIT
    step = pl.program_id(0)

    @pl.when(step == 0)
    def _():
        for ref in (gw_ref, gh_ref, gv_ref, loss_ref):
            ref[...] = jnp.zeros_like(ref)
        turned_ref[WIDTH:, :] = jnp.ones_like(turned_ref[WIDTH:, :])
        turned_ref[0:WIDTH, TILE:] = jnp.zeros_like(turned_ref[0:WIDTH, TILE:])
        dlog_ref[TILE:, :] = jnp.zeros_like(dlog_ref[TILE:, :])
        for k in range(3):
            wh_ref[:, k * WIDTH:(k + 1) * WIDTH] = w_ref[blocks + k]
        columns = vec_ref[...].T

        def scale(i, carry):
            wg_ref[i] = gained(w_ref[i], columns, 7 + SPLIT + i)
            return carry

        lax.fori_loop(0, blocks, scale, 0)

    s_ref[0:TILE, :] = s_in_ref[...]
    save = (act_ref, n_ref, slope_ref, r_ref)
    forward_layers(SPLIT, layers, layers, s_ref, save, vec_ref, w_ref, SPLIT, SPLIT)
    heads(ints_ref, s_ref, ds_ref, low_ref, wh_ref, hb_ref, latents_ref, turned_ref, dlog_ref, loss_ref, *chunk_refs)

    def beside(j, k):
        rows = pl.ds(pl.multiple_of(j * HEAD_CHUNK, 128), HEAD_CHUNK)
        columns = pl.ds(pl.multiple_of(k * WIDTH, WIDTH), WIDTH)
        gh_ref[k] += mm(turned_ref[:, rows], dlog_ref[rows, columns])

    backward_layers(SPLIT, layers, layers, ds_ref, low_ref, da_ref, save, wg_ref, SPLIT, SPLIT, gw_ref, gv_ref, SPLIT, None, beside)

    @pl.when(step == pl.num_programs(0) - 1)
    def _():
        def put(m, carry):
            cut_pieces(out_ref, m, gw_ref.at[m])
            return carry

        lax.fori_loop(0, blocks, put, 0)
        for k in range(3):
            cut_pieces(out_ref, blocks + k, gh_ref.at[k])
        row = lax.broadcasted_iota(jnp.int32, (8, WIDTH), 0)
        total = jnp.where(row == 3, jnp.concatenate([fold(loss_ref[...]), jnp.zeros((1, 128), F32)], axis=1), 0.0)
        for k in range(3):
            total = jnp.where(row == k, gh_ref[k, WIDTH:WIDTH + 1, :], total)
        rep_ref[...] = total
        at = (blocks + 3) * WIDTH // out_ref.shape[0]
        high, low = split_low(total)
        for f in range(out_ref.shape[0]):
            out_ref[f, at:at + 16, :] = jnp.concatenate([high, low], axis=0)


def last_kernel(layers, rows_dev, fronts, core_ref, latent_ref, ints_ref, ds_in_ref, n_in, slope_in, r_in, act_in, gv_in_ref, *refs):
    front_refs = refs[:fronts]
    (
        d_pre_ref, out_ref, stem_ref, w_ref, lat_ref, hot_ref, ds_ref, low_ref, da_ref, chunk_ref, n_ref, slope_ref, r_ref, act_ref, gw_ref, gv_ref,
        sems,
    ) = refs[fronts:]
    step, steps = pl.program_id(0), pl.num_programs(0)
    refs, away = (n_ref, slope_ref, r_ref, act_ref), (n_in, slope_in, r_in, act_in)

    def start(i, to, count=4):
        for copy in copies(refs[:count], away, sems, i, tile_span(to), True):
            copy.start()

    def wait(i, count=4):
        for copy in copies(refs[:count], away, sems, i, tile_span(step), True):
            copy.wait()

    @pl.when(step == 0)
    def _():
        start(SPLIT - 1, 0)
        join_front(core_ref, front_refs, w_ref)
        stem_ref[...] = w_ref[1]
        columns = w_ref[0, :, 0:128].astype(F32)

        def scale(i, carry):
            w_ref[2 + i] = gained(w_ref[2 + i], columns, 7 + i)
            return carry

        lax.fori_loop(0, SPLIT, scale, 0)
        gw_ref[...] = jnp.zeros_like(gw_ref)
        gv_ref[...] = gv_in_ref[...]

    clean_latent(latent_ref, lat_ref, rows_dev)
    hot_ref[...] = moves_hot(ints_ref[...])
    ds_ref[...] = ds_in_ref[...]
    low_ref[...] = ds_in_ref[...].astype(BF16)

    def after_block(i):
        @pl.when(step < steps - 1)
        def _():
            start(i, step + 1)

        @pl.when(i > 0)
        def _():
            wait(i - 1)

    wait(SPLIT - 1)

    @pl.when(step == 0)
    def _():
        for i in reversed(range(SPLIT - 1)):
            start(i, 0)
        start(SPLIT, 0, 3)

    save = (act_ref, n_ref, slope_ref, r_ref)
    backward_layers(0, SPLIT, layers, ds_ref, low_ref, da_ref, save, w_ref, -2, 0, gw_ref, gv_ref, -1, after_block)
    wait(SPLIT, 3)
    stem_backward(lat_ref, hot_ref, ds_ref, chunk_ref, n_ref, slope_ref, r_ref, SPLIT, d_pre_ref, gw_ref, 0, gv_ref)

    @pl.when(step < steps - 1)
    def _():
        start(SPLIT, step + 1, 3)

    @pl.when(step == steps - 1)
    def _():
        for m in range(SPLIT + 1):
            cut_pieces(out_ref, m, gw_ref[m])
        high, low = split_low(jnp.concatenate([gv_ref[...], jnp.zeros((64 - gv_ref.shape[0], WIDTH), F32)], axis=0))
        wide = jnp.concatenate([high, low], axis=0).astype(F32).T
        cut_vectors(out_ref, (SPLIT + 1) * WIDTH // out_ref.shape[0], wide)


def pack_kernel(
    fronts, core_ref, stem_ref, table_ref, stem_bias_ref, stem_gain_ref, stem_shift_ref, block_ref, gain_ref, shift_ref, bias_ref, value_ref, chance_ref, front_ref,
    back_ref, vec_ref,
):
    layers, shard = block_ref.shape[0], block_ref.shape[1]
    nq, nc = value_ref.shape[1], chance_ref.shape[1]
    vec_ref[...] = jnp.zeros_like(vec_ref)
    at = 0
    for ref in (table_ref, stem_bias_ref, stem_gain_ref, stem_shift_ref, gain_ref, shift_ref, bias_ref):
        rows = ref[...].astype(F32)
        rows = rows[None] if len(ref.shape) == 1 else rows
        vec_ref[at:at + rows.shape[0], 0:shard] = rows
        at += rows.shape[0]
    vectors = vec_ref[...].T[0:shard, :]
    vectors = jnp.concatenate([vectors, jnp.zeros_like(vectors)], axis=1).astype(BF16)
    entries = [lambda: vectors, lambda: stem_ref[...]] + [functools.partial(block_ref.__getitem__, i) for i in range(SPLIT)]
    half = len(entries) // fronts
    for core in range(fronts):
        @pl.when(core_ref[0] == core if fronts > 1 else core_ref[0] >= 0)
        def _():
            for m in range(half):
                entry = entries[core * half + m]()
                for f in range(front_ref.shape[0]):
                    front_ref[f, m * shard:(m + 1) * shard, :] = entry
    for i in range(SPLIT, layers):
        back_ref[i - SPLIT] = block_ref[i]
    at = layers - SPLIT
    back_ref[at:] = jnp.zeros_like(back_ref[at:])
    for k in range(3):
        width = min(WIDTH, nq - k * WIDTH)
        back_ref[at + k, :, 0:width] = value_ref[:, k * WIDTH:k * WIDTH + width]
    back_ref[at + 2, :, 128:128 + nc] = chance_ref[...]


def outputs_kernel(latents_ref, d_pre_ref, w_ref, hb_ref, stem_ref, value_ref, chance_ref, lgrad_ref, turned_ref, bias_ref):
    count = turned_ref.shape[0] // WIDTH

    @pl.when(pl.program_id(0) == 0)
    def _():
        at = w_ref.shape[0] - count
        for k in range(count):
            turned_ref[k * WIDTH:(k + 1) * WIDTH, :] = w_ref[at + k].T
        columns = jnp.broadcast_to(hb_ref[...].astype(F32), (8, count * WIDTH)).T
        bias_ref[...] = jnp.broadcast_to(columns[:, 0:1], bias_ref.shape)

    nq, nc = value_ref.shape[0], chance_ref.shape[0]
    wide = [slice(k, k + 128) for k in range(0, HEAD_CHUNK, 128)]

    def chunk(c, carry):
        span = pl.ds(pl.multiple_of(c * HEAD_CHUNK, 128), HEAD_CHUNK)
        logits = mm_nt(turned_ref[...], latents_ref[span, :])
        logits = jnp.concatenate([logits[:, x] + bias_ref[...] for x in wide], axis=1).astype(BF16)
        value_ref[:, span] = logits[0:nq]
        chance_ref[:, span] = logits[640:640 + nc]
        lgrad_ref[span, :] = mm_nt(d_pre_ref[span, :], stem_ref[...]).astype(BF16)
        return carry

    lax.fori_loop(0, TILE // HEAD_CHUNK, chunk, 0)


def total_rows(refs, rows):
    total = refs[0][rows, :].astype(F32)
    for ref in refs[1:]:
        total = total + ref[rows, :].astype(F32)
    return total


def sum_mid_kernel(in_ref, out_ref):
    refs = [in_ref.at[f] for f in range(in_ref.shape[0])]
    end = in_ref.shape[1]
    for at in range(0, end - 16, 32):
        out_ref[at:at + 32, :] = total_rows(refs, slice(at, at + 32)).astype(BF16)
    total = total_rows(refs, slice(end - 16, end))
    high, low = split_low(total[0:8] + total[8:16])
    out_ref[end - 16:end, :] = jnp.concatenate([high, low], axis=0)


def sum_end_kernel(in_ref, out_ref):
    refs = [in_ref.at[f] for f in range(in_ref.shape[0])]
    end, vec = in_ref.shape[1], WIDTH // in_ref.shape[0] // 2
    for at in range(0, end - vec, 32):
        out_ref[at:at + 32, :] = total_rows(refs, slice(at, at + 32)).astype(BF16)
    total = total_rows(refs, slice(end - vec, end))
    parts = []
    for k in (0, 128):
        parts += split_low(total[:, k:k + 64] + total[:, k + 64:k + 128])
    out_ref[end - vec:end, :] = jnp.concatenate(parts, axis=1)


def finish_kernel(count, compact, scale, stem_scale_ref, gain_ref, *refs):
    mids, ends = refs[:count], refs[count:2 * count]
    (
        loss_ref, stem_ref, table_ref, stem_bias_ref, stem_gain_ref, stem_shift_ref, block_ref, block_gain_ref, block_shift_ref,
        block_bias_ref, value_ref, value_bias_ref, chance_ref, chance_bias_ref,
    ) = refs[2 * count:]
    layers, shard, moves = block_ref.shape[0], block_ref.shape[1], table_ref.shape[0]
    nq, nc = value_ref.shape[1], chance_ref.shape[1]

    def mid_of(at, rows):
        return total_rows(mids, slice(at, at + rows)) * scale

    def end_of(at, rows):
        return total_rows(ends, slice(at, at + rows)) * scale

    for i in range(SPLIT, layers):
        block_ref[i] = mid_of((i - SPLIT) * shard, shard)
    for i in range(SPLIT):
        block_ref[i] = end_of((1 + i) * shard, shard)
    stem_ref[...] = end_of(0, shard)
    for k in range(3):
        width = min(WIDTH, nq - k * WIDTH)
        part = mid_of((layers - SPLIT + k) * shard, shard)
        value_ref[:, k * WIDTH:k * WIDTH + width] = part[:, 0:width]
    chance_ref[...] = part[:, 128:128 + nc]
    rep = mid_of((layers - SPLIT + 3) * shard, 16)
    rep = rep[0:8] + rep[8:16]
    only = lax.broadcasted_iota(jnp.int32, rep.shape, 0)
    bias = jnp.concatenate([jnp.sum(jnp.where(only == k, rep, 0.0), axis=0) for k in range(3)])
    value_bias_ref[...] = bias[0:nq]
    chance_bias_ref[...] = bias[640:640 + nc]
    loss_ref[0] = jnp.sum(rep[3:4])
    at = (1 + SPLIT) * shard
    if compact:
        small = end_of(at, shard // 2)
        small = jnp.concatenate([small[:, 0:128], small[:, 128:256]], axis=0)
    else:
        small = end_of(at, shard)[:, 0:128]
    if shard % 128:
        small = jnp.concatenate([small, jnp.zeros((128 - shard, 128), F32)], axis=0)
    small = small.T[:, 0:shard]
    small = small[0:64] + small[64:128]
    table_ref[...] = small[0:moves]
    stem_gain = stem_scale_ref[...].astype(F32)[None]
    stem_bias_ref[...] = small[moves:moves + 1]
    stem_gain_ref[...] = small[moves + 1:moves + 2] / stem_gain
    stem_shift_ref[...] = small[moves + 2:moves + 3] / (16.0 * stem_gain)
    at = moves + 3
    gain = gain_ref[...].astype(F32)
    block_gain_ref[...] = small[at:at + layers] / gain
    block_shift_ref[...] = small[at + layers:at + 2 * layers] / (16.0 * gain)
    block_bias_ref[...] = small[at + 2 * layers:at + 3 * layers]


SMEM = pl.BlockSpec(memory_space=pltpu.SMEM)
VMEM = pl.BlockSpec(memory_space=pltpu.VMEM)
ANY = pl.BlockSpec(memory_space=pl.ANY)


def params(mib):
    return pltpu.CompilerParams(vmem_limit_bytes=mib << 20)


def tiled(shape, dim):
    block = shape[:dim] + (TILE,) + shape[dim + 1:]
    return pl.BlockSpec(block, lambda i: (0,) * dim + (i,) + (0,) * (len(shape) - dim - 1))


def whole(shape):
    return pl.BlockSpec(shape, lambda i: (0,) * len(shape))


def once(shape):
    return pl.BlockSpec(shape, lambda i: (0,) * len(shape), pipeline_mode=pl.Buffered(1))


def struct(shape, dtype):
    return jax.ShapeDtypeStruct(shape, dtype)


def exchange(x, axis, size):
    return [lax.ppermute(x, axis, [(i, i ^ k) for i in range(size)]) for k in range(1, size)]


def per_device(
    latent, actions, value_bins, chance_codes, step_mask, stem_weight, action_table, stem_bias, stem_gain, stem_shift,
    block_weight, block_gain, block_shift, block_bias, value_weight, value_bias, chance_weight, chance_bias,
):
    n_dp, n_fsdp = lax.axis_size("dp"), lax.axis_size("fsdp")
    rows_dev = latent.shape[0]
    layers, shard = block_weight.shape[0], block_weight.shape[1]
    nq, nc = value_weight.shape[1], chance_weight.shape[1]
    moves = action_table.shape[0]
    steps = -(-rows_dev // TILE)
    padded = steps * TILE
    fast = shard % 16 == 0 and n_dp & (n_dp - 1) == 0

    pieces, piece_rows = (n_fsdp, shard) if fast else (1, WIDTH)
    fronts = 2 if fast and n_dp % 2 == 0 and SPLIT % 2 == 0 else 1
    core = (lax.axis_index("dp") % 2).astype(jnp.int32).reshape(1)
    n_front = (2 + SPLIT) // fronts
    front, back = pl.pallas_call(
        functools.partial(pack_kernel, fronts),
        in_specs=[SMEM] + [VMEM] * 11,
        out_specs=[VMEM] * 2,
        out_shape=[struct((pieces, n_front * shard, WIDTH), BF16), struct((layers - SPLIT + 3, shard, WIDTH), BF16)],
        scratch_shapes=[pltpu.VMEM((128, max(shard, 128)), F32)],
        name="pack",
    )(
        core, stem_weight, action_table, stem_bias, stem_gain, stem_shift, block_weight, block_gain, block_shift, block_bias,
        value_weight, chance_weight,
    )
    ints = jnp.pad(jnp.stack([actions, value_bins, chance_codes, step_mask]), ((0, 4), (0, padded - rows_dev)))
    none = lambda n: jnp.full((n,), -1e30, BF16)
    head_bias = jnp.concatenate([value_bias, none(640 - nq), chance_bias, none(128 - nc)])[None]
    if fast:
        w_fronts = [lax.all_to_all(front, "fsdp", 0, 0)]
        if fronts > 1:
            w_fronts[0], ints, head_bias = lax.optimization_barrier((w_fronts[0], ints, head_bias))
            w_fronts.append(lax.ppermute(w_fronts[0], "dp", [(i, i ^ 1) for i in range(n_dp)]))
    else:
        front = lax.all_gather(front.reshape(n_front, shard, WIDTH), "fsdp", axis=1, tiled=True)
        w_fronts = [front.reshape(1, n_front * WIDTH, WIDTH)]
    w_back = lax.all_gather(back, "fsdp", axis=1, tiled=True)

    ints_spec = pl.BlockSpec((8, TILE), lambda i: (0, i))
    saved = [
        struct((SPLIT + 1, padded, WIDTH), BF16),
        struct((SPLIT + 1, padded, WIDTH), BF16),
        struct((SPLIT + 1, padded, 128), F32),
        struct((SPLIT, padded, WIDTH), BF16),
    ]
    scratch = pltpu.VMEM
    kept = [scratch((x.shape[0], TILE, x.shape[2]), x.dtype) for x in saved] + [pltpu.SemaphoreType.DMA((SPLIT + 1, 4))]
    stream = struct((padded, WIDTH), F32)
    front_shape = (2 + SPLIT, WIDTH, WIDTH)
    *held, s_mid, vec = pl.pallas_call(
        functools.partial(first_kernel, layers, rows_dev, fronts),
        grid=(steps,),
        in_specs=[SMEM, tiled((rows_dev, WIDTH), 0), ints_spec] + [once(x.shape) for x in w_fronts],
        out_specs=[ANY] * 4 + [tiled(stream.shape, 0), whole((128, WIDTH))],
        out_shape=saved + [stream, struct((128, WIDTH), F32)],
        scratch_shapes=[
            scratch(front_shape, BF16), scratch((TILE, WIDTH), BF16), scratch((TILE, 16), BF16), scratch((CHUNK, WIDTH), F32),
            scratch((TILE + CHUNK, WIDTH), F32),
        ] + kept,
        compiler_params=params(62),
        cost_estimate=pl.CostEstimate(flops=rows_dev * WIDTH * WIDTH * 200, bytes_accessed=60 << 20, transcendentals=0),
        name="first",
    )(core, latent, ints, *w_fronts)

    blocks = layers - SPLIT
    compact = piece_rows % 32 == 0 and fast
    mid_shape = (pieces, (blocks + 3) * piece_rows + 16, WIDTH)
    end_shape = (pieces, (SPLIT + 1) * piece_rows + piece_rows // 2, WIDTH)
    latents, ds_mid, gv_mid, rep, parts_mid = pl.pallas_call(
        functools.partial(middle_kernel, layers),
        grid=(steps,),
        in_specs=[tiled(stream.shape, 0), ints_spec, once(vec.shape), once(head_bias.shape), once(w_back.shape)],
        out_specs=[
            tiled((rows_dev, WIDTH), 0), tiled(stream.shape, 0), whole((48, WIDTH)), whole((8, WIDTH)), whole(mid_shape),
        ],
        out_shape=[
            struct((rows_dev, WIDTH), BF16), stream, struct((48, WIDTH), F32), struct((8, WIDTH), F32), struct(mid_shape, BF16),
        ],
        scratch_shapes=[
            scratch((WIDTH, 3 * WIDTH), BF16),
            scratch((blocks, WIDTH, WIDTH), BF16),
            scratch((TILE + CHUNK, WIDTH), F32),
            scratch((blocks, TILE, WIDTH), BF16),
            scratch((blocks, TILE, WIDTH), BF16),
            scratch((blocks, TILE, WIDTH), F32),
            scratch((blocks, TILE, 128), F32),
            scratch((TILE, WIDTH), BF16),
            scratch((BACK, WIDTH), F32),
            scratch((WIDTH + 16, max(blocks * HEAD_CHUNK, TILE)), BF16),
            scratch((max(blocks * HEAD_CHUNK, TILE), 3 * WIDTH), BF16),
            scratch((blocks, WIDTH, WIDTH), F32),
            scratch((3, WIDTH + 16, WIDTH), F32),
            scratch((UNIT, 128), F32),
            scratch((HEAD_CHUNK, 3 * WIDTH), F32),
            scratch((TILE, 8), F32),
            scratch((2, HEAD_CHUNK, 128), F32),
            scratch((2, HEAD_CHUNK, 128), F32),
            scratch((HEAD_CHUNK, 3 * WIDTH), F32),
        ],
        compiler_params=params(62),
        cost_estimate=pl.CostEstimate(flops=rows_dev * WIDTH * WIDTH * 600, bytes_accessed=40 << 20, transcendentals=0),
        name="middle",
    )(s_mid, ints, vec, head_bias, w_back)

    d_pre, parts_end, w_stem = pl.pallas_call(
        functools.partial(last_kernel, layers, rows_dev, fronts),
        grid=(steps,),
        in_specs=[SMEM, tiled((rows_dev, WIDTH), 0), ints_spec, tiled(stream.shape, 0)]
        + [ANY] * 4 + [once((48, WIDTH))] + [once(x.shape) for x in w_fronts],
        out_specs=[tiled((padded, WIDTH), 0), whole(end_shape), whole((WIDTH, WIDTH))],
        out_shape=[struct((padded, WIDTH), BF16), struct(end_shape, BF16), struct((WIDTH, WIDTH), BF16)],
        scratch_shapes=[
            scratch(front_shape, BF16),
            scratch((TILE, WIDTH), BF16),
            scratch((16, TILE), BF16),
            scratch((TILE, WIDTH), F32),
            scratch((TILE, WIDTH), BF16),
            scratch((BACK, WIDTH), F32),
            scratch((CHUNK, WIDTH), BF16),
        ] + kept[:4] + [
            scratch((SPLIT + 1, WIDTH, WIDTH), F32),
            scratch((48, WIDTH), F32),
        ] + kept[4:],
        compiler_params=params(62),
        cost_estimate=pl.CostEstimate(flops=rows_dev * WIDTH * WIDTH * 150, bytes_accessed=60 << 20, transcendentals=0),
        name="last",
    )(core, latent, ints, ds_mid, *held, gv_mid, *w_fronts)

    def outputs_of(states):
        return pl.pallas_call(
            outputs_kernel,
            grid=(steps,),
            in_specs=[tiled((rows_dev, WIDTH), 0), tiled((padded, WIDTH), 0)]
            + [once(x.shape) for x in (w_back, head_bias, w_stem)],
            out_specs=[tiled((nq, rows_dev), 1), tiled((nc, rows_dev), 1), tiled((rows_dev, WIDTH), 0)],
            out_shape=[struct((nq, rows_dev), BF16), struct((nc, rows_dev), BF16), struct((rows_dev, WIDTH), BF16)],
            scratch_shapes=[scratch((3 * WIDTH, WIDTH), BF16), scratch((3 * WIDTH, 128), F32)],
            compiler_params=params(48),
            cost_estimate=pl.CostEstimate(flops=rows_dev * WIDTH * WIDTH * 20, bytes_accessed=16 << 20, transcendentals=0),
            name="outputs",
        )(states, d_pre, w_back, head_bias, w_stem)

    if fast:
        got_mid = lax.all_to_all(parts_mid, "fsdp", 0, 0)
        parts_end, got_mid, states = lax.optimization_barrier((parts_end, got_mid, latents))
        got_end = lax.all_to_all(parts_end, "fsdp", 0, 0)
        outputs = outputs_of(states)
        got_end, outputs = lax.optimization_barrier((got_end, outputs))

        def add(body, got, name):
            return pl.pallas_call(
                body, in_specs=[VMEM], out_specs=VMEM, out_shape=struct(got.shape[1:], BF16), name=name,
            )(got)

        mine_mid, mine_end = add(sum_mid_kernel, got_mid, "sum_mid"), add(sum_end_kernel, got_end, "sum_end")
        mids = [mine_mid] + exchange(mine_mid, "dp", n_dp)
        ends = [mine_end] + exchange(mine_end, "dp", n_dp)
    else:
        outputs = outputs_of(latents)

        def scatter(x, count):
            x = x[0, :count * WIDTH].reshape(count, WIDTH, WIDTH)
            x = lax.psum_scatter(x, "fsdp", scatter_dimension=1, tiled=True).astype(F32)
            return lax.psum(x, "dp").reshape(count * shard, WIDTH)

        rep = lax.psum(rep, ("dp", "fsdp"))
        vectors = parts_end[0, (SPLIT + 1) * WIDTH:]
        vectors = jnp.concatenate([vectors[:, 0:128], vectors[:, 128:256]], axis=0)
        vectors = jnp.concatenate([vectors, jnp.zeros_like(vectors)], axis=1)
        parts_end = jnp.concatenate([parts_end[:, :(SPLIT + 1) * WIDTH], vectors[None]], axis=1)
        mids = [jnp.concatenate([scatter(parts_mid, blocks + 3), rep, jnp.zeros((8, WIDTH), F32)])]
        ends = [scatter(parts_end, SPLIT + 2)]

    value_logits, chance_logits, latent_grad = outputs
    shapes = [
        (1,), (shard, WIDTH), (moves, shard), (1, shard), (1, shard), (1, shard), (layers, shard, WIDTH), (layers, shard),
        (layers, shard), (layers, shard), (shard, nq), (nq,), (shard, nc), (nc,),
    ]
    (
        loss, stem_grad, table_grad, stem_bias_grad, stem_gain_grad, stem_shift_grad, block_grad, gain_grad, shift_grad, bias_grad,
        value_grad, value_bias_grad, chance_grad, chance_bias_grad,
    ) = pl.pallas_call(
        functools.partial(finish_kernel, len(mids), compact, 1.0 / (rows_dev * n_dp * n_fsdp)),
        in_specs=[VMEM] * (2 + 2 * len(mids)),
        out_specs=[SMEM] + [VMEM] * (len(shapes) - 1),
        out_shape=[struct(x, F32) for x in shapes],
        name="finish",
    )(stem_gain, block_gain, *mids, *ends)
    return (
        latents,
        value_logits.T,
        chance_logits.T,
        loss.reshape(()),
        latent_grad,
        stem_grad,
        table_grad,
        stem_bias_grad.reshape(shard),
        stem_gain_grad.reshape(shard),
        stem_shift_grad.reshape(shard),
        block_grad,
        gain_grad,
        shift_grad,
        bias_grad,
        value_grad,
        value_bias_grad,
        chance_grad,
        chance_bias_grad,
    )


def solution(mesh):
    placed = (
        P(("dp", "fsdp"), None),
        P(("dp", "fsdp")),
        P(("dp", "fsdp")),
        P(("dp", "fsdp")),
        P(("dp", "fsdp")),
        P("fsdp", None),
        P(None, "fsdp"),
        P("fsdp"),
        P("fsdp"),
        P("fsdp"),
        P(None, "fsdp", None),
        P(None, "fsdp"),
        P(None, "fsdp"),
        P(None, "fsdp"),
        P("fsdp", None),
        P(),
        P("fsdp", None),
        P(),
    )
    return jax.shard_map(
        per_device,
        mesh=mesh,
        in_specs=placed,
        out_specs=(
            P(("dp", "fsdp"), None),
            P(("dp", "fsdp"), None),
            P(("dp", "fsdp"), None),
            P(),
            P(("dp", "fsdp"), None),
            P("fsdp", None),
            P(None, "fsdp"),
            P("fsdp"),
            P("fsdp"),
            P("fsdp"),
            P(None, "fsdp", None),
            P(None, "fsdp"),
            P(None, "fsdp"),
            P(None, "fsdp"),
            P("fsdp", None),
            P(),
            P("fsdp", None),
            P(),
        ),
        check_vma=False,
    )
```

```python
import functools
import jax
import jax.numpy as jnp
from jax import lax
from jax.experimental import pallas as pl
from jax.experimental.pallas import tpu as pltpu
from jax.sharding import PartitionSpec as P

F32 = jnp.float32
BF16 = jnp.bfloat16
WIDTH = 256
UNIT = 16
WIDE = 32
TILE = 1920
BACK = 640
CHUNK = 640
PARTS = TILE // CHUNK
HEAD_CHUNK = 384
SPLIT = 4
K0 = 2 * 0.7978845608028654
K1 = 8 * 0.7978845608028654 * 0.044715


def mm(a, b):
    return lax.dot_general(a, b, (((1,), (0,)), ((), ())), preferred_element_type=F32)


def mm_nt(a, b):
    return lax.dot_general(a, b, (((1,), (1,)), ((), ())), preferred_element_type=F32)


def mm_tn(a, b):
    return lax.dot_general(a, b, (((0,), (0,)), ((), ())), preferred_element_type=F32)


def norm_gelu(s, gain8, gain_slope, shift_half):
    mean = jnp.sum(s, axis=1, keepdims=True) * (1.0 / WIDTH)
    center = s - mean
    r = lax.rsqrt(jnp.sum(center * center, axis=1, keepdims=True) + WIDTH * 1e-5)
    n = center * r
    h = n * gain8 + shift_half
    y = h * h
    t = jnp.tanh(h * (K0 + K1 * y))
    e1 = 1.0 + t
    bend = (h * (y + K0 / (3 * K1))) * (1.0 - t)
    slope = e1 * (1.0 / (3 * K1) + bend)
    if gain_slope is not None:
        slope = slope * gain_slope
    return h * e1, n.astype(BF16), slope, jnp.broadcast_to(r, (s.shape[0], 128))


def scales(vec_ref, at, layers, slope):
    gain = vec_ref[pl.ds(at, 1), :]
    return gain * 8.0, gain * (8.0 * 3 * K1) if slope else None, vec_ref[pl.ds(at + layers, 1), :] * 0.5


def gained(w, columns, at):
    lane = lax.broadcasted_iota(jnp.int32, columns.shape, 1)
    gain = jnp.sum(jnp.where(lane == at, columns, 0.0), axis=1, keepdims=True)
    return (w.astype(F32) * (gain * (8.0 * 3 * K1))).astype(BF16)


def lane_sums(x):
    total = lax.reduce_sum(x[:, 0:128] + x[:, 128:256], (1,))
    return jnp.broadcast_to(total[:, None], (x.shape[0], 128))


def norm_back(da, slope, n, r):
    w = da * slope.astype(F32)
    w16 = w.astype(BF16)
    wn = w16 * n
    m1 = lane_sums(w16) * BF16(1.0 / WIDTH)
    m2 = lane_sums(wn)
    halves = [
        (w[:, k:k + 128] - (m1 + n[:, k:k + 128] * m2).astype(F32)) * r for k in (0, 128)
    ]
    return jnp.concatenate(halves, axis=1), w, wn


def rows_of(c):
    return pl.multiple_of(c * CHUNK, UNIT)


def activate(base, s_ref, save, i, scale):
    act_ref, n_ref, slope_ref, r_ref = save
    for u in range(0, CHUNK, WIDE):
        rows = pl.ds(base + u, WIDE)
        act, n, slope, r = norm_gelu(s_ref[rows, :], *scale)
        act_ref[i, rows, :] = act.astype(BF16)
        n_ref[i, rows, :] = n
        slope_ref[i, rows, :] = slope.astype(slope_ref.dtype)
        r_ref[i, rows, :] = r


def following(i, c, parts, change):
    end = c == parts - 1
    return jnp.where(end, i + change, i), jnp.where(end, 0, c + 1)


def forward_layers(first, last, layers, s_ref, save, vec_ref, w_ref, w_at, save_at, before_block=None, after_block=None):
    act_ref = save[0]

    def product(i, c):
        return mm(act_ref[i - save_at, pl.ds(rows_of(c), CHUNK), :], w_ref[i - w_at])

    def residual(i, base, out):
        bias = vec_ref[pl.ds(7 + 2 * layers + i, 1), :]
        for u in range(0, CHUNK, WIDE):
            rows = pl.ds(base + u, WIDE)
            s_ref[rows, :] = s_ref[rows, :] + (out[u:u + WIDE, :] + bias)

    def block(i, carry):
        if before_block is not None:
            before_block(i)

        def chunk(c, carry):
            old_i, old_c, base = carry
            out = product(old_i, old_c)
            activate(rows_of(c), s_ref, save, i - save_at, scales(vec_ref, 7 + i, layers, False))
            residual(old_i, pl.multiple_of(base, UNIT), out)
            return i, c, c * CHUNK

        carry = lax.fori_loop(0, PARTS, chunk, carry)
        if after_block is not None:
            after_block(i)
        return carry

    start = jnp.int32(first), jnp.int32(0), jnp.int32(TILE)
    i, c, base = lax.fori_loop(first, last, block, start)
    residual(i, pl.multiple_of(base, UNIT), product(i, c))


def column_sums(parts):
    total = parts[0]
    for part in parts[1:]:
        total = total + part
    return total.astype(F32)


GROUP = 4


def fold(x):
    return jnp.sum(x, axis=0, keepdims=True)


def backward_layers(first, last, layers, s_ref, low_ref, da_ref, save, w_ref, w_at, save_at, gw_ref, gv_ref, g_at, after_block=None, beside=None):
    act_ref, n_ref, slope_ref, r_ref = save

    def product(i, c):
        return mm_nt(low_ref[pl.ds(pl.multiple_of(c * BACK, UNIT), BACK), :], w_ref[i - w_at])

    def chunk(i, c):
        base = pl.multiple_of(c * BACK, UNIT)
        next_i, next_c = following(i, c, TILE // BACK, -1)
        next_i = jnp.maximum(next_i, first)
        next_da = product(next_i, next_c)
        gw_ref[i - g_at] += mm_tn(act_ref[i - save_at, pl.ds(base, BACK), :], low_ref[pl.ds(base, BACK), :])
        if beside is not None:
            beside(last - 1 - i, c)
        zero = jnp.zeros((WIDE, WIDTH), F32)
        shift, gain, bias = zero, zero, zero
        held = []
        for u in range(0, BACK, WIDE):
            rows = pl.ds(base + u, WIDE)
            at = (i - save_at, rows, slice(None))
            d_in, wf, wn = norm_back(da_ref[u:u + WIDE, :], slope_ref[at], n_ref[at], r_ref[at])
            shift = shift + wf
            held.append(wn)
            if len(held) == GROUP:
                gain = gain + column_sums(held)
                held = []
            ds = s_ref[rows, :]
            bias = bias + ds
            ds = ds + d_in
            s_ref[rows, :] = ds
            low_ref[rows, :] = ds.astype(BF16)
        da_ref[...] = next_da
        for k, x in enumerate((gain, shift, bias)):
            gv_ref[pl.ds(7 + k * layers + i, 1), :] += fold(x)

    def block(j, carry):
        i = last - 1 - j
        lax.fori_loop(0, TILE // BACK, lambda c, carry: chunk(i, c) or carry, 0)
        if after_block is not None:
            after_block(i)
        return carry

    da_ref[...] = product(last - 1, 0)
    lax.fori_loop(0, last - first, block, 0)


def softmax(full_ref, col_ref, top_ref, total_ref, expon_ref, dlog_ref, at, loss_ref):
    units = [slice(u, u + UNIT) for u in range(0, HEAD_CHUNK, UNIT)]
    lane = lax.broadcasted_iota(jnp.int32, (1, 128), 1).astype(F32)
    spread = lambda x: jnp.broadcast_to(x, (UNIT, 128))
    cols = [slice(k * 128, (k + 1) * 128) for k in range(6)]
    for rows in units:
        logits = [full_ref[rows, cols[k]] for k in range(6)]
        top = functools.reduce(jnp.maximum, logits[:5])
        top_ref[0, rows, :] = spread(jnp.max(top, axis=1, keepdims=True))
        top_ref[1, rows, :] = spread(jnp.max(logits[5], axis=1, keepdims=True))
    for rows in units:
        expon = [jnp.exp(full_ref[rows, cols[k]] - top_ref[k // 5, rows, :]) for k in range(6)]
        for k in range(6):
            expon_ref[rows, cols[k]] = expon[k]
        total_ref[0, rows, :] = spread(jnp.sum(functools.reduce(jnp.add, expon[:5]), axis=1, keepdims=True))
        total_ref[1, rows, :] = spread(jnp.sum(expon[5], axis=1, keepdims=True))
    loss = jnp.zeros((UNIT, 128), F32)
    for rows in units:
        _, *targets, mask = (spread(col_ref[pl.ds(at + rows.start, UNIT), k:k + 1]) for k in range(4))
        zero = jnp.zeros_like(mask)
        hits = [zero, zero]
        weights = [mask / total_ref[j, rows, :] for j in range(2)]
        for k in range(6):
            j = k // 5
            hit = lane + 128.0 * (k % 5) == targets[j]
            hits[j] = jnp.where(hit, full_ref[rows, cols[k]], hits[j])
            grad = expon_ref[rows, cols[k]] * weights[j] - jnp.where(hit, mask, zero)
            dlog_ref[pl.ds(at + rows.start, UNIT), cols[k]] = grad.astype(BF16)
        row = jnp.log(total_ref[0, rows, :]) + jnp.log(total_ref[1, rows, :]) + (top_ref[0, rows, :] + top_ref[1, rows, :])
        loss = loss + mask * (row * (1.0 / 128) - (hits[0] + hits[1]))
    loss_ref[...] += loss


def heads(
    ints_ref, s_ref, ds_ref, low_ref, wh_ref, hb_ref, latents_ref, turned_ref, dlog_ref, loss_ref, full_ref, col_ref, top_ref, total_ref,
    expon_ref,
):
    size = HEAD_CHUNK
    count = TILE // size

    def span_of(t):
        return pl.ds(pl.multiple_of(t * size, 128), size)

    def logits(t):
        lat = s_ref[span_of(t), :].astype(BF16)
        latents_ref[span_of(t), :] = lat
        return mm(lat, wh_ref[...])

    def keep(parts):
        full_ref[...] = parts + hb_ref[...].astype(F32)

    def turn(t):
        turned_ref[0:WIDTH, span_of(t)] = latents_ref[span_of(t), :].T

    def product(t):
        return mm_nt(dlog_ref[span_of(t), :], wh_ref[...])

    def store(t, ds):
        ds_ref[span_of(t), :] = ds
        low_ref[span_of(t), :] = ds.astype(BF16)

    def body(t, carry):
        before = jnp.maximum(t - 1, 0)
        following = logits(jnp.minimum(t + 1, count - 1))
        turn(before)
        ds = product(before)
        softmax(full_ref, col_ref, top_ref, total_ref, expon_ref, dlog_ref, pl.multiple_of(t * size, 128), loss_ref)
        store(before, ds)
        keep(following)
        return carry

    col_ref[...] = ints_ref[...].astype(F32).T
    keep(logits(jnp.int32(0)))
    lax.fori_loop(0, count, body, 0)
    end = jnp.int32(count - 1)
    turn(end)
    store(end, product(end))


def unpack_vec(w, vec_ref):
    vec_ref[...] = w[:, 0:128].astype(F32).T


def moves_hot(ints):
    rows = lax.broadcasted_iota(jnp.int32, (16, ints.shape[1]), 0)
    return jnp.where((rows == ints[0:1]) | (rows == 4), 1.0, 0.0).astype(BF16)


def table_of(vec_ref):
    rows = lax.broadcasted_iota(jnp.int32, (16, WIDTH), 0)
    return jnp.where(rows < 5, vec_ref[0:16, :], 0.0).astype(BF16)


def stem_forward(latent_ref, hot_ref, vec_ref, w, s_ref, n_ref, slope_ref, r_ref, pre_ref, n_at):
    table = table_of(vec_ref)
    scale = scales(vec_ref, 5, 1, True)

    def product(c):
        span = pl.ds(rows_of(c), CHUNK)
        return mm(latent_ref[span, :], w) + mm(hot_ref[span, :], table)

    def body(c, carry):
        following = product(jnp.minimum(c + 1, PARTS - 1))
        for u in range(0, CHUNK, WIDE):
            rows = pl.ds(rows_of(c) + u, WIDE)
            act, n, slope, r = norm_gelu(pre_ref[u:u + WIDE, :], *scale)
            s_ref[rows, :] = act
            n_ref[n_at, rows, :] = n
            slope_ref[n_at, rows, :] = slope.astype(slope_ref.dtype)
            r_ref[n_at, rows, :] = r
        pre_ref[...] = following
        return carry

    pre_ref[...] = product(jnp.int32(0))
    lax.fori_loop(0, PARTS, body, 0)


def stem_backward(latent_ref, hot_ref, s_ref, low_ref, n_ref, slope_ref, r_ref, n_at, d_pre_ref, gw_ref, g_at, gv_ref):
    def products(c):
        span = pl.ds(rows_of(c), CHUNK)
        low = low_ref[...]
        gw_ref[g_at] += mm_tn(latent_ref[span, :], low)
        gv_ref[0:16, :] += mm(hot_ref[:, span], low)

    def body(c, carry):
        products(jnp.maximum(c - 1, 0))
        shift = jnp.zeros((WIDE, WIDTH), F32)
        gain = shift
        held = []
        for u in range(0, CHUNK, WIDE):
            rows = pl.ds(rows_of(c) + u, WIDE)
            d_in, wf, wn = norm_back(s_ref[rows, :], slope_ref[n_at, rows, :], n_ref[n_at, rows, :], r_ref[n_at, rows, :])
            shift = shift + wf
            held.append(wn)
            if len(held) == GROUP:
                gain = gain + column_sums(held)
                held = []
            low = d_in.astype(BF16)
            low_ref[u:u + WIDE, :] = low
            d_pre_ref[rows, :] = low
        gv_ref[5:6, :] += fold(gain)
        gv_ref[6:7, :] += fold(shift)
        return carry

    low_ref[...] = jnp.zeros_like(low_ref)
    lax.fori_loop(0, PARTS, body, 0)
    products(PARTS - 1)


def clean_latent(latent_ref, lat_ref, rows_dev):
    lat_ref[...] = latent_ref[...]
    steps = -(-rows_dev // TILE)
    tail = rows_dev - (steps - 1) * TILE
    if tail < TILE:
        @pl.when(pl.program_id(0) == steps - 1)
        def _():
            lat_ref[tail:TILE, :] = jnp.zeros((TILE - tail, WIDTH), BF16)


def split_low(x):
    high = x.astype(BF16)
    return high, (x - high.astype(F32)).astype(BF16)


def join_pieces(pieces_ref, w_ref, at):
    rows = WIDTH // pieces_ref.shape[0]
    for f in range(pieces_ref.shape[0]):
        for m in range(pieces_ref.shape[1] // rows):
            w_ref[at + m, f * rows:(f + 1) * rows, :] = pieces_ref[f, m * rows:(m + 1) * rows, :]


def join_front(core_ref, front_refs, w_ref):
    if len(front_refs) == 1:
        join_pieces(front_refs[0], w_ref, 0)
    else:
        half = w_ref.shape[0] // 2
        for core in range(2):
            @pl.when(core_ref[0] == core)
            def _():
                join_pieces(front_refs[core], w_ref, 0)
                join_pieces(front_refs[1 - core], w_ref, half)


def cut_pieces(out_ref, m, matrix):
    rows = WIDTH // out_ref.shape[0]
    at = m * rows if isinstance(m, int) else pl.multiple_of(m * rows, rows)
    for f in range(out_ref.shape[0]):
        out_ref[f, pl.ds(at, rows), :] = matrix[f * rows:(f + 1) * rows, :].astype(BF16)


def cut_vectors(out_ref, at, wide):
    rows = WIDTH // out_ref.shape[0]
    half = rows // 2
    for f in range(out_ref.shape[0]):
        part = wide[f * rows:(f + 1) * rows, :]
        out_ref[f, at:at + half, :] = jnp.concatenate([part[0:half], part[half:rows]], axis=1).astype(BF16)


def copies(refs, away, sems, i, span, inward):
    out = []
    for k, (near, far) in enumerate(zip(refs, away)):
        ends = (far.at[i, span, :], near.at[i]) if inward else (near.at[i], far.at[i, span, :])
        out.append(pltpu.make_async_copy(*ends, sems.at[i, k]))
    return out


def tile_span(step):
    return pl.ds(pl.multiple_of(step * TILE, 128), TILE)


def first_kernel(layers, rows_dev, fronts, nq, nc, core_ref, latent_ref, ints_ref, *refs):
    front_refs = refs[:fronts]
    (
        n_out, slope_out, r_out, act_out, s_out_ref, vec_ref, head_ref, w_ref, lat_ref, hot_ref, pre_ref, s_ref, n_ref, slope_ref, r_ref, act_ref, sems,
    ) = refs[fronts:]
    step, steps = pl.program_id(0), pl.num_programs(0)
    span = tile_span(step)
    refs, away = (n_ref, slope_ref, r_ref, act_ref), (n_out, slope_out, r_out, act_out)

    def start(i, count=4):
        for copy in copies(refs[:count], away, sems, i, span, False):
            copy.start()

    def wait(i, count=4):
        for copy in copies(refs[:count], away, sems, i, span, False):
            copy.wait()

    @pl.when(step == 0)
    def _():
        join_front(core_ref, front_refs, w_ref)
        unpack_vec(w_ref[0], vec_ref)
        tail = w_ref[0, :, 128:256]
        lane = lax.broadcasted_iota(jnp.int32, (1, 128), 1)
        head_ref[:, 0:128] = jnp.where(lane < nq - 2 * WIDTH, tail.astype(F32), 0.0).astype(BF16)
        row = lax.broadcasted_iota(jnp.int32, (128, 128), 0)
        pick = (row == lane + (128 - nc)) & (lane < nc)
        head_ref[:, 128:256] = mm(tail, jnp.where(pick, 1.0, 0.0).astype(BF16)).astype(BF16)

    clean_latent(latent_ref, lat_ref, rows_dev)
    hot_ref[...] = moves_hot(ints_ref[...]).T

    @pl.when(step > 0)
    def _():
        wait(SPLIT, 3)

    stem_forward(lat_ref, hot_ref, vec_ref, w_ref[1], s_ref, n_ref, slope_ref, r_ref, pre_ref, SPLIT)
    start(SPLIT, 3)

    def before_block(i):
        @pl.when(step > 0)
        def _():
            wait(i)

    save = (act_ref, n_ref, slope_ref, r_ref)
    forward_layers(0, SPLIT, layers, s_ref, save, vec_ref, w_ref, -2, 0, before_block, start)
    s_out_ref[...] = s_ref[0:TILE, :]

    @pl.when(step == steps - 1)
    def _():
        wait(SPLIT, 3)
        for i in range(SPLIT):
            wait(i)


def middle_kernel(
    layers, s_in_ref, ints_ref, vec_ref, hb_ref, w_ref, head_ref, latents_ref, ds_ref, gv_ref, rep_ref, out_ref,
    wh_ref, wg_ref, s_ref, act_ref, n_ref, slope_ref, r_ref, low_ref, da_ref, turned_ref, dlog_ref, gw_ref, gh_ref, loss_ref, *chunk_refs,
):
    blocks = layers - SPLIT
    step = pl.program_id(0)

    @pl.when(step == 0)
    def _():
        for ref in (gw_ref, gh_ref, gv_ref, loss_ref):
            ref[...] = jnp.zeros_like(ref)
        turned_ref[WIDTH:, :] = jnp.ones_like(turned_ref[WIDTH:, :])
        turned_ref[0:WIDTH, TILE:] = jnp.zeros_like(turned_ref[0:WIDTH, TILE:])
        dlog_ref[TILE:, :] = jnp.zeros_like(dlog_ref[TILE:, :])
        for k in range(3):
            wh_ref[:, k * WIDTH:(k + 1) * WIDTH] = w_ref[blocks + k] if k < 2 else head_ref[...]
        columns = vec_ref[...].T

        def scale(i, carry):
            wg_ref[i] = gained(w_ref[i], columns, 7 + SPLIT + i)
            return carry

        lax.fori_loop(0, blocks, scale, 0)

    s_ref[0:TILE, :] = s_in_ref[...]
    save = (act_ref, n_ref, slope_ref, r_ref)
    forward_layers(SPLIT, layers, layers, s_ref, save, vec_ref, w_ref, SPLIT, SPLIT)
    heads(ints_ref, s_ref, ds_ref, low_ref, wh_ref, hb_ref, latents_ref, turned_ref, dlog_ref, loss_ref, *chunk_refs)

    def beside(j, k):
        rows = pl.ds(pl.multiple_of(j * HEAD_CHUNK, 128), HEAD_CHUNK)
        columns = pl.ds(pl.multiple_of(k * WIDTH, WIDTH), WIDTH)
        gh_ref[k] += mm(turned_ref[:, rows], dlog_ref[rows, columns])

    backward_layers(SPLIT, layers, layers, ds_ref, low_ref, da_ref, save, wg_ref, SPLIT, SPLIT, gw_ref, gv_ref, SPLIT, None, beside)

    @pl.when(step == pl.num_programs(0) - 1)
    def _():
        def put(m, carry):
            cut_pieces(out_ref, m, gw_ref.at[m])
            return carry

        lax.fori_loop(0, blocks, put, 0)
        for k in range(3):
            cut_pieces(out_ref, blocks + k, gh_ref.at[k])
        row = lax.broadcasted_iota(jnp.int32, (8, WIDTH), 0)
        total = jnp.where(row == 3, jnp.concatenate([fold(loss_ref[...]), jnp.zeros((1, 128), F32)], axis=1), 0.0)
        for k in range(3):
            total = jnp.where(row == k, gh_ref[k, WIDTH:WIDTH + 1, :], total)
        rep_ref[...] = total
        at = (blocks + 3) * WIDTH // out_ref.shape[0]
        high, low = split_low(total)
        for f in range(out_ref.shape[0]):
            out_ref[f, at:at + 16, :] = jnp.concatenate([high, low], axis=0)


def last_kernel(layers, rows_dev, fronts, core_ref, latent_ref, ints_ref, ds_in_ref, n_in, slope_in, r_in, act_in, gv_in_ref, *refs):
    front_refs = refs[:fronts]
    (
        d_pre_ref, out_ref, stem_ref, w_ref, lat_ref, hot_ref, ds_ref, low_ref, da_ref, chunk_ref, n_ref, slope_ref, r_ref, act_ref, gw_ref, gv_ref,
        sems,
    ) = refs[fronts:]
    step, steps = pl.program_id(0), pl.num_programs(0)
    refs, away = (n_ref, slope_ref, r_ref, act_ref), (n_in, slope_in, r_in, act_in)

    def start(i, to, count=4):
        for copy in copies(refs[:count], away, sems, i, tile_span(to), True):
            copy.start()

    def wait(i, count=4):
        for copy in copies(refs[:count], away, sems, i, tile_span(step), True):
            copy.wait()

    @pl.when(step == 0)
    def _():
        start(SPLIT - 1, 0)
        join_front(core_ref, front_refs, w_ref)
        stem_ref[...] = w_ref[1]
        columns = w_ref[0, :, 0:128].astype(F32)

        def scale(i, carry):
            w_ref[2 + i] = gained(w_ref[2 + i], columns, 7 + i)
            return carry

        lax.fori_loop(0, SPLIT, scale, 0)
        gw_ref[...] = jnp.zeros_like(gw_ref)
        gv_ref[...] = gv_in_ref[...]

    clean_latent(latent_ref, lat_ref, rows_dev)
    hot_ref[...] = moves_hot(ints_ref[...])
    ds_ref[...] = ds_in_ref[...]
    low_ref[...] = ds_in_ref[...].astype(BF16)

    def after_block(i):
        @pl.when(step < steps - 1)
        def _():
            start(i, step + 1)

        @pl.when(i > 0)
        def _():
            wait(i - 1)

    wait(SPLIT - 1)

    @pl.when(step == 0)
    def _():
        for i in reversed(range(SPLIT - 1)):
            start(i, 0)
        start(SPLIT, 0, 3)

    save = (act_ref, n_ref, slope_ref, r_ref)
    backward_layers(0, SPLIT, layers, ds_ref, low_ref, da_ref, save, w_ref, -2, 0, gw_ref, gv_ref, -1, after_block)
    wait(SPLIT, 3)
    stem_backward(lat_ref, hot_ref, ds_ref, chunk_ref, n_ref, slope_ref, r_ref, SPLIT, d_pre_ref, gw_ref, 0, gv_ref)

    @pl.when(step < steps - 1)
    def _():
        start(SPLIT, step + 1, 3)

    @pl.when(step == steps - 1)
    def _():
        for m in range(SPLIT + 1):
            cut_pieces(out_ref, m, gw_ref[m])
        high, low = split_low(jnp.concatenate([gv_ref[...], jnp.zeros((64 - gv_ref.shape[0], WIDTH), F32)], axis=0))
        wide = jnp.concatenate([high, low], axis=0).astype(F32).T
        cut_vectors(out_ref, (SPLIT + 1) * WIDTH // out_ref.shape[0], wide)


def shifted_eye(rows, columns, shift):
    row = lax.broadcasted_iota(jnp.int32, (rows, columns), 0)
    return jnp.where(row + shift == lax.broadcasted_iota(jnp.int32, (rows, columns), 1), 1.0, 0.0).astype(BF16)


def pack_kernel(
    fronts, core_ref, stem_ref, table_ref, stem_bias_ref, stem_gain_ref, stem_shift_ref, block_ref, gain_ref, shift_ref, bias_ref, value_ref, chance_ref, front_ref,
    back_ref, vec_ref,
):
    layers, shard = block_ref.shape[0], block_ref.shape[1]
    nq, nc = value_ref.shape[1], chance_ref.shape[1]
    vec_ref[...] = jnp.zeros_like(vec_ref)
    at = 0
    for ref in (table_ref, stem_bias_ref, stem_gain_ref, stem_shift_ref, gain_ref, shift_ref, bias_ref):
        rows = ref[...].astype(F32)
        rows = rows[None] if len(ref.shape) == 1 else rows
        vec_ref[at:at + rows.shape[0], 0:shard] = rows
        at += rows.shape[0]
    vectors = vec_ref[0:128, :].T[0:shard, :]
    vec_ref[...] = jnp.zeros_like(vec_ref)
    vec_ref[0:shard, 0:nq - 2 * WIDTH] = value_ref[:, 2 * WIDTH:].astype(F32)
    tail = vec_ref[0:shard, 0:128] + mm(chance_ref[...], shifted_eye(nc, 128, 128 - nc))
    vectors = jnp.concatenate([vectors, tail], axis=1).astype(BF16)
    entries = [lambda: vectors, lambda: stem_ref[...]] + [functools.partial(block_ref.__getitem__, i) for i in range(SPLIT)]
    half = len(entries) // fronts
    for core in range(fronts):
        @pl.when(core_ref[0] == core if fronts > 1 else core_ref[0] >= 0)
        def _():
            for m in range(half):
                entry = entries[core * half + m]()
                for f in range(front_ref.shape[0]):
                    front_ref[f, m * shard:(m + 1) * shard, :] = entry
    for i in range(SPLIT, layers):
        back_ref[i - SPLIT] = block_ref[i]
    at = layers - SPLIT
    for k in range(2):
        back_ref[at + k] = value_ref[:, k * WIDTH:(k + 1) * WIDTH]


def outputs_kernel(latents_ref, d_pre_ref, w_ref, head_ref, hb_ref, stem_ref, value_ref, chance_ref, lgrad_ref, turned_ref, bias_ref):
    count = turned_ref.shape[0] // WIDTH

    @pl.when(pl.program_id(0) == 0)
    def _():
        at = w_ref.shape[0] - 2
        for k in range(count):
            turned_ref[k * WIDTH:(k + 1) * WIDTH, :] = (w_ref[at + k] if k < 2 else head_ref[...]).T
        columns = jnp.broadcast_to(hb_ref[...].astype(F32), (8, count * WIDTH)).T
        bias_ref[...] = jnp.broadcast_to(columns[:, 0:1], bias_ref.shape)

    nq, nc = value_ref.shape[0], chance_ref.shape[0]
    wide = [slice(k, k + 128) for k in range(0, HEAD_CHUNK, 128)]

    def chunk(c, carry):
        span = pl.ds(pl.multiple_of(c * HEAD_CHUNK, 128), HEAD_CHUNK)
        logits = mm_nt(turned_ref[...], latents_ref[span, :])
        logits = jnp.concatenate([logits[:, x] + bias_ref[...] for x in wide], axis=1).astype(BF16)
        value_ref[:, span] = logits[0:nq]
        chance_ref[:, span] = logits[640:640 + nc]
        lgrad_ref[span, :] = mm_nt(d_pre_ref[span, :], stem_ref[...]).astype(BF16)
        return carry

    lax.fori_loop(0, TILE // HEAD_CHUNK, chunk, 0)


def total_rows(refs, rows):
    total = refs[0][rows, :].astype(F32)
    for ref in refs[1:]:
        total = total + ref[rows, :].astype(F32)
    return total


def sum_mid_kernel(in_ref, out_ref):
    refs = [in_ref.at[f] for f in range(in_ref.shape[0])]
    end = in_ref.shape[1]
    for at in range(0, end - 16, 32):
        out_ref[at:at + 32, :] = total_rows(refs, slice(at, at + 32)).astype(BF16)
    total = total_rows(refs, slice(end - 16, end))
    high, low = split_low(total[0:8] + total[8:16])
    out_ref[end - 16:end, :] = jnp.concatenate([high, low], axis=0)


def sum_end_kernel(in_ref, out_ref):
    refs = [in_ref.at[f] for f in range(in_ref.shape[0])]
    end, vec = in_ref.shape[1], WIDTH // in_ref.shape[0] // 2
    for at in range(0, end - vec, 32):
        out_ref[at:at + 32, :] = total_rows(refs, slice(at, at + 32)).astype(BF16)
    total = total_rows(refs, slice(end - vec, end))
    parts = []
    for k in (0, 128):
        parts += split_low(total[:, k:k + 64] + total[:, k + 64:k + 128])
    out_ref[end - vec:end, :] = jnp.concatenate(parts, axis=1)


def finish_kernel(count, compact, scale, stem_scale_ref, gain_ref, *refs):
    mids, ends = refs[:count], refs[count:2 * count]
    (
        loss_ref, stem_ref, table_ref, stem_bias_ref, stem_gain_ref, stem_shift_ref, block_ref, block_gain_ref, block_shift_ref,
        block_bias_ref, value_ref, value_bias_ref, chance_ref, chance_bias_ref,
    ) = refs[2 * count:]
    layers, shard, moves = block_ref.shape[0], block_ref.shape[1], table_ref.shape[0]
    nq, nc = value_ref.shape[1], chance_ref.shape[1]

    def mid_of(at, rows):
        return total_rows(mids, slice(at, at + rows)) * scale

    def end_of(at, rows):
        return total_rows(ends, slice(at, at + rows)) * scale

    for i in range(SPLIT, layers):
        block_ref[i] = mid_of((i - SPLIT) * shard, shard)
    for i in range(SPLIT):
        block_ref[i] = end_of((1 + i) * shard, shard)
    stem_ref[...] = end_of(0, shard)
    for k in range(3):
        width = min(WIDTH, nq - k * WIDTH)
        part = mid_of((layers - SPLIT + k) * shard, shard)
        value_ref[:, k * WIDTH:k * WIDTH + width] = part[:, 0:width]
    chance_ref[...] = part[:, 128:128 + nc]
    rep = mid_of((layers - SPLIT + 3) * shard, 16)
    rep = rep[0:8] + rep[8:16]
    only = lax.broadcasted_iota(jnp.int32, rep.shape, 0)
    bias = jnp.concatenate([jnp.sum(jnp.where(only == k, rep, 0.0), axis=0) for k in range(3)])
    value_bias_ref[...] = bias[0:nq]
    chance_bias_ref[...] = bias[640:640 + nc]
    loss_ref[0] = jnp.sum(rep[3:4])
    at = (1 + SPLIT) * shard
    if compact:
        small = end_of(at, shard // 2)
        small = jnp.concatenate([small[:, 0:128], small[:, 128:256]], axis=0)
    else:
        small = end_of(at, shard)[:, 0:128]
    if shard % 128:
        small = jnp.concatenate([small, jnp.zeros((128 - shard, 128), F32)], axis=0)
    small = small.T[:, 0:shard]
    small = small[0:64] + small[64:128]
    table_ref[...] = small[0:moves]
    stem_gain = stem_scale_ref[...].astype(F32)[None]
    stem_bias_ref[...] = small[moves:moves + 1]
    stem_gain_ref[...] = small[moves + 1:moves + 2] / stem_gain
    stem_shift_ref[...] = small[moves + 2:moves + 3] / (16.0 * stem_gain)
    at = moves + 3
    gain = gain_ref[...].astype(F32)
    block_gain_ref[...] = small[at:at + layers] / gain
    block_shift_ref[...] = small[at + layers:at + 2 * layers] / (16.0 * gain)
    block_bias_ref[...] = small[at + 2 * layers:at + 3 * layers]


SMEM = pl.BlockSpec(memory_space=pltpu.SMEM)
VMEM = pl.BlockSpec(memory_space=pltpu.VMEM)
ANY = pl.BlockSpec(memory_space=pl.ANY)


def params(mib):
    return pltpu.CompilerParams(vmem_limit_bytes=mib << 20)


def tiled(shape, dim):
    block = shape[:dim] + (TILE,) + shape[dim + 1:]
    return pl.BlockSpec(block, lambda i: (0,) * dim + (i,) + (0,) * (len(shape) - dim - 1))


def whole(shape):
    return pl.BlockSpec(shape, lambda i: (0,) * len(shape))


def once(shape):
    return pl.BlockSpec(shape, lambda i: (0,) * len(shape), pipeline_mode=pl.Buffered(1))


def struct(shape, dtype):
    return jax.ShapeDtypeStruct(shape, dtype)


def exchange(x, axis, size):
    return [lax.ppermute(x, axis, [(i, i ^ k) for i in range(size)]) for k in range(1, size)]


def per_device(
    latent, actions, value_bins, chance_codes, step_mask, stem_weight, action_table, stem_bias, stem_gain, stem_shift,
    block_weight, block_gain, block_shift, block_bias, value_weight, value_bias, chance_weight, chance_bias,
):
    n_dp, n_fsdp = lax.axis_size("dp"), lax.axis_size("fsdp")
    rows_dev = latent.shape[0]
    layers, shard = block_weight.shape[0], block_weight.shape[1]
    nq, nc = value_weight.shape[1], chance_weight.shape[1]
    moves = action_table.shape[0]
    steps = -(-rows_dev // TILE)
    padded = steps * TILE
    fast = shard % 16 == 0 and n_dp & (n_dp - 1) == 0

    pieces, piece_rows = (n_fsdp, shard) if fast else (1, WIDTH)
    fronts = 2 if fast and n_dp % 2 == 0 and SPLIT % 2 == 0 else 1
    core = (lax.axis_index("dp") % 2).astype(jnp.int32).reshape(1)
    n_front = (2 + SPLIT) // fronts
    front, back = pl.pallas_call(
        functools.partial(pack_kernel, fronts),
        in_specs=[SMEM] + [VMEM] * 11,
        out_specs=[VMEM] * 2,
        out_shape=[struct((pieces, n_front * shard, WIDTH), BF16), struct((layers - SPLIT + 2, shard, WIDTH), BF16)],
        scratch_shapes=[pltpu.VMEM((max(shard, 128), max(shard, 128)), F32)],
        name="pack",
    )(
        core, stem_weight, action_table, stem_bias, stem_gain, stem_shift, block_weight, block_gain, block_shift, block_bias,
        value_weight, chance_weight,
    )
    ints = jnp.pad(jnp.stack([actions, value_bins, chance_codes, step_mask]), ((0, 4), (0, padded - rows_dev)))
    none = lambda n: jnp.full((n,), -1e30, BF16)
    head_bias = jnp.concatenate([value_bias, none(640 - nq), chance_bias, none(128 - nc)])[None]
    if fast:
        w_fronts = [lax.all_to_all(front, "fsdp", 0, 0)]
        if fronts > 1:
            w_fronts[0], ints, head_bias = lax.optimization_barrier((w_fronts[0], ints, head_bias))
            w_fronts.append(lax.ppermute(w_fronts[0], "dp", [(i, i ^ 1) for i in range(n_dp)]))
    else:
        front = lax.all_gather(front.reshape(n_front, shard, WIDTH), "fsdp", axis=1, tiled=True)
        w_fronts = [front.reshape(1, n_front * WIDTH, WIDTH)]
    w_back = lax.all_gather(back, "fsdp", axis=1, tiled=True)

    ints_spec = pl.BlockSpec((8, TILE), lambda i: (0, i))
    saved = [
        struct((SPLIT + 1, padded, WIDTH), BF16),
        struct((SPLIT + 1, padded, WIDTH), BF16),
        struct((SPLIT + 1, padded, 128), F32),
        struct((SPLIT, padded, WIDTH), BF16),
    ]
    scratch = pltpu.VMEM
    kept = [scratch((x.shape[0], TILE, x.shape[2]), x.dtype) for x in saved] + [pltpu.SemaphoreType.DMA((SPLIT + 1, 4))]
    stream = struct((padded, WIDTH), F32)
    front_shape = (2 + SPLIT, WIDTH, WIDTH)
    *held, s_mid, vec, w_head = pl.pallas_call(
        functools.partial(first_kernel, layers, rows_dev, fronts, nq, nc),
        grid=(steps,),
        in_specs=[SMEM, tiled((rows_dev, WIDTH), 0), ints_spec] + [once(x.shape) for x in w_fronts],
        out_specs=[ANY] * 4 + [tiled(stream.shape, 0), whole((128, WIDTH)), whole((WIDTH, WIDTH))],
        out_shape=saved + [stream, struct((128, WIDTH), F32), struct((WIDTH, WIDTH), BF16)],
        scratch_shapes=[
            scratch(front_shape, BF16), scratch((TILE, WIDTH), BF16), scratch((TILE, 16), BF16), scratch((CHUNK, WIDTH), F32),
            scratch((TILE + CHUNK, WIDTH), F32),
        ] + kept,
        compiler_params=params(62),
        cost_estimate=pl.CostEstimate(flops=rows_dev * WIDTH * WIDTH * 200, bytes_accessed=60 << 20, transcendentals=0),
        name="first",
    )(core, latent, ints, *w_fronts)

    blocks = layers - SPLIT
    compact = piece_rows % 32 == 0 and fast
    mid_shape = (pieces, (blocks + 3) * piece_rows + 16, WIDTH)
    end_shape = (pieces, (SPLIT + 1) * piece_rows + piece_rows // 2, WIDTH)
    latents, ds_mid, gv_mid, rep, parts_mid = pl.pallas_call(
        functools.partial(middle_kernel, layers),
        grid=(steps,),
        in_specs=[tiled(stream.shape, 0), ints_spec, once(vec.shape), once(head_bias.shape), once(w_back.shape),
            once(w_head.shape)],
        out_specs=[
            tiled((rows_dev, WIDTH), 0), tiled(stream.shape, 0), whole((48, WIDTH)), whole((8, WIDTH)), whole(mid_shape),
        ],
        out_shape=[
            struct((rows_dev, WIDTH), BF16), stream, struct((48, WIDTH), F32), struct((8, WIDTH), F32), struct(mid_shape, BF16),
        ],
        scratch_shapes=[
            scratch((WIDTH, 3 * WIDTH), BF16),
            scratch((blocks, WIDTH, WIDTH), BF16),
            scratch((TILE + CHUNK, WIDTH), F32),
            scratch((blocks, TILE, WIDTH), BF16),
            scratch((blocks, TILE, WIDTH), BF16),
            scratch((blocks, TILE, WIDTH), F32),
            scratch((blocks, TILE, 128), F32),
            scratch((TILE, WIDTH), BF16),
            scratch((BACK, WIDTH), F32),
            scratch((WIDTH + 16, max(blocks * HEAD_CHUNK, TILE)), BF16),
            scratch((max(blocks * HEAD_CHUNK, TILE), 3 * WIDTH), BF16),
            scratch((blocks, WIDTH, WIDTH), F32),
            scratch((3, WIDTH + 16, WIDTH), F32),
            scratch((UNIT, 128), F32),
            scratch((HEAD_CHUNK, 3 * WIDTH), F32),
            scratch((TILE, 8), F32),
            scratch((2, HEAD_CHUNK, 128), F32),
            scratch((2, HEAD_CHUNK, 128), F32),
            scratch((HEAD_CHUNK, 3 * WIDTH), F32),
        ],
        compiler_params=params(62),
        cost_estimate=pl.CostEstimate(flops=rows_dev * WIDTH * WIDTH * 600, bytes_accessed=40 << 20, transcendentals=0),
        name="middle",
    )(s_mid, ints, vec, head_bias, w_back, w_head)

    d_pre, parts_end, w_stem = pl.pallas_call(
        functools.partial(last_kernel, layers, rows_dev, fronts),
        grid=(steps,),
        in_specs=[SMEM, tiled((rows_dev, WIDTH), 0), ints_spec, tiled(stream.shape, 0)]
        + [ANY] * 4 + [once((48, WIDTH))] + [once(x.shape) for x in w_fronts],
        out_specs=[tiled((padded, WIDTH), 0), whole(end_shape), whole((WIDTH, WIDTH))],
        out_shape=[struct((padded, WIDTH), BF16), struct(end_shape, BF16), struct((WIDTH, WIDTH), BF16)],
        scratch_shapes=[
            scratch(front_shape, BF16),
            scratch((TILE, WIDTH), BF16),
            scratch((16, TILE), BF16),
            scratch((TILE, WIDTH), F32),
            scratch((TILE, WIDTH), BF16),
            scratch((BACK, WIDTH), F32),
            scratch((CHUNK, WIDTH), BF16),
        ] + kept[:4] + [
            scratch((SPLIT + 1, WIDTH, WIDTH), F32),
            scratch((48, WIDTH), F32),
        ] + kept[4:],
        compiler_params=params(62),
        cost_estimate=pl.CostEstimate(flops=rows_dev * WIDTH * WIDTH * 150, bytes_accessed=60 << 20, transcendentals=0),
        name="last",
    )(core, latent, ints, ds_mid, *held, gv_mid, *w_fronts)

    def outputs_of(states):
        return pl.pallas_call(
            outputs_kernel,
            grid=(steps,),
            in_specs=[tiled((rows_dev, WIDTH), 0), tiled((padded, WIDTH), 0)]
            + [once(x.shape) for x in (w_back, w_head, head_bias, w_stem)],
            out_specs=[tiled((nq, rows_dev), 1), tiled((nc, rows_dev), 1), tiled((rows_dev, WIDTH), 0)],
            out_shape=[struct((nq, rows_dev), BF16), struct((nc, rows_dev), BF16), struct((rows_dev, WIDTH), BF16)],
            scratch_shapes=[scratch((3 * WIDTH, WIDTH), BF16), scratch((3 * WIDTH, 128), F32)],
            compiler_params=params(48),
            cost_estimate=pl.CostEstimate(flops=rows_dev * WIDTH * WIDTH * 20, bytes_accessed=16 << 20, transcendentals=0),
            name="outputs",
        )(states, d_pre, w_back, w_head, head_bias, w_stem)

    if fast:
        got_mid = lax.all_to_all(parts_mid, "fsdp", 0, 0)
        parts_end, got_mid, states = lax.optimization_barrier((parts_end, got_mid, latents))
        got_end = lax.all_to_all(parts_end, "fsdp", 0, 0)
        outputs = outputs_of(states)
        got_end, outputs = lax.optimization_barrier((got_end, outputs))

        def add(body, got, name):
            return pl.pallas_call(
                body, in_specs=[VMEM], out_specs=VMEM, out_shape=struct(got.shape[1:], BF16), name=name,
            )(got)

        mine_mid, mine_end = add(sum_mid_kernel, got_mid, "sum_mid"), add(sum_end_kernel, got_end, "sum_end")
        mids = [mine_mid] + exchange(mine_mid, "dp", n_dp)
        ends = [mine_end] + exchange(mine_end, "dp", n_dp)
    else:
        outputs = outputs_of(latents)

        def scatter(x, count):
            x = x[0, :count * WIDTH].reshape(count, WIDTH, WIDTH)
            x = lax.psum_scatter(x, "fsdp", scatter_dimension=1, tiled=True).astype(F32)
            return lax.psum(x, "dp").reshape(count * shard, WIDTH)

        rep = lax.psum(rep, ("dp", "fsdp"))
        vectors = parts_end[0, (SPLIT + 1) * WIDTH:]
        vectors = jnp.concatenate([vectors[:, 0:128], vectors[:, 128:256]], axis=0)
        vectors = jnp.concatenate([vectors, jnp.zeros_like(vectors)], axis=1)
        parts_end = jnp.concatenate([parts_end[:, :(SPLIT + 1) * WIDTH], vectors[None]], axis=1)
        mids = [jnp.concatenate([scatter(parts_mid, blocks + 3), rep, jnp.zeros((8, WIDTH), F32)])]
        ends = [scatter(parts_end, SPLIT + 2)]

    value_logits, chance_logits, latent_grad = outputs
    shapes = [
        (1,), (shard, WIDTH), (moves, shard), (1, shard), (1, shard), (1, shard), (layers, shard, WIDTH), (layers, shard),
        (layers, shard), (layers, shard), (shard, nq), (nq,), (shard, nc), (nc,),
    ]
    (
        loss, stem_grad, table_grad, stem_bias_grad, stem_gain_grad, stem_shift_grad, block_grad, gain_grad, shift_grad, bias_grad,
        value_grad, value_bias_grad, chance_grad, chance_bias_grad,
    ) = pl.pallas_call(
        functools.partial(finish_kernel, len(mids), compact, 1.0 / (rows_dev * n_dp * n_fsdp)),
        in_specs=[VMEM] * (2 + 2 * len(mids)),
        out_specs=[SMEM] + [VMEM] * (len(shapes) - 1),
        out_shape=[struct(x, F32) for x in shapes],
        name="finish",
    )(stem_gain, block_gain, *mids, *ends)
    return (
        latents,
        value_logits.T,
        chance_logits.T,
        loss.reshape(()),
        latent_grad,
        stem_grad,
        table_grad,
        stem_bias_grad.reshape(shard),
        stem_gain_grad.reshape(shard),
        stem_shift_grad.reshape(shard),
        block_grad,
        gain_grad,
        shift_grad,
        bias_grad,
        value_grad,
        value_bias_grad,
        chance_grad,
        chance_bias_grad,
    )


def solution(mesh):
    placed = (
        P(("dp", "fsdp"), None),
        P(("dp", "fsdp")),
        P(("dp", "fsdp")),
        P(("dp", "fsdp")),
        P(("dp", "fsdp")),
        P("fsdp", None),
        P(None, "fsdp"),
        P("fsdp"),
        P("fsdp"),
        P("fsdp"),
        P(None, "fsdp", None),
        P(None, "fsdp"),
        P(None, "fsdp"),
        P(None, "fsdp"),
        P("fsdp", None),
        P(),
        P("fsdp", None),
        P(),
    )
    return jax.shard_map(
        per_device,
        mesh=mesh,
        in_specs=placed,
        out_specs=(
            P(("dp", "fsdp"), None),
            P(("dp", "fsdp"), None),
            P(("dp", "fsdp"), None),
            P(),
            P(("dp", "fsdp"), None),
            P("fsdp", None),
            P(None, "fsdp"),
            P("fsdp"),
            P("fsdp"),
            P("fsdp"),
            P(None, "fsdp", None),
            P(None, "fsdp"),
            P(None, "fsdp"),
            P(None, "fsdp"),
            P("fsdp", None),
            P(),
            P("fsdp", None),
            P(),
        ),
        check_vma=False,
    )
```

```python
import functools
import jax
import jax.numpy as jnp
from jax import lax
from jax.experimental import pallas as pl
from jax.experimental.pallas import tpu as pltpu
from jax.sharding import PartitionSpec as P

F32 = jnp.float32
BF16 = jnp.bfloat16
WIDTH = 256
UNIT = 16
WIDE = 32
TILE = 1920
BACK = 640
CHUNK = 640
PARTS = TILE // CHUNK
HEAD_CHUNK = 384
SPLIT = 4
K0 = 2 * 0.7978845608028654
K1 = 8 * 0.7978845608028654 * 0.044715


def mm(a, b):
    return lax.dot_general(a, b, (((1,), (0,)), ((), ())), preferred_element_type=F32)


def mm_nt(a, b):
    return lax.dot_general(a, b, (((1,), (1,)), ((), ())), preferred_element_type=F32)


def mm_tn(a, b):
    return lax.dot_general(a, b, (((0,), (0,)), ((), ())), preferred_element_type=F32)


def norm_gelu(s, gain8, gain_slope, shift_half):
    mean = jnp.sum(s, axis=1, keepdims=True) * (1.0 / WIDTH)
    center = s - mean
    r = lax.rsqrt(jnp.sum(center * center, axis=1, keepdims=True) + WIDTH * 1e-5)
    n = center * r
    h = n * gain8 + shift_half
    y = h * h
    t = jnp.tanh(h * (K0 + K1 * y))
    e1 = 1.0 + t
    bend = (h * (y + K0 / (3 * K1))) * (1.0 - t)
    slope = e1 * (1.0 / (3 * K1) + bend)
    if gain_slope is not None:
        slope = slope * gain_slope
    return h * e1, n.astype(BF16), slope, jnp.broadcast_to(r, (s.shape[0], 128))


def scales(vec_ref, at, layers, slope):
    gain = vec_ref[pl.ds(at, 1), :]
    return gain * 8.0, gain * (8.0 * 3 * K1) if slope else None, vec_ref[pl.ds(at + layers, 1), :] * 0.5


def gained(w, columns, at):
    lane = lax.broadcasted_iota(jnp.int32, columns.shape, 1)
    gain = jnp.sum(jnp.where(lane == at, columns, 0.0), axis=1, keepdims=True)
    return (w.astype(F32) * (gain * (8.0 * 3 * K1))).astype(BF16)


def lane_sums(x):
    total = lax.reduce_sum(x[:, 0:128] + x[:, 128:256], (1,))
    return jnp.broadcast_to(total[:, None], (x.shape[0], 128))


def norm_back(da, slope, n, r):
    w = da * slope.astype(F32)
    w16 = w.astype(BF16)
    wn = w16 * n
    m1 = lane_sums(w16) * BF16(1.0 / WIDTH)
    m2 = lane_sums(wn)
    halves = [
        (w[:, k:k + 128] - (m1 + n[:, k:k + 128] * m2).astype(F32)) * r for k in (0, 128)
    ]
    return jnp.concatenate(halves, axis=1), w, wn


def rows_of(c):
    return pl.multiple_of(c * CHUNK, UNIT)


def activate(base, s_ref, save, i, scale):
    act_ref, n_ref, slope_ref, r_ref = save
    for u in range(0, CHUNK, WIDE):
        rows = pl.ds(base + u, WIDE)
        act, n, slope, r = norm_gelu(s_ref[rows, :], *scale)
        act_ref[i, rows, :] = act.astype(BF16)
        n_ref[i, rows, :] = n
        slope_ref[i, rows, :] = slope.astype(slope_ref.dtype)
        r_ref[i, rows, :] = r


def following(i, c, parts, change):
    end = c == parts - 1
    return jnp.where(end, i + change, i), jnp.where(end, 0, c + 1)


def forward_layers(first, last, layers, s_ref, save, vec_ref, w_ref, w_at, save_at, before_block=None, after_block=None):
    act_ref = save[0]

    def product(i, c):
        return mm(act_ref[i - save_at, pl.ds(rows_of(c), CHUNK), :], w_ref[i - w_at])

    def residual(i, base, out):
        bias = vec_ref[pl.ds(7 + 2 * layers + i, 1), :]
        for u in range(0, CHUNK, WIDE):
            rows = pl.ds(base + u, WIDE)
            s_ref[rows, :] = s_ref[rows, :] + (out[u:u + WIDE, :] + bias)

    def block(i, carry):
        if before_block is not None:
            before_block(i)

        def chunk(c, carry):
            old_i, old_c, base = carry
            out = product(old_i, old_c)
            activate(rows_of(c), s_ref, save, i - save_at, scales(vec_ref, 7 + i, layers, False))
            residual(old_i, pl.multiple_of(base, UNIT), out)
            return i, c, c * CHUNK

        carry = lax.fori_loop(0, PARTS, chunk, carry)
        if after_block is not None:
            after_block(i)
        return carry

    start = jnp.int32(first), jnp.int32(0), jnp.int32(TILE)
    i, c, base = lax.fori_loop(first, last, block, start)
    residual(i, pl.multiple_of(base, UNIT), product(i, c))


def column_sums(parts):
    total = parts[0]
    for part in parts[1:]:
        total = total + part
    return total.astype(F32)


GROUP = 4


def fold(x):
    return jnp.sum(x, axis=0, keepdims=True)


def backward_layers(first, last, layers, s_ref, low_ref, da_ref, save, w_ref, w_at, save_at, gw_ref, gv_ref, g_at, after_block=None, beside=None):
    act_ref, n_ref, slope_ref, r_ref = save

    def product(i, c):
        return mm_nt(low_ref[pl.ds(pl.multiple_of(c * BACK, UNIT), BACK), :], w_ref[i - w_at])

    def chunk(i, c):
        base = pl.multiple_of(c * BACK, UNIT)
        next_i, next_c = following(i, c, TILE // BACK, -1)
        next_i = jnp.maximum(next_i, first)
        next_da = product(next_i, next_c)
        gw_ref[i - g_at] += mm_tn(act_ref[i - save_at, pl.ds(base, BACK), :], low_ref[pl.ds(base, BACK), :])
        if beside is not None:
            beside(last - 1 - i, c)
        zero = jnp.zeros((WIDE, WIDTH), F32)
        shift, gain, bias = zero, zero, zero
        held = []
        for u in range(0, BACK, WIDE):
            rows = pl.ds(base + u, WIDE)
            at = (i - save_at, rows, slice(None))
            d_in, wf, wn = norm_back(da_ref[u:u + WIDE, :], slope_ref[at], n_ref[at], r_ref[at])
            shift = shift + wf
            held.append(wn)
            if len(held) == GROUP:
                gain = gain + column_sums(held)
                held = []
            ds = s_ref[rows, :]
            bias = bias + ds
            ds = ds + d_in
            s_ref[rows, :] = ds
            low_ref[rows, :] = ds.astype(BF16)
        da_ref[...] = next_da
        for k, x in enumerate((gain, shift, bias)):
            gv_ref[pl.ds(7 + k * layers + i, 1), :] += fold(x)

    def block(j, carry):
        i = last - 1 - j
        lax.fori_loop(0, TILE // BACK, lambda c, carry: chunk(i, c) or carry, 0)
        if after_block is not None:
            after_block(i)
        return carry

    da_ref[...] = product(last - 1, 0)
    lax.fori_loop(0, last - first, block, 0)


def softmax(full_ref, col_ref, top_ref, total_ref, expon_ref, dlog_ref, at, loss_ref):
    units = [slice(u, u + UNIT) for u in range(0, HEAD_CHUNK, UNIT)]
    lane = lax.broadcasted_iota(jnp.int32, (1, 128), 1).astype(F32)
    spread = lambda x: jnp.broadcast_to(x, (UNIT, 128))
    cols = [slice(k * 128, (k + 1) * 128) for k in range(6)]
    for rows in units:
        logits = [full_ref[rows, cols[k]] for k in range(6)]
        top = functools.reduce(jnp.maximum, logits[:5])
        top_ref[0, rows, :] = spread(jnp.max(top, axis=1, keepdims=True))
        top_ref[1, rows, :] = spread(jnp.max(logits[5], axis=1, keepdims=True))
    for rows in units:
        expon = [jnp.exp(full_ref[rows, cols[k]] - top_ref[k // 5, rows, :]) for k in range(6)]
        for k in range(6):
            expon_ref[rows, cols[k]] = expon[k]
        total_ref[0, rows, :] = spread(jnp.sum(functools.reduce(jnp.add, expon[:5]), axis=1, keepdims=True))
        total_ref[1, rows, :] = spread(jnp.sum(expon[5], axis=1, keepdims=True))
    loss = jnp.zeros((UNIT, 128), F32)
    for rows in units:
        _, *targets, mask = (spread(col_ref[pl.ds(at + rows.start, UNIT), k:k + 1]) for k in range(4))
        zero = jnp.zeros_like(mask)
        hits = [zero, zero]
        weights = [mask / total_ref[j, rows, :] for j in range(2)]
        for k in range(6):
            j = k // 5
            hit = lane + 128.0 * (k % 5) == targets[j]
            hits[j] = jnp.where(hit, full_ref[rows, cols[k]], hits[j])
            grad = expon_ref[rows, cols[k]] * weights[j] - jnp.where(hit, mask, zero)
            dlog_ref[pl.ds(at + rows.start, UNIT), cols[k]] = grad.astype(BF16)
        row = jnp.log(total_ref[0, rows, :]) + jnp.log(total_ref[1, rows, :]) + (top_ref[0, rows, :] + top_ref[1, rows, :])
        loss = loss + mask * (row * (1.0 / 128) - (hits[0] + hits[1]))
    loss_ref[...] += loss


def heads(
    ints_ref, s_ref, ds_ref, low_ref, wh_ref, hb_ref, latents_ref, turned_ref, dlog_ref, loss_ref, full_ref, col_ref, top_ref, total_ref,
    expon_ref,
):
    size = HEAD_CHUNK
    count = TILE // size

    def span_of(t):
        return pl.ds(pl.multiple_of(t * size, 128), size)

    def logits(t):
        lat = s_ref[span_of(t), :].astype(BF16)
        latents_ref[span_of(t), :] = lat
        return mm(lat, wh_ref[...])

    def keep(parts):
        full_ref[...] = parts + hb_ref[...].astype(F32)

    def turn(t):
        turned_ref[0:WIDTH, span_of(t)] = latents_ref[span_of(t), :].T

    def product(t):
        return mm_nt(dlog_ref[span_of(t), :], wh_ref[...])

    def store(t, ds):
        ds_ref[span_of(t), :] = ds
        low_ref[span_of(t), :] = ds.astype(BF16)

    def body(t, carry):
        before = jnp.maximum(t - 1, 0)
        following = logits(jnp.minimum(t + 1, count - 1))
        turn(before)
        ds = product(before)
        softmax(full_ref, col_ref, top_ref, total_ref, expon_ref, dlog_ref, pl.multiple_of(t * size, 128), loss_ref)
        store(before, ds)
        keep(following)
        return carry

    col_ref[...] = ints_ref[...].astype(F32).T
    keep(logits(jnp.int32(0)))
    lax.fori_loop(0, count, body, 0)
    end = jnp.int32(count - 1)
    turn(end)
    store(end, product(end))


def unpack_vec(w, vec_ref):
    vec_ref[...] = w[:, 0:128].astype(F32).T


def moves_hot(ints):
    rows = lax.broadcasted_iota(jnp.int32, (16, ints.shape[1]), 0)
    return jnp.where((rows == ints[0:1]) | (rows == 4), 1.0, 0.0).astype(BF16)


def table_of(vec_ref):
    rows = lax.broadcasted_iota(jnp.int32, (16, WIDTH), 0)
    return jnp.where(rows < 5, vec_ref[0:16, :], 0.0).astype(BF16)


def stem_forward(latent_ref, hot_ref, vec_ref, w, s_ref, n_ref, slope_ref, r_ref, pre_ref, n_at):
    table = table_of(vec_ref)
    scale = scales(vec_ref, 5, 1, True)

    def product(c):
        span = pl.ds(rows_of(c), CHUNK)
        return mm(latent_ref[span, :], w) + mm(hot_ref[span, :], table)

    def body(c, carry):
        following = product(jnp.minimum(c + 1, PARTS - 1))
        for u in range(0, CHUNK, WIDE):
            rows = pl.ds(rows_of(c) + u, WIDE)
            act, n, slope, r = norm_gelu(pre_ref[u:u + WIDE, :], *scale)
            s_ref[rows, :] = act
            n_ref[n_at, rows, :] = n
            slope_ref[n_at, rows, :] = slope.astype(slope_ref.dtype)
            r_ref[n_at, rows, :] = r
        pre_ref[...] = following
        return carry

    pre_ref[...] = product(jnp.int32(0))
    lax.fori_loop(0, PARTS, body, 0)


def stem_backward(latent_ref, hot_ref, s_ref, low_ref, n_ref, slope_ref, r_ref, n_at, d_pre_ref, gw_ref, g_at, gv_ref):
    def products(c):
        span = pl.ds(rows_of(c), CHUNK)
        low = low_ref[...]
        gw_ref[g_at] += mm_tn(latent_ref[span, :], low)
        gv_ref[0:16, :] += mm(hot_ref[:, span], low)

    def body(c, carry):
        products(jnp.maximum(c - 1, 0))
        shift = jnp.zeros((WIDE, WIDTH), F32)
        gain = shift
        held = []
        for u in range(0, CHUNK, WIDE):
            rows = pl.ds(rows_of(c) + u, WIDE)
            d_in, wf, wn = norm_back(s_ref[rows, :], slope_ref[n_at, rows, :], n_ref[n_at, rows, :], r_ref[n_at, rows, :])
            shift = shift + wf
            held.append(wn)
            if len(held) == GROUP:
                gain = gain + column_sums(held)
                held = []
            low = d_in.astype(BF16)
            low_ref[u:u + WIDE, :] = low
            d_pre_ref[rows, :] = low
        gv_ref[5:6, :] += fold(gain)
        gv_ref[6:7, :] += fold(shift)
        return carry

    low_ref[...] = jnp.zeros_like(low_ref)
    lax.fori_loop(0, PARTS, body, 0)
    products(PARTS - 1)


def clean_latent(latent_ref, lat_ref, rows_dev):
    lat_ref[...] = latent_ref[...]
    steps = -(-rows_dev // TILE)
    tail = rows_dev - (steps - 1) * TILE
    if tail < TILE:
        @pl.when(pl.program_id(0) == steps - 1)
        def _():
            lat_ref[tail:TILE, :] = jnp.zeros((TILE - tail, WIDTH), BF16)


def split_low(x):
    high = x.astype(BF16)
    return high, (x - high.astype(F32)).astype(BF16)


def join_pieces(pieces_ref, w_ref, at):
    rows = WIDTH // pieces_ref.shape[0]
    for f in range(pieces_ref.shape[0]):
        for m in range(pieces_ref.shape[1] // rows):
            w_ref[at + m, f * rows:(f + 1) * rows, :] = pieces_ref[f, m * rows:(m + 1) * rows, :]


def join_front(core_ref, front_refs, w_ref):
    if len(front_refs) == 1:
        join_pieces(front_refs[0], w_ref, 0)
    else:
        half = w_ref.shape[0] // 2
        for core in range(2):
            @pl.when(core_ref[0] == core)
            def _():
                join_pieces(front_refs[core], w_ref, 0)
                join_pieces(front_refs[1 - core], w_ref, half)


def cut_pieces(out_ref, m, matrix):
    rows = WIDTH // out_ref.shape[0]
    at = m * rows if isinstance(m, int) else pl.multiple_of(m * rows, rows)
    for f in range(out_ref.shape[0]):
        out_ref[f, pl.ds(at, rows), :] = matrix[f * rows:(f + 1) * rows, :].astype(BF16)


def cut_vectors(out_ref, at, wide):
    rows = WIDTH // out_ref.shape[0]
    half = rows // 2
    for f in range(out_ref.shape[0]):
        part = wide[f * rows:(f + 1) * rows, :]
        out_ref[f, at:at + half, :] = jnp.concatenate([part[0:half], part[half:rows]], axis=1).astype(BF16)


def copies(refs, away, sems, i, span, inward):
    out = []
    for k, (near, far) in enumerate(zip(refs, away)):
        ends = (far.at[i, span, :], near.at[i]) if inward else (near.at[i], far.at[i, span, :])
        out.append(pltpu.make_async_copy(*ends, sems.at[i, k]))
    return out


def tile_span(step):
    return pl.ds(pl.multiple_of(step * TILE, 128), TILE)


def first_kernel(layers, rows_dev, fronts, nq, nc, core_ref, latent_ref, ints_ref, *refs):
    front_refs = refs[:fronts]
    (
        n_out, slope_out, r_out, act_out, s_out_ref, vec_ref, head_ref, w_ref, lat_ref, hot_ref, pre_ref, s_ref, n_ref, slope_ref, r_ref, act_ref, sems,
    ) = refs[fronts:]
    step, steps = pl.program_id(0), pl.num_programs(0)
    span = tile_span(step)
    refs, away = (n_ref, slope_ref, r_ref, act_ref), (n_out, slope_out, r_out, act_out)

    def start(i, count=4):
        for copy in copies(refs[:count], away, sems, i, span, False):
            copy.start()

    def wait(i, count=4):
        for copy in copies(refs[:count], away, sems, i, span, False):
            copy.wait()

    @pl.when(step == 0)
    def _():
        join_front(core_ref, front_refs, w_ref)
        unpack_vec(w_ref[0], vec_ref)
        tail = w_ref[0, :, 128:256]
        lane = lax.broadcasted_iota(jnp.int32, (1, 128), 1)
        head_ref[:, 0:128] = jnp.where(lane < nq - 2 * WIDTH, tail.astype(F32), 0.0).astype(BF16)
        row = lax.broadcasted_iota(jnp.int32, (128, 128), 0)
        pick = (row == lane + (128 - nc)) & (lane < nc)
        head_ref[:, 128:256] = mm(tail, jnp.where(pick, 1.0, 0.0).astype(BF16)).astype(BF16)

    clean_latent(latent_ref, lat_ref, rows_dev)
    hot_ref[...] = moves_hot(ints_ref[...]).T

    @pl.when(step > 0)
    def _():
        wait(SPLIT, 3)

    stem_forward(lat_ref, hot_ref, vec_ref, w_ref[1], s_ref, n_ref, slope_ref, r_ref, pre_ref, SPLIT)
    start(SPLIT, 3)

    def before_block(i):
        @pl.when(step > 0)
        def _():
            wait(i)

    save = (act_ref, n_ref, slope_ref, r_ref)
    forward_layers(0, SPLIT, layers, s_ref, save, vec_ref, w_ref, -2, 0, before_block, start)
    s_out_ref[...] = s_ref[0:TILE, :]

    @pl.when(step == steps - 1)
    def _():
        wait(SPLIT, 3)
        for i in range(SPLIT):
            wait(i)


def middle_kernel(
    layers, s_in_ref, ints_ref, vec_ref, hb_ref, w_ref, head_ref, latents_ref, ds_ref, gv_ref, rep_ref, out_ref,
    wh_ref, wg_ref, s_ref, act_ref, n_ref, slope_ref, r_ref, low_ref, da_ref, turned_ref, dlog_ref, gw_ref, gh_ref, loss_ref, *chunk_refs,
):
    blocks = layers - SPLIT
    step = pl.program_id(0)

    @pl.when(step == 0)
    def _():
        for ref in (gw_ref, gh_ref, gv_ref, loss_ref):
            ref[...] = jnp.zeros_like(ref)
        turned_ref[WIDTH:, :] = jnp.ones_like(turned_ref[WIDTH:, :])
        turned_ref[0:WIDTH, TILE:] = jnp.zeros_like(turned_ref[0:WIDTH, TILE:])
        dlog_ref[TILE:, :] = jnp.zeros_like(dlog_ref[TILE:, :])
        for k in range(3):
            wh_ref[:, k * WIDTH:(k + 1) * WIDTH] = w_ref[blocks + k] if k < 2 else head_ref[...]
        columns = vec_ref[...].T

        def scale(i, carry):
            wg_ref[i] = gained(w_ref[i], columns, 7 + SPLIT + i)
            return carry

        lax.fori_loop(0, blocks, scale, 0)

    s_ref[0:TILE, :] = s_in_ref[...]
    save = (act_ref, n_ref, slope_ref, r_ref)
    forward_layers(SPLIT, layers, layers, s_ref, save, vec_ref, w_ref, SPLIT, SPLIT)
    heads(ints_ref, s_ref, ds_ref, low_ref, wh_ref, hb_ref, latents_ref, turned_ref, dlog_ref, loss_ref, *chunk_refs)

    def beside(j, k):
        rows = pl.ds(pl.multiple_of(j * HEAD_CHUNK, 128), HEAD_CHUNK)
        columns = pl.ds(pl.multiple_of(k * WIDTH, WIDTH), WIDTH)
        gh_ref[k] += mm(turned_ref[:, rows], dlog_ref[rows, columns])

    backward_layers(SPLIT, layers, layers, ds_ref, low_ref, da_ref, save, wg_ref, SPLIT, SPLIT, gw_ref, gv_ref, SPLIT, None, beside)

    @pl.when(step == pl.num_programs(0) - 1)
    def _():
        def put(m, carry):
            cut_pieces(out_ref, m, gw_ref.at[m])
            return carry

        lax.fori_loop(0, blocks, put, 0)
        for k in range(3):
            cut_pieces(out_ref, blocks + k, gh_ref.at[k])
        row = lax.broadcasted_iota(jnp.int32, (8, WIDTH), 0)
        total = jnp.where(row == 3, jnp.concatenate([fold(loss_ref[...]), jnp.zeros((1, 128), F32)], axis=1), 0.0)
        for k in range(3):
            total = jnp.where(row == k, gh_ref[k, WIDTH:WIDTH + 1, :], total)
        rep_ref[...] = total
        at = (blocks + 3) * WIDTH // out_ref.shape[0]
        high, low = split_low(total)
        for f in range(out_ref.shape[0]):
            out_ref[f, at:at + 16, :] = jnp.concatenate([high, low], axis=0)


def last_kernel(layers, rows_dev, fronts, core_ref, latent_ref, ints_ref, ds_in_ref, n_in, slope_in, r_in, act_in, gv_in_ref, *refs):
    front_refs = refs[:fronts]
    (
        d_pre_ref, out_ref, stem_ref, w_ref, lat_ref, hot_ref, ds_ref, low_ref, da_ref, chunk_ref, n_ref, slope_ref, r_ref, act_ref, gw_ref, gv_ref,
        sems,
    ) = refs[fronts:]
    step, steps = pl.program_id(0), pl.num_programs(0)
    refs, away = (n_ref, slope_ref, r_ref, act_ref), (n_in, slope_in, r_in, act_in)

    def start(i, to, count=4):
        for copy in copies(refs[:count], away, sems, i, tile_span(to), True):
            copy.start()

    def wait(i, count=4):
        for copy in copies(refs[:count], away, sems, i, tile_span(step), True):
            copy.wait()

    @pl.when(step == 0)
    def _():
        start(SPLIT - 1, 0)
        join_front(core_ref, front_refs, w_ref)
        stem_ref[...] = w_ref[1]
        columns = w_ref[0, :, 0:128].astype(F32)

        def scale(i, carry):
            w_ref[2 + i] = gained(w_ref[2 + i], columns, 7 + i)
            return carry

        lax.fori_loop(0, SPLIT, scale, 0)
        gw_ref[...] = jnp.zeros_like(gw_ref)
        gv_ref[...] = gv_in_ref[...]

    clean_latent(latent_ref, lat_ref, rows_dev)
    hot_ref[...] = moves_hot(ints_ref[...])
    ds_ref[...] = ds_in_ref[...]
    low_ref[...] = ds_in_ref[...].astype(BF16)

    def after_block(i):
        @pl.when(step < steps - 1)
        def _():
            start(i, step + 1)

        @pl.when(i > 0)
        def _():
            wait(i - 1)

    wait(SPLIT - 1)

    @pl.when(step == 0)
    def _():
        for i in reversed(range(SPLIT - 1)):
            start(i, 0)
        start(SPLIT, 0, 3)

    save = (act_ref, n_ref, slope_ref, r_ref)
    backward_layers(0, SPLIT, layers, ds_ref, low_ref, da_ref, save, w_ref, -2, 0, gw_ref, gv_ref, -1, after_block)
    wait(SPLIT, 3)
    stem_backward(lat_ref, hot_ref, ds_ref, chunk_ref, n_ref, slope_ref, r_ref, SPLIT, d_pre_ref, gw_ref, 0, gv_ref)

    @pl.when(step < steps - 1)
    def _():
        start(SPLIT, step + 1, 3)

    @pl.when(step == steps - 1)
    def _():
        for m in range(SPLIT + 1):
            cut_pieces(out_ref, m, gw_ref[m])
        high, low = split_low(jnp.concatenate([gv_ref[...], jnp.zeros((64 - gv_ref.shape[0], WIDTH), F32)], axis=0))
        wide = jnp.concatenate([high, low], axis=0).astype(F32).T
        cut_vectors(out_ref, (SPLIT + 1) * WIDTH // out_ref.shape[0], wide)


def shifted_eye(rows, columns, shift):
    row = lax.broadcasted_iota(jnp.int32, (rows, columns), 0)
    return jnp.where(row + shift == lax.broadcasted_iota(jnp.int32, (rows, columns), 1), 1.0, 0.0).astype(BF16)


def pack_kernel(
    fronts, core_ref, stem_ref, table_ref, stem_bias_ref, stem_gain_ref, stem_shift_ref, block_ref, gain_ref, shift_ref, bias_ref, value_ref, chance_ref, front_ref,
    back_ref, vec_ref,
):
    layers, shard = block_ref.shape[0], block_ref.shape[1]
    nq, nc = value_ref.shape[1], chance_ref.shape[1]
    vec_ref[...] = jnp.zeros_like(vec_ref)
    at = 0
    for ref in (table_ref, stem_bias_ref, stem_gain_ref, stem_shift_ref, gain_ref, shift_ref, bias_ref):
        rows = ref[...].astype(F32)
        rows = rows[None] if len(ref.shape) == 1 else rows
        vec_ref[at:at + rows.shape[0], 0:shard] = rows
        at += rows.shape[0]
    vectors = vec_ref[0:128, :].T[0:shard, :]
    vec_ref[...] = jnp.zeros_like(vec_ref)
    vec_ref[0:shard, 0:nq - 2 * WIDTH] = value_ref[:, 2 * WIDTH:].astype(F32)
    tail = vec_ref[0:shard, 0:128] + mm(chance_ref[...], shifted_eye(nc, 128, 128 - nc))
    vectors = jnp.concatenate([vectors, tail], axis=1).astype(BF16)
    entries = [lambda: vectors, lambda: stem_ref[...]] + [functools.partial(block_ref.__getitem__, i) for i in range(SPLIT)]
    half = len(entries) // fronts
    for core in range(fronts):
        @pl.when(core_ref[0] == core if fronts > 1 else core_ref[0] >= 0)
        def _():
            for m in range(half):
                entry = entries[core * half + m]()
                for f in range(front_ref.shape[0]):
                    front_ref[f, m * shard:(m + 1) * shard, :] = entry
    for i in range(SPLIT, layers):
        back_ref[i - SPLIT] = block_ref[i]
    at = layers - SPLIT
    for k in range(2):
        back_ref[at + k] = value_ref[:, k * WIDTH:(k + 1) * WIDTH]


def outputs_kernel(latents_ref, d_pre_ref, w_ref, head_ref, hb_ref, stem_ref, value_ref, chance_ref, lgrad_ref, turned_ref, bias_ref):
    count = turned_ref.shape[0] // WIDTH

    @pl.when(pl.program_id(0) == 0)
    def _():
        at = w_ref.shape[0] - 2
        for k in range(count):
            turned_ref[k * WIDTH:(k + 1) * WIDTH, :] = (w_ref[at + k] if k < 2 else head_ref[...]).T
        columns = jnp.broadcast_to(hb_ref[...].astype(F32), (8, count * WIDTH)).T
        bias_ref[...] = jnp.broadcast_to(columns[:, 0:1], bias_ref.shape)

    nq, nc = value_ref.shape[0], chance_ref.shape[0]
    wide = [slice(k, k + 128) for k in range(0, HEAD_CHUNK, 128)]

    def chunk(c, carry):
        span = pl.ds(pl.multiple_of(c * HEAD_CHUNK, 128), HEAD_CHUNK)
        logits = mm_nt(turned_ref[...], latents_ref[span, :])
        logits = jnp.concatenate([logits[:, x] + bias_ref[...] for x in wide], axis=1).astype(BF16)
        value_ref[:, span] = logits[0:nq]
        chance_ref[:, span] = logits[640:640 + nc]
        lgrad_ref[span, :] = mm_nt(d_pre_ref[span, :], stem_ref[...]).astype(BF16)
        return carry

    lax.fori_loop(0, TILE // HEAD_CHUNK, chunk, 0)


def total_rows(refs, rows):
    total = refs[0][rows, :].astype(F32)
    for ref in refs[1:]:
        total = total + ref[rows, :].astype(F32)
    return total


def sum_mid_kernel(in_ref, out_ref):
    refs = [in_ref.at[f] for f in range(in_ref.shape[0])]
    end = in_ref.shape[1]
    for at in range(0, end - 16, 32):
        out_ref[at:at + 32, :] = total_rows(refs, slice(at, at + 32)).astype(BF16)
    total = total_rows(refs, slice(end - 16, end))
    high, low = split_low(total[0:8] + total[8:16])
    out_ref[end - 16:end, :] = jnp.concatenate([high, low], axis=0)


def sum_end_kernel(in_ref, out_ref):
    refs = [in_ref.at[f] for f in range(in_ref.shape[0])]
    end, vec = in_ref.shape[1], WIDTH // in_ref.shape[0] // 2
    for at in range(0, end - vec, 32):
        out_ref[at:at + 32, :] = total_rows(refs, slice(at, at + 32)).astype(BF16)
    total = total_rows(refs, slice(end - vec, end))
    parts = []
    for k in (0, 128):
        parts += split_low(total[:, k:k + 64] + total[:, k + 64:k + 128])
    out_ref[end - vec:end, :] = jnp.concatenate(parts, axis=1)


def finish_kernel(count, compact, scale, stem_scale_ref, gain_ref, *refs):
    mids, ends = refs[:count], refs[count:2 * count]
    (
        loss_ref, stem_ref, table_ref, stem_bias_ref, stem_gain_ref, stem_shift_ref, block_ref, block_gain_ref, block_shift_ref,
        block_bias_ref, value_ref, value_bias_ref, chance_ref, chance_bias_ref,
    ) = refs[2 * count:]
    layers, shard, moves = block_ref.shape[0], block_ref.shape[1], table_ref.shape[0]
    nq, nc = value_ref.shape[1], chance_ref.shape[1]

    def mid_of(at, rows):
        return total_rows(mids, slice(at, at + rows)) * scale

    def end_of(at, rows):
        return total_rows(ends, slice(at, at + rows)) * scale

    for i in range(SPLIT, layers):
        block_ref[i] = mid_of((i - SPLIT) * shard, shard)
    for i in range(SPLIT):
        block_ref[i] = end_of((1 + i) * shard, shard)
    stem_ref[...] = end_of(0, shard)
    for k in range(3):
        width = min(WIDTH, nq - k * WIDTH)
        part = mid_of((layers - SPLIT + k) * shard, shard)
        value_ref[:, k * WIDTH:k * WIDTH + width] = part[:, 0:width]
    chance_ref[...] = part[:, 128:128 + nc]
    rep = mid_of((layers - SPLIT + 3) * shard, 16)
    rep = rep[0:8] + rep[8:16]
    only = lax.broadcasted_iota(jnp.int32, rep.shape, 0)
    bias = jnp.concatenate([jnp.sum(jnp.where(only == k, rep, 0.0), axis=0) for k in range(3)])
    value_bias_ref[...] = bias[0:nq]
    chance_bias_ref[...] = bias[640:640 + nc]
    loss_ref[0] = jnp.sum(rep[3:4])
    at = (1 + SPLIT) * shard
    if compact:
        small = end_of(at, shard // 2)
        small = jnp.concatenate([small[:, 0:128], small[:, 128:256]], axis=0)
    else:
        small = end_of(at, shard)[:, 0:128]
    if shard % 128:
        small = jnp.concatenate([small, jnp.zeros((128 - shard, 128), F32)], axis=0)
    small = small.T[:, 0:shard]
    small = small[0:64] + small[64:128]
    table_ref[...] = small[0:moves]
    stem_gain = stem_scale_ref[...].astype(F32)[None]
    stem_bias_ref[...] = small[moves:moves + 1]
    stem_gain_ref[...] = small[moves + 1:moves + 2] / stem_gain
    stem_shift_ref[...] = small[moves + 2:moves + 3] / (16.0 * stem_gain)
    at = moves + 3
    gain = gain_ref[...].astype(F32)
    block_gain_ref[...] = small[at:at + layers] / gain
    block_shift_ref[...] = small[at + layers:at + 2 * layers] / (16.0 * gain)
    block_bias_ref[...] = small[at + 2 * layers:at + 3 * layers]


SMEM = pl.BlockSpec(memory_space=pltpu.SMEM)
VMEM = pl.BlockSpec(memory_space=pltpu.VMEM)
ANY = pl.BlockSpec(memory_space=pl.ANY)


def params(mib):
    return pltpu.CompilerParams(vmem_limit_bytes=mib << 20)


def tiled(shape, dim):
    block = shape[:dim] + (TILE,) + shape[dim + 1:]
    return pl.BlockSpec(block, lambda i: (0,) * dim + (i,) + (0,) * (len(shape) - dim - 1))


def whole(shape):
    return pl.BlockSpec(shape, lambda i: (0,) * len(shape))


def once(shape):
    return pl.BlockSpec(shape, lambda i: (0,) * len(shape), pipeline_mode=pl.Buffered(1))


def struct(shape, dtype):
    return jax.ShapeDtypeStruct(shape, dtype)


def exchange(x, axis, size):
    return [lax.ppermute(x, axis, [(i, i ^ k) for i in range(size)]) for k in reversed(range(1, size))]


def per_device(
    latent, actions, value_bins, chance_codes, step_mask, stem_weight, action_table, stem_bias, stem_gain, stem_shift,
    block_weight, block_gain, block_shift, block_bias, value_weight, value_bias, chance_weight, chance_bias,
):
    n_dp, n_fsdp = lax.axis_size("dp"), lax.axis_size("fsdp")
    rows_dev = latent.shape[0]
    layers, shard = block_weight.shape[0], block_weight.shape[1]
    nq, nc = value_weight.shape[1], chance_weight.shape[1]
    moves = action_table.shape[0]
    steps = -(-rows_dev // TILE)
    padded = steps * TILE
    fast = shard % 16 == 0 and n_dp & (n_dp - 1) == 0

    pieces, piece_rows = (n_fsdp, shard) if fast else (1, WIDTH)
    fronts = 2 if fast and n_dp % 2 == 0 and SPLIT % 2 == 0 else 1
    core = (lax.axis_index("dp") % 2).astype(jnp.int32).reshape(1)
    n_front = (2 + SPLIT) // fronts
    front, back = pl.pallas_call(
        functools.partial(pack_kernel, fronts),
        in_specs=[SMEM] + [VMEM] * 11,
        out_specs=[VMEM] * 2,
        out_shape=[struct((pieces, n_front * shard, WIDTH), BF16), struct((layers - SPLIT + 2, shard, WIDTH), BF16)],
        scratch_shapes=[pltpu.VMEM((max(shard, 128), max(shard, 128)), F32)],
        name="pack",
    )(
        core, stem_weight, action_table, stem_bias, stem_gain, stem_shift, block_weight, block_gain, block_shift, block_bias,
        value_weight, chance_weight,
    )
    ints = jnp.pad(jnp.stack([actions, value_bins, chance_codes, step_mask]), ((0, 4), (0, padded - rows_dev)))
    none = lambda n: jnp.full((n,), -1e30, BF16)
    head_bias = jnp.concatenate([value_bias, none(640 - nq), chance_bias, none(128 - nc)])[None]
    if fast:
        w_fronts = [lax.all_to_all(front, "fsdp", 0, 0)]
        if fronts > 1:
            w_fronts[0], ints, head_bias = lax.optimization_barrier((w_fronts[0], ints, head_bias))
            w_fronts.append(lax.ppermute(w_fronts[0], "dp", [(i, i ^ 1) for i in range(n_dp)]))
    else:
        front = lax.all_gather(front.reshape(n_front, shard, WIDTH), "fsdp", axis=1, tiled=True)
        w_fronts = [front.reshape(1, n_front * WIDTH, WIDTH)]
    w_back = lax.all_gather(back, "fsdp", axis=1, tiled=True)

    ints_spec = pl.BlockSpec((8, TILE), lambda i: (0, i))
    saved = [
        struct((SPLIT + 1, padded, WIDTH), BF16),
        struct((SPLIT + 1, padded, WIDTH), BF16),
        struct((SPLIT + 1, padded, 128), F32),
        struct((SPLIT, padded, WIDTH), BF16),
    ]
    scratch = pltpu.VMEM
    kept = [scratch((x.shape[0], TILE, x.shape[2]), x.dtype) for x in saved] + [pltpu.SemaphoreType.DMA((SPLIT + 1, 4))]
    stream = struct((padded, WIDTH), F32)
    front_shape = (2 + SPLIT, WIDTH, WIDTH)
    *held, s_mid, vec, w_head = pl.pallas_call(
        functools.partial(first_kernel, layers, rows_dev, fronts, nq, nc),
        grid=(steps,),
        in_specs=[SMEM, tiled((rows_dev, WIDTH), 0), ints_spec] + [once(x.shape) for x in w_fronts],
        out_specs=[ANY] * 4 + [tiled(stream.shape, 0), whole((128, WIDTH)), whole((WIDTH, WIDTH))],
        out_shape=saved + [stream, struct((128, WIDTH), F32), struct((WIDTH, WIDTH), BF16)],
        scratch_shapes=[
            scratch(front_shape, BF16), scratch((TILE, WIDTH), BF16), scratch((TILE, 16), BF16), scratch((CHUNK, WIDTH), F32),
            scratch((TILE + CHUNK, WIDTH), F32),
        ] + kept,
        compiler_params=params(62),
        cost_estimate=pl.CostEstimate(flops=rows_dev * WIDTH * WIDTH * 200, bytes_accessed=60 << 20, transcendentals=0),
        name="first",
    )(core, latent, ints, *w_fronts)

    blocks = layers - SPLIT
    compact = piece_rows % 32 == 0 and fast
    mid_shape = (pieces, (blocks + 3) * piece_rows + 16, WIDTH)
    end_shape = (pieces, (SPLIT + 1) * piece_rows + piece_rows // 2, WIDTH)
    latents, ds_mid, gv_mid, rep, parts_mid = pl.pallas_call(
        functools.partial(middle_kernel, layers),
        grid=(steps,),
        in_specs=[tiled(stream.shape, 0), ints_spec, once(vec.shape), once(head_bias.shape), once(w_back.shape),
            once(w_head.shape)],
        out_specs=[
            tiled((rows_dev, WIDTH), 0), tiled(stream.shape, 0), whole((48, WIDTH)), whole((8, WIDTH)), whole(mid_shape),
        ],
        out_shape=[
            struct((rows_dev, WIDTH), BF16), stream, struct((48, WIDTH), F32), struct((8, WIDTH), F32), struct(mid_shape, BF16),
        ],
        scratch_shapes=[
            scratch((WIDTH, 3 * WIDTH), BF16),
            scratch((blocks, WIDTH, WIDTH), BF16),
            scratch((TILE + CHUNK, WIDTH), F32),
            scratch((blocks, TILE, WIDTH), BF16),
            scratch((blocks, TILE, WIDTH), BF16),
            scratch((blocks, TILE, WIDTH), F32),
            scratch((blocks, TILE, 128), F32),
            scratch((TILE, WIDTH), BF16),
            scratch((BACK, WIDTH), F32),
            scratch((WIDTH + 16, max(blocks * HEAD_CHUNK, TILE)), BF16),
            scratch((max(blocks * HEAD_CHUNK, TILE), 3 * WIDTH), BF16),
            scratch((blocks, WIDTH, WIDTH), F32),
            scratch((3, WIDTH + 16, WIDTH), F32),
            scratch((UNIT, 128), F32),
            scratch((HEAD_CHUNK, 3 * WIDTH), F32),
            scratch((TILE, 8), F32),
            scratch((2, HEAD_CHUNK, 128), F32),
            scratch((2, HEAD_CHUNK, 128), F32),
            scratch((HEAD_CHUNK, 3 * WIDTH), F32),
        ],
        compiler_params=params(62),
        cost_estimate=pl.CostEstimate(flops=rows_dev * WIDTH * WIDTH * 600, bytes_accessed=40 << 20, transcendentals=0),
        name="middle",
    )(s_mid, ints, vec, head_bias, w_back, w_head)

    d_pre, parts_end, w_stem = pl.pallas_call(
        functools.partial(last_kernel, layers, rows_dev, fronts),
        grid=(steps,),
        in_specs=[SMEM, tiled((rows_dev, WIDTH), 0), ints_spec, tiled(stream.shape, 0)]
        + [ANY] * 4 + [once((48, WIDTH))] + [once(x.shape) for x in w_fronts],
        out_specs=[tiled((padded, WIDTH), 0), whole(end_shape), whole((WIDTH, WIDTH))],
        out_shape=[struct((padded, WIDTH), BF16), struct(end_shape, BF16), struct((WIDTH, WIDTH), BF16)],
        scratch_shapes=[
            scratch(front_shape, BF16),
            scratch((TILE, WIDTH), BF16),
            scratch((16, TILE), BF16),
            scratch((TILE, WIDTH), F32),
            scratch((TILE, WIDTH), BF16),
            scratch((BACK, WIDTH), F32),
            scratch((CHUNK, WIDTH), BF16),
        ] + kept[:4] + [
            scratch((SPLIT + 1, WIDTH, WIDTH), F32),
            scratch((48, WIDTH), F32),
        ] + kept[4:],
        compiler_params=params(62),
        cost_estimate=pl.CostEstimate(flops=rows_dev * WIDTH * WIDTH * 150, bytes_accessed=60 << 20, transcendentals=0),
        name="last",
    )(core, latent, ints, ds_mid, *held, gv_mid, *w_fronts)

    def outputs_of(states):
        return pl.pallas_call(
            outputs_kernel,
            grid=(steps,),
            in_specs=[tiled((rows_dev, WIDTH), 0), tiled((padded, WIDTH), 0)]
            + [once(x.shape) for x in (w_back, w_head, head_bias, w_stem)],
            out_specs=[tiled((nq, rows_dev), 1), tiled((nc, rows_dev), 1), tiled((rows_dev, WIDTH), 0)],
            out_shape=[struct((nq, rows_dev), BF16), struct((nc, rows_dev), BF16), struct((rows_dev, WIDTH), BF16)],
            scratch_shapes=[scratch((3 * WIDTH, WIDTH), BF16), scratch((3 * WIDTH, 128), F32)],
            compiler_params=params(48),
            cost_estimate=pl.CostEstimate(flops=rows_dev * WIDTH * WIDTH * 20, bytes_accessed=16 << 20, transcendentals=0),
            name="outputs",
        )(states, d_pre, w_back, w_head, head_bias, w_stem)

    if fast:
        got_mid = lax.all_to_all(parts_mid, "fsdp", 0, 0)
        parts_end, got_mid, states = lax.optimization_barrier((parts_end, got_mid, latents))
        got_end = lax.all_to_all(parts_end, "fsdp", 0, 0)
        outputs = outputs_of(states)
        got_end, outputs = lax.optimization_barrier((got_end, outputs))

        def add(body, got, name):
            return pl.pallas_call(
                body, in_specs=[VMEM], out_specs=VMEM, out_shape=struct(got.shape[1:], BF16), name=name,
            )(got)

        mine_mid, mine_end = add(sum_mid_kernel, got_mid, "sum_mid"), add(sum_end_kernel, got_end, "sum_end")
        mids = [mine_mid] + exchange(mine_mid, "dp", n_dp)
        ends = [mine_end] + exchange(mine_end, "dp", n_dp)
    else:
        outputs = outputs_of(latents)

        def scatter(x, count):
            x = x[0, :count * WIDTH].reshape(count, WIDTH, WIDTH)
            x = lax.psum_scatter(x, "fsdp", scatter_dimension=1, tiled=True).astype(F32)
            return lax.psum(x, "dp").reshape(count * shard, WIDTH)

        rep = lax.psum(rep, ("dp", "fsdp"))
        vectors = parts_end[0, (SPLIT + 1) * WIDTH:]
        vectors = jnp.concatenate([vectors[:, 0:128], vectors[:, 128:256]], axis=0)
        vectors = jnp.concatenate([vectors, jnp.zeros_like(vectors)], axis=1)
        parts_end = jnp.concatenate([parts_end[:, :(SPLIT + 1) * WIDTH], vectors[None]], axis=1)
        mids = [jnp.concatenate([scatter(parts_mid, blocks + 3), rep, jnp.zeros((8, WIDTH), F32)])]
        ends = [scatter(parts_end, SPLIT + 2)]

    value_logits, chance_logits, latent_grad = outputs
    shapes = [
        (1,), (shard, WIDTH), (moves, shard), (1, shard), (1, shard), (1, shard), (layers, shard, WIDTH), (layers, shard),
        (layers, shard), (layers, shard), (shard, nq), (nq,), (shard, nc), (nc,),
    ]
    (
        loss, stem_grad, table_grad, stem_bias_grad, stem_gain_grad, stem_shift_grad, block_grad, gain_grad, shift_grad, bias_grad,
        value_grad, value_bias_grad, chance_grad, chance_bias_grad,
    ) = pl.pallas_call(
        functools.partial(finish_kernel, len(mids), compact, 1.0 / (rows_dev * n_dp * n_fsdp)),
        in_specs=[VMEM] * (2 + 2 * len(mids)),
        out_specs=[SMEM] + [VMEM] * (len(shapes) - 1),
        out_shape=[struct(x, F32) for x in shapes],
        name="finish",
    )(stem_gain, block_gain, *mids, *ends)
    return (
        latents,
        value_logits.T,
        chance_logits.T,
        loss.reshape(()),
        latent_grad,
        stem_grad,
        table_grad,
        stem_bias_grad.reshape(shard),
        stem_gain_grad.reshape(shard),
        stem_shift_grad.reshape(shard),
        block_grad,
        gain_grad,
        shift_grad,
        bias_grad,
        value_grad,
        value_bias_grad,
        chance_grad,
        chance_bias_grad,
    )


def solution(mesh):
    placed = (
        P(("dp", "fsdp"), None),
        P(("dp", "fsdp")),
        P(("dp", "fsdp")),
        P(("dp", "fsdp")),
        P(("dp", "fsdp")),
        P("fsdp", None),
        P(None, "fsdp"),
        P("fsdp"),
        P("fsdp"),
        P("fsdp"),
        P(None, "fsdp", None),
        P(None, "fsdp"),
        P(None, "fsdp"),
        P(None, "fsdp"),
        P("fsdp", None),
        P(),
        P("fsdp", None),
        P(),
    )
    return jax.shard_map(
        per_device,
        mesh=mesh,
        in_specs=placed,
        out_specs=(
            P(("dp", "fsdp"), None),
            P(("dp", "fsdp"), None),
            P(("dp", "fsdp"), None),
            P(),
            P(("dp", "fsdp"), None),
            P("fsdp", None),
            P(None, "fsdp"),
            P("fsdp"),
            P("fsdp"),
            P("fsdp"),
            P(None, "fsdp", None),
            P(None, "fsdp"),
            P(None, "fsdp"),
            P(None, "fsdp"),
            P("fsdp", None),
            P(),
            P("fsdp", None),
            P(),
        ),
        check_vma=False,
    )
```
